32 devices in a mesh: section: 2 (over x), hid: 4 (over z), wid: 4 (over y, core).
Axes of the slice: x: 2, y: 2, z: 4, core: 2. Of those that a mesh axis runs over, the one named last changes fastest.
Arguments:
- grad_out: float32 [2, 256, 6144], P(None, None, 'wid'), may hold values from -6 to 6
- weight_in: bfloat16 [2, 6144, 24576], P('section', 'wid', 'hid'), may hold values from -0.078125 to 0.078125
- weight_out: bfloat16 [2, 24576, 6144], P('section', 'hid', 'wid'), may hold values from -0.0390625 to 0.0390625
- pre_act: float32 [2, 2, 256, 24576], P('section', None, None, 'hid'), may hold values from -6 to 6
Outputs:
- grads: float32 [2, 2, 256, 6144], P('section', None, None, 'wid')
The draws below stay inside these ranges and needn't reach their ends.
All inputs are finite; a program needn't handle non-finite values.
Results may differ from the reference program's by a relative error of at most 0.003.
Values may be sent and summed in bfloat16 or wider, within the bound.
No kernel may reach another device: no remote copies, remote signals or barrier semaphores. Data moves between devices by JAX's collectives and lax.ppermute only.
A program may use at most 192 MiB of HBM per device.

```python
import jax
import jax.numpy as jnp
from jax import lax

D = 6144
FF = 24576
TOK = 256
MB = 2
N_HID = 4


def block_levels(key, extent, pieces, low, largest):
    level, own = 1.0, jax.random.fold_in(key, 6)
    for position, shards_of in pieces:
        steps = jnp.exp(jax.random.uniform(jax.random.fold_in(own, position), (shards_of,), jnp.float32, low / len(pieces), largest / len(pieces)))
        level = level * jnp.repeat(steps, extent[position] // shards_of).reshape([-1 if axis == position else 1 for axis in range(len(extent))])
    return level


def centred(rng, shape, spread, reach, split=(), dtype=jnp.bfloat16):
    array = jax.random.normal(rng, shape, jnp.float32) * spread
    if len(split) > 0:
        array = block_levels(rng, shape, split, -0.22, 0.18) * array
    return jnp.clip(array, min=-reach, max=reach).astype(dtype)


def setup_inputs(seed: int = 0) -> dict:
    splits = jax.random.split(jax.random.key(seed), 5)
    grad_out = centred(splits[0], (MB, TOK, D), 1.0, 6.0, ((2, 4),), jnp.float32)
    weight_in = centred(splits[1], (2, D, FF), D ** -0.5, 0.078125, ((0, 2), (1, 4), (2, 4)))
    weight_out = centred(splits[2], (2, FF, D), FF ** -0.5, 0.0390625, ((0, 2), (1, 4), (2, 4)))
    pre_act = centred(splits[3], (2, MB, TOK, FF), 1.5, 6.0, ((0, 2), (3, 4)), jnp.float32)
    return {"grad_out": grad_out, "weight_in": weight_in, "weight_out": weight_out, "pre_act": pre_act}


def gelu_slope(pre):
    normal_cdf = 0.5 * (1.0 + jax.scipy.special.erf(pre * 0.7071067811865476))
    density = jnp.exp(-0.5 * pre * pre) * 0.3989422804014327
    return normal_cdf + pre * density


def upstream_weights(weight_in, weight_out):
    tiles = N_HID
    narrow = FF // (2 * tiles)
    mat_in = weight_in[1].reshape(4, D // 4, tiles, FF // tiles).transpose(0, 2, 1, 3)
    mat_in = mat_in.reshape(2, 2, tiles, D // 2, narrow).transpose(0, 3, 2, 1, 4).reshape(D, FF)
    mat_out = weight_out[1].reshape(tiles, FF // tiles, 4, D // 4).transpose(0, 2, 1, 3)
    mat_out = mat_out.reshape(tiles, 2, 2, narrow, D // 2).transpose(0, 2, 3, 1, 4).reshape(FF, D)
    return mat_in, mat_out


def section_back(grad, tile_in, tile_out, pre):
    contract = (((1,), (1,)), ((), ()))
    hidden_grad = lax.dot_general(grad.astype(jnp.bfloat16), tile_out, contract, preferred_element_type=jnp.float32)
    hidden = (hidden_grad * gelu_slope(pre)).astype(jnp.bfloat16)
    return grad + lax.dot_general(hidden, tile_in, contract, preferred_element_type=jnp.float32)


def reference(grad_out, weight_in, weight_out, pre_act):
    up_in, up_out = upstream_weights(weight_in, weight_out)
    first = []
    second = []
    for batch_idx in range(MB):
        between = section_back(grad_out[batch_idx], weight_in[0], weight_out[0], pre_act[0, batch_idx])
        first.append(between)
        second.append(section_back(between, up_in, up_out, pre_act[1, batch_idx]))
    return jnp.stack([jnp.stack(first), jnp.stack(second)])
```

```python
import functools

import jax
import jax.numpy as jnp
from jax import lax
from jax.experimental import pallas as pl
from jax.experimental.pallas import tpu as pltpu
from jax.sharding import PartitionSpec as P

CHUNKS = 4
PARTS = 4
LIMIT = 40 * 1024 * 1024
NT = (((1,), (1,)), ((), ()))
LOW = jnp.bfloat16
F32 = jnp.float32


def gelu_slope(pre):
    normal_cdf = 0.5 * (1.0 + jax.scipy.special.erf(pre * 0.7071067811865476))
    density = jnp.exp(-0.5 * pre * pre) * 0.3989422804014327
    return normal_cdf + pre * density


def nt_dot(rows, block):
    return lax.dot_general(rows, block, NT, preferred_element_type=F32)


def params(limit=LIMIT):
    return pltpu.CompilerParams(
        vmem_limit_bytes=limit, dimension_semantics=("arbitrary",)
    )


def first_product(scalars, lhs, lhs_at, tokens, mat, block, place, steps, out_shape, out_block, out_map):
    depth = lhs.shape[1]

    def body(s, lhs_ref, mat_ref, out_ref):
        @pl.when(s[0] == 1)
        def _():
            got = nt_dot(lhs_ref[...].astype(LOW), mat_ref[...])
            out_ref[...] = got.reshape(out_ref.shape).astype(out_ref.dtype)

    return pl.pallas_call(
        body,
        grid_spec=pltpu.PrefetchScalarGridSpec(
            num_scalar_prefetch=1,
            grid=(steps,),
            in_specs=[
                pl.BlockSpec((tokens, depth), lambda i, s: (lhs_at, 0)),
                pl.BlockSpec(block, lambda i, s: place(i * s[0], s)),
            ],
            out_specs=pl.BlockSpec(out_block, lambda i, s: out_map(i * s[0])),
        ),
        out_shape=out_shape,
        compiler_params=params(),
        cost_estimate=pl.CostEstimate(
            flops=2 * tokens * block[0] * block[1] * steps,
            bytes_accessed=2 * block[0] * block[1] * steps,
            transcendentals=0,
        ),
    )(scalars, lhs, mat)


def hidden_product(scalars, lhs, lhs_at, tokens, mat, block, place, steps, base):
    depth = lhs.shape[1]
    width = block[0]

    def body(s, lhs_ref, mat_ref, base_ref, full_ref, low_ref):
        @pl.when(s[0] == 1)
        def _():
            got = nt_dot(lhs_ref[...].astype(LOW), mat_ref[...])
            got = got + base_ref[...].astype(F32)
            full_ref[...] = got
            low_ref[...] = got.astype(LOW)

    spec = pl.BlockSpec((tokens, width), lambda i, s: (0, i * s[0]))
    return pl.pallas_call(
        body,
        grid_spec=pltpu.PrefetchScalarGridSpec(
            num_scalar_prefetch=1,
            grid=(steps,),
            in_specs=[
                pl.BlockSpec((tokens, depth), lambda i, s: (lhs_at, 0)),
                pl.BlockSpec(block, lambda i, s: place(i * s[0], s)),
                spec,
            ],
            out_specs=[spec, spec],
        ),
        out_shape=[
            jax.ShapeDtypeStruct((tokens, width * steps), F32),
            jax.ShapeDtypeStruct((tokens, width * steps), LOW),
        ],
        compiler_params=params(),
        cost_estimate=pl.CostEstimate(
            flops=2 * tokens * block[0] * block[1] * steps,
            bytes_accessed=2 * block[0] * block[1] * steps,
            transcendentals=0,
        ),
    )(scalars, lhs, mat, base)


def back_product(scalars, lhs, mat, block, place, base):
    tokens, depth = lhs.shape
    width = block[0]

    def part_of(i, s):
        return lax.bitwise_xor(s[2], lax.rem(i + 1, PARTS)) * s[0]

    def body(s, lhs_ref, mat_ref, base_ref, one_ref, two_ref, three_ref, own_ref):
        i = pl.program_id(0)

        @pl.when(s[0] == 1)
        def _():
            got = nt_dot(lhs_ref[...], mat_ref[...])
            got = got + base_ref[0].astype(F32)
            for slot, ref in enumerate((one_ref, two_ref, three_ref, own_ref)):

                @pl.when(i == slot)
                def _(ref=ref):
                    ref[...] = got.astype(ref.dtype)

    spec = pl.BlockSpec((tokens, width), lambda i, s: (0, 0))
    return pl.pallas_call(
        body,
        grid_spec=pltpu.PrefetchScalarGridSpec(
            num_scalar_prefetch=1,
            grid=(PARTS,),
            in_specs=[
                pl.BlockSpec((tokens, depth), lambda i, s: (0, 0)),
                pl.BlockSpec(block, lambda i, s: place(part_of(i, s), s)),
                pl.BlockSpec((1, tokens, width), lambda i, s: (part_of(i, s), 0, 0)),
            ],
            out_specs=[spec] * 4,
        ),
        out_shape=[jax.ShapeDtypeStruct((tokens, width), LOW)] * 3
        + [jax.ShapeDtypeStruct((tokens, width), F32)],
        compiler_params=params(),
        cost_estimate=pl.CostEstimate(
            flops=2 * tokens * block[0] * block[1] * PARTS,
            bytes_accessed=2 * block[0] * block[1] * PARTS,
            transcendentals=0,
        ),
    )(scalars, lhs, mat, base)


def split_rows(scalars, mat):
    rows, cols = mat.shape
    step = 256
    half = step // 2

    def body(s, mat_ref, out_ref):
        @pl.when(s[0] == 1)
        def _():
            to = lax.broadcasted_iota(jnp.int32, (step, step), 0)
            source = lax.broadcasted_iota(jnp.int32, (step, step), 1)
            wanted = jnp.where(to < half, 2 * to, 2 * (to - half) + 1)
            pick = jnp.where(source == wanted, 1.0, 0.0).astype(LOW)
            got = jnp.dot(pick, mat_ref[...], preferred_element_type=F32).astype(LOW)
            out_ref[0] = got[:half]
            out_ref[1] = got[half:]

    out = pl.pallas_call(
        body,
        grid_spec=pltpu.PrefetchScalarGridSpec(
            num_scalar_prefetch=1,
            grid=(rows // step,),
            in_specs=[pl.BlockSpec((step, cols), lambda i, s: (i * s[0], 0))],
            out_specs=pl.BlockSpec((2, half, cols), lambda i, s: (0, i * s[0], 0)),
        ),
        out_shape=jax.ShapeDtypeStruct((2, rows // 2, cols), LOW),
        compiler_params=params(),
        cost_estimate=pl.CostEstimate(
            flops=2 * rows * step * cols, bytes_accessed=4 * rows * cols, transcendentals=0
        ),
    )(scalars, mat)
    return out.reshape(rows, cols)


def between_sections(scalars, grad, at, tokens, own, others):
    width = own.shape[1]

    def body(s, grad_ref, own_ref, one_ref, two_ref, three_ref, full_ref, low_ref):
        for slot, ref in enumerate((own_ref, one_ref, two_ref, three_ref)):
            start = pl.multiple_of(lax.bitwise_xor(s[2], slot) * width, 128)
            cols = pl.ds(start, width)
            total = grad_ref[:, cols] + ref[...].astype(F32)
            full_ref[:, cols] = total
            low_ref[:, cols] = total.astype(LOW)

    part = pl.BlockSpec((tokens, width), lambda i, s: (0, 0))
    whole = pl.BlockSpec((tokens, PARTS * width), lambda i, s: (0, 0))
    return pl.pallas_call(
        body,
        grid_spec=pltpu.PrefetchScalarGridSpec(
            num_scalar_prefetch=1,
            grid=(1,),
            in_specs=[pl.BlockSpec((tokens, PARTS * width), lambda i, s: (at, 0))] + [part] * 4,
            out_specs=[whole, whole],
        ),
        out_shape=[
            jax.ShapeDtypeStruct((tokens, PARTS * width), F32),
            jax.ShapeDtypeStruct((tokens, PARTS * width), LOW),
        ],
        compiler_params=params(),
    )(scalars, grad, own, *others)


def finish(scalars, out, between, at, total_tokens, own, others):
    tokens, columns = between.shape
    width = own.shape[1]
    lanes = 128

    def body(s, *refs):
        between_ref, own_ref, one_ref, two_ref, three_ref = refs[:5]
        out_ref, parts_ref = refs[-2:]

        @pl.when(s[0] == 0)
        def _():
            out_ref[...] = between_ref[...]

        @pl.when(s[0] == 1)
        def _():
            for slot, ref in enumerate((own_ref, one_ref, two_ref, three_ref)):
                parts_ref[lax.bitwise_xor(s[2], slot)] = ref[...]
            source = lax.broadcasted_iota(jnp.int32, (2 * lanes, 2 * lanes), 0)
            to = lax.broadcasted_iota(jnp.int32, (2 * lanes, 2 * lanes), 1)
            wanted = jnp.where(source < lanes, 2 * source, 2 * (source - lanes) + 1)
            pick = jnp.where(to == wanted, 1.0, 0.0).astype(LOW)
            for group in range(columns // (2 * lanes)):
                part, inside = divmod(group * lanes, width)
                even = parts_ref[part, :, inside : inside + lanes]
                odd = parts_ref[part + PARTS // 2, :, inside : inside + lanes]
                pair = jnp.concatenate([even, odd], axis=1)
                woven = jnp.dot(pair, pick, preferred_element_type=F32)
                cols = slice(group * 2 * lanes, (group + 1) * 2 * lanes)
                out_ref[:, cols] = between_ref[:, cols] + woven

    part = pl.BlockSpec((tokens, width), lambda i, s: (0, 0))
    earlier = [] if out is None else [out]
    return pl.pallas_call(
        body,
        grid_spec=pltpu.PrefetchScalarGridSpec(
            num_scalar_prefetch=1,
            grid=(1,),
            in_specs=[pl.BlockSpec((tokens, columns), lambda i, s: (0, 0))]
            + [part] * 4
            + [pl.BlockSpec(memory_space=pl.ANY)] * len(earlier),
            out_specs=pl.BlockSpec((tokens, columns), lambda i, s: (at, 0)),
            scratch_shapes=[pltpu.VMEM((PARTS, tokens, width), LOW)],
        ),
        out_shape=jax.ShapeDtypeStruct((total_tokens, columns), F32),
        input_output_aliases={6: 0} if earlier else {},
        compiler_params=params(),
    )(scalars, between, own, *others, *earlier)


def local(grad_out, weight_in, weight_out, pre_act):
    sections = lax.axis_size("section")
    hids = lax.axis_size("hid")
    wids = lax.axis_size("wid")
    section = lax.axis_index("section")
    hid = lax.axis_index("hid")
    wid = lax.axis_index("wid")
    side = wid % 2
    is_up = section == 1

    def scalars(active_section):
        active = (section == active_section).astype(jnp.int32)
        return jnp.stack([active, side, hid % PARTS]).astype(jnp.int32)

    down, up = scalars(0), scalars(1)

    def within(active, distance, axis, block):
        size = lax.axis_size(axis)
        pairs = [(active * size + i, active * size + (i ^ distance)) for i in range(size)]
        return lax.ppermute(block, ("section", axis), pairs)

    def both(distance, axis, block):
        return lax.ppermute(block, axis, [(i, i ^ distance) for i in range(lax.axis_size(axis))])

    mat_in = weight_in[0]
    mat_out = weight_out[0]
    quarter, hid_tile = mat_in.shape
    half = hid_tile // 2
    batches, batch_tokens, _ = grad_out.shape
    total = batches * batch_tokens
    tokens = total // CHUNKS
    grad = grad_out.reshape(total, quarter)
    pre = pre_act[0].reshape(total, hid_tile)
    pre = lax.dynamic_slice_in_dim(pre, side * half, half, 1)

    rows = max(r for r in (512, 384, 256, 128) if half % r == 0)
    per_half = half // rows
    width = quarter // PARTS

    split_out = split_rows(up, mat_out)

    def slope_of(k):
        return lax.optimization_barrier(gelu_slope(pre[k * tokens : (k + 1) * tokens]))

    slopes = [slope_of(k) for k in range(CHUNKS)]

    def reduce_hid(active, parts):
        one, two, three, own = parts
        got = [within(active, d, "hid", part) for d, part in ((1, one), (2, two), (3, three))]
        own = own + got[0].astype(F32) + got[1].astype(F32) + got[2].astype(F32)
        distance = PARTS
        while distance < hids:
            own = own + within(active, distance, "hid", own)
            distance *= 2
        return own.astype(LOW)

    def backward(k, active, flags, hidden_grad, low_grad):
        other = within(active, 2, "wid", low_grad)
        return ((hidden_grad + other.astype(F32)) * slopes[k]).astype(LOW)

    k1 = dict(tokens=tokens, block=(rows, quarter), steps=per_half)

    def down_chunk(k):
        sent = first_product(
            down, grad, k, mat=mat_out, place=lambda i, s: ((1 - s[1]) * s[0] * per_half + i, 0),
            out_shape=jax.ShapeDtypeStruct((tokens, half), LOW),
            out_block=(tokens, rows), out_map=lambda i: (0, i), **k1,
        )
        got = within(0, 1, "wid", sent)
        full, low = hidden_product(
            down, grad, k, mat=mat_out, place=lambda i, s: (s[1] * s[0] * per_half + i, 0),
            base=got, **k1,
        )
        hidden = backward(k, 0, down, full, low)
        swapped = within(0, 1, "wid", hidden)
        partial = first_product(
            down, hidden, 0, tokens=tokens, mat=mat_in, block=(width, half),
            place=lambda i, s: (i, s[1] * s[0]), steps=PARTS,
            out_shape=jax.ShapeDtypeStruct((PARTS, tokens, width), F32),
            out_block=(1, tokens, width), out_map=lambda i: (i, 0, 0),
        )
        parts = back_product(
            down, swapped, mat_in, (width, half),
            lambda part, s: (part, (1 - s[1]) * s[0]), partial,
        )
        term = reduce_hid(0, parts)
        crossed = lax.ppermute(term, "section", [(0, 1)])
        term = jnp.where(is_up, crossed, term)
        others = [both(d, "hid", term) for d in (1, 2, 3)]
        return between_sections(up, grad, k, tokens, term, others)

    def up_chunk(k, out, between, low):
        low_other = within(1, 1, "wid", low)
        partial = first_product(
            up, low, 0, mat=split_out, place=lambda i, s: (s[1] * s[0] * per_half + i, 0),
            out_shape=jax.ShapeDtypeStruct((tokens, half), F32),
            out_block=(tokens, rows), out_map=lambda i: (0, i), **k1,
        )
        full, low_grad = hidden_product(
            up, low_other, 0, mat=split_out,
            place=lambda i, s: ((1 - s[1]) * s[0] * per_half + i, 0), base=partial, **k1,
        )
        hidden = backward(k, 1, up, full, low_grad)

        def place(core, part):
            return core * (PARTS // 2) + part % (PARTS // 2), part // (PARTS // 2)

        sent = first_product(
            up, hidden, 0, tokens=tokens, mat=mat_in, block=(width, half),
            place=lambda i, s: place((1 - s[1]) * s[0], i), steps=PARTS,
            out_shape=jax.ShapeDtypeStruct((PARTS, tokens, width), LOW),
            out_block=(1, tokens, width), out_map=lambda i: (i, 0, 0),
        )
        got = within(1, 1, "wid", sent)
        parts = back_product(
            up, hidden, mat_in, (width, half),
            lambda part, s: place(s[1] * s[0], part), got,
        )
        term = reduce_hid(1, parts)
        others = [within(1, d, "hid", term) for d in (1, 2, 3)]
        return finish(up, out, between, k, total, term, others)

    firsts = [down_chunk(k) for k in range(CHUNKS)]
    out = None
    for k in range(CHUNKS):
        out = up_chunk(k, out, *firsts[k])
    return out.reshape(1, batches, batch_tokens, quarter)


def solution(mesh):
    return jax.shard_map(
        local,
        mesh=mesh,
        in_specs=(
            P(None, None, "wid"),
            P("section", "wid", "hid"),
            P("section", "hid", "wid"),
            P("section", None, None, "hid"),
        ),
        out_specs=P("section", None, None, "wid"),
        check_vma=False,
    )
```

```python
import jax
import jax.numpy as jnp
from jax import lax
from jax.experimental import pallas as pl
from jax.experimental.pallas import tpu as pltpu
from jax.sharding import PartitionSpec as P

SHARES = (1, 2, 1)
LIMIT = 40 * 1024 * 1024
LOW = jnp.bfloat16
F32 = jnp.float32


def gelu_slope(pre):
    normal_cdf = 0.5 * (1.0 + jax.scipy.special.erf(pre * 0.7071067811865476))
    density = jnp.exp(-0.5 * pre * pre) * 0.3989422804014327
    return normal_cdf + pre * density


def params():
    return pltpu.CompilerParams(
        vmem_limit_bytes=LIMIT, dimension_semantics=("arbitrary",)
    )


def divisor(size, most):
    return max(r for r in range(16, most + 1, 16) if size % r == 0)


def product(scalars, mat, block, place, steps, right, kinds, base=None):
    depth, tokens = right.shape
    rows = block[0]

    def body(s, mat_ref, right_ref, *refs):
        @pl.when(s[0] == 1)
        def _():
            got = jnp.dot(mat_ref[...], right_ref[...], preferred_element_type=F32)
            outs = refs
            if base is not None:
                got = got + refs[0][...].astype(F32)
                outs = refs[1:]
            for ref in outs:
                ref[...] = got.astype(ref.dtype)

    spec = pl.BlockSpec((rows, tokens), lambda i, s: (i * s[0], 0))
    return pl.pallas_call(
        body,
        grid_spec=pltpu.PrefetchScalarGridSpec(
            num_scalar_prefetch=1,
            grid=(steps,),
            in_specs=[
                pl.BlockSpec(block, lambda i, s: place(i * s[0], s[1] * s[0], s[0])),
                pl.BlockSpec((depth, tokens), lambda i, s: (0, 0)),
            ]
            + [spec] * (base is not None),
            out_specs=[spec] * len(kinds),
        ),
        out_shape=[jax.ShapeDtypeStruct((rows * steps, tokens), kind) for kind in kinds],
        compiler_params=params(),
        cost_estimate=pl.CostEstimate(
            flops=2 * tokens * block[0] * block[1] * steps,
            bytes_accessed=2 * block[0] * block[1] * steps,
            transcendentals=0,
        ),
    )(scalars, mat, right, *([] if base is None else [base]))


def split_rows(scalars, mat):
    rows, cols = mat.shape
    step = 256
    half = step // 2
    group = 2

    def body(s, mat_ref, out_ref):
        @pl.when(s[0] == 1)
        def _():
            to = lax.broadcasted_iota(jnp.int32, (step, step), 0)
            source = lax.broadcasted_iota(jnp.int32, (step, step), 1)
            wanted = jnp.where(to < half, 2 * to, 2 * (to - half) + 1)
            pick = jnp.where(source == wanted, 1.0, 0.0).astype(LOW)
            for g in range(group):
                block = mat_ref[g * step : (g + 1) * step]
                got = jnp.dot(pick, block, preferred_element_type=F32).astype(LOW)
                out_ref[0, g * half : (g + 1) * half] = got[:half]
                out_ref[1, g * half : (g + 1) * half] = got[half:]

    out = pl.pallas_call(
        body,
        grid_spec=pltpu.PrefetchScalarGridSpec(
            num_scalar_prefetch=1,
            grid=(rows // (group * step),),
            in_specs=[pl.BlockSpec((group * step, cols), lambda i, s: (i * s[0], 0))],
            out_specs=pl.BlockSpec((2, group * half, cols), lambda i, s: (0, i * s[0], 0)),
        ),
        out_shape=jax.ShapeDtypeStruct((2, rows // 2, cols), LOW),
        compiler_params=params(),
        cost_estimate=pl.CostEstimate(
            flops=2 * rows * step * cols, bytes_accessed=4 * rows * cols, transcendentals=0
        ),
    )(scalars, mat)
    return out.reshape(rows, cols)


def finish(scalars, out, between, start, total_tokens, term):
    columns, tokens = between.shape
    lanes = 128

    def body(s, *refs):
        between_ref, term_ref = refs[1:3] if out is not None else refs[:2]
        out_ref = refs[-1]
        source = lax.broadcasted_iota(jnp.int32, (2 * lanes, 2 * lanes), 1)
        to = lax.broadcasted_iota(jnp.int32, (2 * lanes, 2 * lanes), 0)
        wanted = jnp.where(source < lanes, 2 * source, 2 * (source - lanes) + 1)
        pick = jnp.where(to == wanted, 1.0, 0.0).astype(LOW)

        @pl.when(s[0] == 0)
        def _():
            out_ref[...] = between_ref[...].T

        @pl.when(s[0] == 1)
        def _():
            for group in range(columns // (2 * lanes)):
                odd_at = columns // 2 + group * lanes
                even = term_ref[group * lanes : (group + 1) * lanes]
                odd = term_ref[odd_at : odd_at + lanes]
                pair = jnp.concatenate([even, odd], axis=0)
                woven = jnp.dot(pick, pair, preferred_element_type=F32)
                at = slice(group * 2 * lanes, (group + 1) * 2 * lanes)
                out_ref[:, at] = (between_ref[at] + woven).T

    earlier = [] if out is None else [out]
    block = pl.BlockSpec((columns, lanes), lambda i, s: (0, i))
    return pl.pallas_call(
        body,
        grid_spec=pltpu.PrefetchScalarGridSpec(
            num_scalar_prefetch=1,
            grid=(tokens // lanes,),
            in_specs=[pl.BlockSpec(memory_space=pl.ANY)] * len(earlier) + [block, block],
            out_specs=pl.BlockSpec((lanes, columns), lambda i, s: (start // lanes + i, 0)),
        ),
        out_shape=jax.ShapeDtypeStruct((total_tokens, columns), F32),
        input_output_aliases={1: 0} if earlier else {},
        compiler_params=params(),
    )(scalars, *earlier, between, term)


def local(grad_out, weight_in, weight_out, pre_act):
    hids = lax.axis_size("hid")
    section = lax.axis_index("section")
    side = lax.axis_index("wid") % 2
    is_up = section == 1

    def scalars(active_section):
        active = (section == active_section).astype(jnp.int32)
        return jnp.stack([active, side]).astype(jnp.int32)

    down, up = scalars(0), scalars(1)

    def within(active, distance, block):
        size = lax.axis_size("wid")
        pairs = [(active * size + i, active * size + (i ^ distance)) for i in range(size)]
        return lax.ppermute(block, ("section", "wid"), pairs)

    mat_in = weight_in[0]
    mat_out = weight_out[0]
    quarter, hid_tile = mat_in.shape
    half = hid_tile // 2
    batches, batch_tokens, _ = grad_out.shape
    total = batches * batch_tokens
    unit = total // sum(SHARES)
    starts = [unit * sum(SHARES[:k]) for k in range(len(SHARES))]
    sizes = [unit * share for share in SHARES]
    chunks = range(len(SHARES))
    grad = grad_out.reshape(total, quarter)
    pre = pre_act[0].reshape(total, hid_tile)

    split_out = split_rows(up, mat_out)

    def slope_of(k):
        own = lax.dynamic_slice(pre, (starts[k], side * half), (sizes[k], half))
        return lax.optimization_barrier(gelu_slope(own).T)

    slopes = [slope_of(k) for k in chunks]
    grads = [grad[starts[k] : starts[k] + sizes[k]].T for k in chunks]

    hid_rows = divisor(half, 1024)
    hid_steps = half // hid_rows
    hid_block = (hid_rows, quarter)
    width_rows = divisor(quarter, 512)
    pair_rows = divisor(quarter // 2, 512)
    pair_steps = quarter // 2 // pair_rows

    def reduce_hid(partial):
        parts = partial.reshape(hids, quarter // hids, partial.shape[1])
        got = lax.all_to_all(parts, "hid", 0, 0)
        return got.astype(F32).sum(0).astype(LOW)

    def gather_hid(term):
        got = lax.all_gather(term, "hid", axis=0)
        return got.reshape(quarter, term.shape[1])

    def backward(k, active, hidden_grad, low_grad):
        other = within(active, 2, low_grad)
        return ((hidden_grad + other.astype(F32)) * slopes[k]).astype(LOW)

    def down_chunk(k, flags):
        low = grads[k].astype(LOW)
        (sent,) = product(
            flags, mat_out, hid_block, lambda i, b, on: ((on - b) * hid_steps + i, 0),
            hid_steps, low, (LOW,),
        )
        got = within(0, 1, sent)
        full, low_grad = product(
            flags, mat_out, hid_block, lambda i, b, on: (b * hid_steps + i, 0),
            hid_steps, low, (F32, LOW), got,
        )
        hidden = backward(k, 0, full, low_grad)
        swapped = within(0, 1, hidden)
        (partial,) = product(
            down, mat_in, (width_rows, half), lambda i, b, on: (i, b),
            quarter // width_rows, hidden, (F32,),
        )
        (partial,) = product(
            down, mat_in, (width_rows, half), lambda i, b, on: (i, on - b),
            quarter // width_rows, swapped, (LOW,), partial,
        )
        term = reduce_hid(partial)
        crossed = lax.ppermute(term, "section", [(0, 1)])
        term = gather_hid(jnp.where(is_up, crossed, term))
        return grads[k] + term.astype(F32), low_grad

    def up_chunk(k, out, between):
        low = between.astype(LOW)
        low_other = within(1, 1, low)
        (partial,) = product(
            up, split_out, hid_block, lambda i, b, on: (b * hid_steps + i, 0),
            hid_steps, low, (F32,),
        )
        full, low_grad = product(
            up, split_out, hid_block, lambda i, b, on: ((on - b) * hid_steps + i, 0),
            hid_steps, low_other, (F32, LOW), partial,
        )
        hidden = backward(k, 1, full, low_grad)

        def place(i, core):
            return core * pair_steps + i % pair_steps, i // pair_steps

        (sent,) = product(
            up, mat_in, (pair_rows, half), lambda i, b, on: place(i, on - b),
            2 * pair_steps, hidden, (F32,),
        )
        got = within(1, 1, sent)
        (partial,) = product(
            up, mat_in, (pair_rows, half), lambda i, b, on: place(i, b),
            2 * pair_steps, hidden, (LOW,), got,
        )
        term = gather_hid(reduce_hid(partial))
        return finish(up, out, between, starts[k], total, term)

    firsts = []
    flags = down
    for k in chunks:
        between, last = down_chunk(k, flags)
        firsts.append(between)
        flags, _ = lax.optimization_barrier((down, last))
    out = None
    for k in chunks:
        out = up_chunk(k, out, firsts[k])
    return out.reshape(1, batches, batch_tokens, quarter)


def solution(mesh):
    return jax.shard_map(
        local,
        mesh=mesh,
        in_specs=(
            P(None, None, "wid"),
            P("section", "wid", "hid"),
            P("section", "hid", "wid"),
            P("section", None, None, "hid"),
        ),
        out_specs=P("section", None, None, "wid"),
        check_vma=False,
    )
```

```python
import functools

import jax
import jax.numpy as jnp
from jax import lax
from jax.experimental import pallas as pl
from jax.experimental.pallas import tpu as pltpu
from jax.sharding import PartitionSpec as P

SHARES = (1, 2, 1)
PARTS = 4
LANES = 128
LIMIT = 26 * 1024 * 1024
LOW = jnp.bfloat16
F32 = jnp.float32


def gelu_slope(pre):
    normal_cdf = 0.5 * (1.0 + lax.erf(pre * 0.7071067811865476))
    density = jnp.exp(-0.5 * pre * pre) * 0.3989422804014327
    return normal_cdf + pre * density


def params():
    return pltpu.CompilerParams(vmem_limit_bytes=LIMIT)


def divisor(size, most):
    return max(r for r in range(16, most + 1, 16) if size % r == 0)


SMEM = pl.BlockSpec(memory_space=pltpu.SMEM)
VMEM = pl.BlockSpec(memory_space=pltpu.VMEM)
ANY = pl.BlockSpec(memory_space=pl.ANY)


def product(flags, mat, block, place, steps, sources, prepare, tokens, outs, store, base=None):
    rows, depth = block
    slots = min(4, steps)
    bare = prepare is None
    count = len(sources)

    def body(s, mat_ref, *refs):
        source_refs, refs = refs[:count], refs[count:]
        base_ref = None
        if base is not None:
            base_ref, refs = refs[0], refs[1:]
        out_refs, (buf, sem) = refs[:-2], refs[-2:]

        def fetch(i):
            row, col = place(i, s)
            piece = mat_ref.at[pl.ds(pl.multiple_of(row, 16), rows), pl.ds(pl.multiple_of(col, LANES), depth)]
            return pltpu.make_async_copy(piece, buf.at[i % slots], sem.at[i % slots])

        @pl.when(s[0] == 1)
        def _():
            for i in range(slots):
                fetch(i).start()
            right_ref = source_refs[0]
            if not bare:
                right_ref = out_refs[-1]
                prepare(right_ref, *source_refs)
            for i in range(steps):
                fetch(i).wait()
                got = jnp.dot(buf[i % slots], right_ref[...], preferred_element_type=F32)
                if i + slots < steps:
                    fetch(i + slots).start()
                targets, base_row = store(i, s)
                if base_ref is not None:
                    start = pl.multiple_of(base_row, 16)
                    got = got + base_ref[pl.ds(start, rows)].astype(F32)
                for which, row in targets:
                    out_refs[which][row : row + rows] = got.astype(out_refs[which].dtype)

    shapes = [jax.ShapeDtypeStruct((size, tokens), kind) for size, kind in outs]
    if not bare:
        shapes.append(jax.ShapeDtypeStruct((depth, tokens), LOW))
    return pl.pallas_call(
        body,
        in_specs=[SMEM, ANY] + [VMEM] * (count + (base is not None)),
        out_specs=[VMEM] * len(shapes),
        out_shape=shapes,
        scratch_shapes=[
            pltpu.VMEM((slots, rows, depth), LOW),
            pltpu.SemaphoreType.DMA((slots,)),
        ],
        compiler_params=params(),
        cost_estimate=pl.CostEstimate(
            flops=2 * tokens * rows * depth * steps,
            bytes_accessed=2 * rows * depth * steps,
            transcendentals=0,
        ),
    )(flags, mat, *sources, *([] if base is None else [base]))


def turned(right_ref, grad_ref):
    right_ref[...] = grad_ref[...].T.astype(LOW)


def hidden_of(right_ref, own_ref, other_ref, slope_ref):
    total = own_ref[...] + other_ref[...].astype(F32)
    right_ref[...] = (total * slope_ref[...]).astype(LOW)


def split_rows(flags, mat):
    rows, cols = mat.shape
    step = 256
    half = step // 2
    count = rows // step
    slots = 4

    def body(s, mat_ref, out_ref, buf, done, sem_in, sem_out):
        def fetch(i, slot):
            piece = mat_ref.at[pl.ds(pl.multiple_of(i * step, step), step)]
            return pltpu.make_async_copy(piece, buf.at[slot], sem_in.at[slot])

        def put(i, slot):
            piece = out_ref.at[:, pl.ds(pl.multiple_of(i * half, half), half)]
            return pltpu.make_async_copy(done.at[slot], piece, sem_out.at[slot])

        @pl.when(s[0] == 1)
        def _():
            to = lax.broadcasted_iota(jnp.int32, (step, step), 0)
            source = lax.broadcasted_iota(jnp.int32, (step, step), 1)
            wanted = jnp.where(to < half, 2 * to, 2 * (to - half) + 1)
            pick = jnp.where(source == wanted, 1.0, 0.0).astype(LOW)
            for i in range(slots):
                fetch(i, i).start()

            @pl.loop(0, count // slots)
            def _(turn):
                for slot in range(slots):
                    i = turn * slots + slot
                    fetch(i, slot).wait()

                    @pl.when(turn > 0)
                    def _():
                        put(i - slots, slot).wait()

                    got = jnp.dot(pick, buf[slot], preferred_element_type=F32).astype(LOW)
                    done[slot, 0] = got[:half]
                    done[slot, 1] = got[half:]

                    @pl.when(turn < count // slots - 1)
                    def _():
                        fetch(i + slots, slot).start()

                    put(i, slot).start()

            for slot in range(slots):
                put(count - slots + slot, slot).wait()

    out = pl.pallas_call(
        body,
        in_specs=[SMEM, ANY],
        out_specs=ANY,
        out_shape=jax.ShapeDtypeStruct((2, rows // 2, cols), LOW),
        scratch_shapes=[
            pltpu.VMEM((slots, step, cols), LOW),
            pltpu.VMEM((slots, 2, half, cols), LOW),
            pltpu.SemaphoreType.DMA((slots,)),
            pltpu.SemaphoreType.DMA((slots,)),
        ],
        compiler_params=params(),
        cost_estimate=pl.CostEstimate(
            flops=2 * rows * step * cols, bytes_accessed=4 * rows * cols, transcendentals=0
        ),
    )(flags, mat)
    return out.reshape(rows, cols)


def slope_of(flags, pre, start, tokens, half):
    cols = divisor(half, 768)
    per_half = half // cols

    def body(s, pre_ref, out_ref):
        out_ref[...] = gelu_slope(pre_ref[...]).T

    return pl.pallas_call(
        body,
        grid_spec=pltpu.PrefetchScalarGridSpec(
            num_scalar_prefetch=1,
            grid=(tokens // LANES, per_half),
            in_specs=[
                pl.BlockSpec((LANES, cols), lambda i, j, s: (start // LANES + i, s[1] * per_half + j))
            ],
            out_specs=pl.BlockSpec((cols, LANES), lambda i, j, s: (j, i)),
        ),
        out_shape=jax.ShapeDtypeStruct((half, tokens), F32),
        compiler_params=params(),
        cost_estimate=pl.CostEstimate(
            flops=40 * half * tokens, bytes_accessed=8 * half * tokens, transcendentals=0
        ),
    )(flags, pre)


def join(flags, grad, parts):
    tokens, columns = grad.shape
    width = columns // PARTS

    def body(s, grad_ref, *refs):
        part_refs, (low_ref, term_ref) = refs[:PARTS], refs[PARTS:]

        @pl.when(s[0] == 1)
        def _():
            for slot, ref in enumerate(part_refs):
                start = pl.multiple_of(lax.bitwise_xor(s[2], slot) * width, LANES)
                term = ref[...]
                term_ref[pl.ds(start, width)] = term
                total = grad_ref[:, pl.ds(start, width)].T + term.astype(F32)
                low_ref[pl.ds(start, width)] = total.astype(LOW)

    shape = jax.ShapeDtypeStruct((columns, tokens), LOW)
    return pl.pallas_call(
        body,
        in_specs=[SMEM] + [VMEM] * (1 + PARTS),
        out_specs=[VMEM, VMEM],
        out_shape=[shape, shape],
        compiler_params=params(),
        cost_estimate=pl.CostEstimate(
            flops=4 * columns * tokens, bytes_accessed=4 * columns * tokens, transcendentals=0
        ),
    )(flags, grad, *parts)


def finish(flags, out, grad, start, term, parts):
    columns, tokens = term.shape
    width = columns // PARTS
    total_tokens = grad.shape[0]

    def body(s, *refs):
        grad_ref, term_ref, *part_refs = refs[int(out is not None) : -2]
        out_ref, joined = refs[-2:]
        for slot, ref in enumerate(part_refs):
            start = pl.multiple_of(lax.bitwise_xor(s[2], slot) * width, LANES)
            joined[pl.ds(start, width)] = ref[...]

        @pl.when(s[0] == 0)
        def _():
            out_ref[...] = grad_ref[...] + joined[...].astype(F32).T

        @pl.when(s[0] == 1)
        def _():
            source = lax.broadcasted_iota(jnp.int32, (2 * LANES, 2 * LANES), 1)
            to = lax.broadcasted_iota(jnp.int32, (2 * LANES, 2 * LANES), 0)
            wanted = jnp.where(source < LANES, 2 * source, 2 * (source - LANES) + 1)
            pick = jnp.where(to == wanted, 1.0, 0.0).astype(LOW)
            for group in range(columns // (2 * LANES)):
                even_at = group * LANES
                odd_at = columns // 2 + group * LANES
                even = joined[even_at : even_at + LANES]
                odd = joined[odd_at : odd_at + LANES]
                pair = jnp.concatenate([even, odd], axis=0)
                woven = jnp.dot(pick, pair, preferred_element_type=F32)
                at = slice(group * 2 * LANES, (group + 1) * 2 * LANES)
                first = term_ref[at].astype(F32).T
                out_ref[:, at] = grad_ref[:, at] + first + woven.T

    earlier = [] if out is None else [out]
    piece = pl.BlockSpec((width, LANES), lambda i, s: (0, i))
    rows = pl.BlockSpec((LANES, columns), lambda i, s: (start // LANES + i, 0))
    return pl.pallas_call(
        body,
        grid_spec=pltpu.PrefetchScalarGridSpec(
            num_scalar_prefetch=1,
            grid=(tokens // LANES,),
            in_specs=[ANY] * len(earlier)
            + [rows, pl.BlockSpec((columns, LANES), lambda i, s: (0, i))]
            + [piece] * PARTS,
            out_specs=rows,
            scratch_shapes=[pltpu.VMEM((columns, LANES), LOW)],
        ),
        out_shape=jax.ShapeDtypeStruct((total_tokens, columns), F32),
        input_output_aliases={1: 0} if earlier else {},
        compiler_params=params(),
    )(flags, *earlier, grad, term, *parts)


def local(grad_out, weight_in, weight_out, pre_act):
    hids = lax.axis_size("hid")
    section = lax.axis_index("section")
    side = lax.axis_index("wid") % 2
    is_up = section == 1

    def scalars(active_section):
        active = (section == active_section).astype(jnp.int32)
        return jnp.stack([active, side, lax.axis_index("hid") % PARTS]).astype(jnp.int32)

    down, up = scalars(0), scalars(1)

    def within(active, distance, block, axis="wid"):
        size = lax.axis_size(axis)
        pairs = [(active * size + i, active * size + (i ^ distance)) for i in range(size)]
        return lax.ppermute(block, ("section", axis), pairs)

    def everywhere(distance, block, axis="hid"):
        size = lax.axis_size(axis)
        return lax.ppermute(block, axis, [(i, i ^ distance) for i in range(size)])

    mat_in = weight_in[0]
    mat_out = weight_out[0]
    quarter, hid_tile = mat_in.shape
    half = hid_tile // 2
    batches, batch_tokens, _ = grad_out.shape
    total = batches * batch_tokens
    unit = total // sum(SHARES)
    starts = [unit * sum(SHARES[:k]) for k in range(len(SHARES))]
    sizes = [unit * share for share in SHARES]
    chunks = range(len(SHARES))
    grad = grad_out.reshape(total, quarter)
    pre = pre_act[0].reshape(total, hid_tile)
    grads = [grad[starts[k] : starts[k] + sizes[k]] for k in chunks]

    split_out = split_rows(up, mat_out)

    hid_rows = divisor(half, 512)
    hid_steps = half // hid_rows
    part_rows = quarter // PARTS

    def in_order(*which):
        return lambda i, s, rows: ([(w, i * rows) for w in which], i * rows)

    def product_out(flags, mat, first_row, sources, prepare, tokens, kinds, base=None):
        return product(
            flags, mat, (hid_rows, quarter),
            lambda i, s: (first_row(s) + i * hid_rows, 0), hid_steps,
            sources, prepare, tokens, [(half, kind) for kind in kinds],
            functools.partial(in_order(*range(len(kinds))), rows=hid_rows), base,
        )

    def product_in(flags, place, sources, prepare, tokens, kind):
        return product(
            flags, mat_in, (part_rows, half), place, PARTS, sources, prepare, tokens,
            [(quarter, kind)], functools.partial(in_order(0), rows=part_rows),
        )

    def product_parts(flags, place, right, tokens, base):
        def part_of(i, s):
            return lax.bitwise_xor(s[2], (i + 1) % PARTS)

        return product(
            flags, mat_in, (part_rows, half), lambda i, s: place(part_of(i, s), s), PARTS,
            [right], None, tokens, [(part_rows, LOW)] * 3 + [(part_rows, F32)],
            lambda i, s: ([(i, 0)], part_of(i, s) * part_rows), base,
        )

    def scatter_hid(active, parts):
        *others, own = parts
        got = [within(active, d + 1, part, "hid") for d, part in enumerate(others)]
        for part in got:
            own = own + part.astype(F32)
        distance = PARTS
        while distance < hids:
            own = own + within(active, distance, own, "hid")
            distance *= 2
        return own.astype(LOW)

    def down_chunk(k, flags):
        tokens = sizes[k]
        sent, low = product_out(
            flags, mat_out, lambda s: (1 - s[1]) * half, [grads[k]], turned, tokens, (LOW,)
        )
        got = within(0, 1, sent)
        full, low_grad = product_out(
            flags, mat_out, lambda s: s[1] * half, [low], None, tokens, (F32, LOW), got
        )
        other = within(0, 2, low_grad)
        late, _ = lax.optimization_barrier((down, low_grad))
        slope = slope_of(late, pre, starts[k], tokens, half)
        hidden = ((full + other.astype(F32)) * slope).astype(LOW)
        swapped = within(0, 1, hidden)
        (partial,) = product_in(
            down, lambda i, s: (i * part_rows, s[1] * half), [hidden], None, tokens, F32
        )
        parts = product_parts(
            down, lambda i, s: (i * part_rows, (1 - s[1]) * half), swapped, tokens, partial
        )
        term = scatter_hid(0, parts)
        crossed = lax.ppermute(term, "section", [(0, 1)])
        gathered = [crossed] + [within(1, d, crossed, "hid") for d in range(1, PARTS)]
        return term, gathered, slope, low_grad

    def up_chunk(k, out, own_term, gathered, slope):
        tokens = sizes[k]
        low, term = join(up, grads[k], gathered)
        low_other = within(1, 1, low)
        (partial,) = product_out(
            up, split_out, lambda s: s[1] * half, [low], None, tokens, (F32,)
        )
        full, low_grad = product_out(
            up, split_out, lambda s: (1 - s[1]) * half, [low_other], None, tokens, (F32, LOW), partial
        )
        other = within(1, 2, low_grad)

        def place(part, core):
            row = core * (PARTS // 2) + part % (PARTS // 2)
            return row * part_rows, part // (PARTS // 2) * half

        sent, hidden = product_in(
            up, lambda i, s: place(i, 1 - s[1]), [full, other, slope], hidden_of, tokens, F32
        )
        got = within(1, 1, sent)
        parts = product_parts(up, lambda i, s: place(i, s[1]), hidden, tokens, got)
        last = jnp.where(is_up, scatter_hid(1, parts), own_term)
        parts = [last] + [everywhere(d, last) for d in range(1, PARTS)]
        return finish(up, out, grad, starts[k], term, parts)

    firsts = []
    flags = down
    for k in chunks:
        *first, low_grad = down_chunk(k, flags)
        firsts.append(first)
        flags, _ = lax.optimization_barrier((down, low_grad))
    out = None
    for k in chunks:
        out = up_chunk(k, out, *firsts[k])
    return out.reshape(1, batches, batch_tokens, quarter)


def solution(mesh):
    return jax.shard_map(
        local,
        mesh=mesh,
        in_specs=(
            P(None, None, "wid"),
            P("section", "wid", "hid"),
            P("section", "hid", "wid"),
            P("section", None, None, "hid"),
        ),
        out_specs=P("section", None, None, "wid"),
        check_vma=False,
    )
```

```python
import functools

import jax
import jax.numpy as jnp
from jax import lax
from jax.experimental import pallas as pl
from jax.experimental.pallas import tpu as pltpu
from jax.sharding import PartitionSpec as P

SHARES = (1, 2, 1)
PARTS = 4
LANES = 128
WEIGHT = 4096
LIMIT = 46 * 1024 * 1024
LOW = jnp.bfloat16
F32 = jnp.float32


def gelu_slope(pre):
    normal_cdf = 0.5 * (1.0 + lax.erf(pre * 0.7071067811865476))
    density = jnp.exp(-0.5 * pre * pre) * 0.3989422804014327
    return normal_cdf + pre * density


def params():
    return pltpu.CompilerParams(vmem_limit_bytes=LIMIT)


def divisor(size, most):
    return max(r for r in range(16, most + 1, 16) if size % r == 0)


SMEM = pl.BlockSpec(memory_space=pltpu.SMEM)
VMEM = pl.BlockSpec(memory_space=pltpu.VMEM)
ANY = pl.BlockSpec(memory_space=pl.ANY)


def product(flags, mat, block, place, steps, sources, prepare, tokens, outs, store, base=None):
    rows, depth = block
    slots = min(4, steps)
    bare = prepare is None
    count = len(sources)

    def body(s, mat_ref, *refs):
        source_refs, refs = refs[:count], refs[count:]
        base_ref = None
        if base is not None:
            base_ref, refs = refs[0], refs[1:]
        out_refs, (buf, sem) = refs[:-2], refs[-2:]

        def fetch(i):
            row, col = place(i, s)
            piece = mat_ref.at[pl.ds(pl.multiple_of(row, 16), rows), pl.ds(pl.multiple_of(col, LANES), depth)]
            return pltpu.make_async_copy(piece, buf.at[i % slots], sem.at[i % slots])

        @pl.when(s[0] == 1)
        def _():
            for i in range(slots):
                fetch(i).start()
            right_ref = source_refs[0]
            if not bare:
                right_ref = out_refs[-1]
                prepare(right_ref, *source_refs)
            for i in range(steps):
                fetch(i).wait()
                got = jnp.dot(buf[i % slots], right_ref[...], preferred_element_type=F32)
                if i + slots < steps:
                    fetch(i + slots).start()
                targets, base_row = store(i, s)
                if base_ref is not None:
                    start = pl.multiple_of(base_row, 16)
                    got = got + base_ref[pl.ds(start, rows)].astype(F32)
                for which, row in targets:
                    out_refs[which][row : row + rows] = got.astype(out_refs[which].dtype)

    shapes = [jax.ShapeDtypeStruct((size, tokens), kind) for size, kind in outs]
    if not bare:
        shapes.append(jax.ShapeDtypeStruct((depth, tokens), LOW))
    return pl.pallas_call(
        body,
        in_specs=[SMEM, ANY] + [VMEM] * (count + (base is not None)),
        out_specs=[VMEM] * len(shapes),
        out_shape=shapes,
        scratch_shapes=[
            pltpu.VMEM((slots, rows, depth), LOW),
            pltpu.SemaphoreType.DMA((slots,)),
        ],
        compiler_params=params(),
        cost_estimate=pl.CostEstimate(
            flops=2 * tokens * rows * depth * steps // WEIGHT,
            bytes_accessed=2 * rows * depth * steps // WEIGHT,
            transcendentals=0,
        ),
    )(flags, mat, *sources, *([] if base is None else [base]))


def turned(right_ref, grad_ref):
    right_ref[...] = grad_ref[...].T.astype(LOW)


def hidden_of(right_ref, own_ref, other_ref, slope_ref):
    total = own_ref[...] + other_ref[...].astype(F32)
    right_ref[...] = (total * slope_ref[...]).astype(LOW)


def split_rows(flags, mat):
    rows, cols = mat.shape
    step = 256
    half = step // 2
    count = rows // step
    slots = 4

    def body(s, mat_ref, out_ref, buf, done, sem_in, sem_out):
        def fetch(i, slot):
            piece = mat_ref.at[pl.ds(pl.multiple_of(i * step, step), step)]
            return pltpu.make_async_copy(piece, buf.at[slot], sem_in.at[slot])

        def put(i, slot):
            piece = out_ref.at[:, pl.ds(pl.multiple_of(i * half, half), half)]
            return pltpu.make_async_copy(done.at[slot], piece, sem_out.at[slot])

        @pl.when(s[0] == 1)
        def _():
            to = lax.broadcasted_iota(jnp.int32, (step, step), 0)
            source = lax.broadcasted_iota(jnp.int32, (step, step), 1)
            wanted = jnp.where(to < half, 2 * to, 2 * (to - half) + 1)
            pick = jnp.where(source == wanted, 1.0, 0.0).astype(LOW)
            for i in range(slots):
                fetch(i, i).start()

            @pl.loop(0, count // slots)
            def _(turn):
                for slot in range(slots):
                    i = turn * slots + slot
                    fetch(i, slot).wait()

                    @pl.when(turn > 0)
                    def _():
                        put(i - slots, slot).wait()

                    got = jnp.dot(pick, buf[slot], preferred_element_type=F32).astype(LOW)
                    done[slot, 0] = got[:half]
                    done[slot, 1] = got[half:]

                    @pl.when(turn < count // slots - 1)
                    def _():
                        fetch(i + slots, slot).start()

                    put(i, slot).start()

            for slot in range(slots):
                put(count - slots + slot, slot).wait()

    out = pl.pallas_call(
        body,
        in_specs=[SMEM, ANY],
        out_specs=ANY,
        out_shape=jax.ShapeDtypeStruct((2, rows // 2, cols), LOW),
        scratch_shapes=[
            pltpu.VMEM((slots, step, cols), LOW),
            pltpu.VMEM((slots, 2, half, cols), LOW),
            pltpu.SemaphoreType.DMA((slots,)),
            pltpu.SemaphoreType.DMA((slots,)),
        ],
        compiler_params=params(),
        cost_estimate=pl.CostEstimate(
            flops=2 * rows * step * cols // WEIGHT, bytes_accessed=4 * rows * cols // WEIGHT, transcendentals=0
        ),
    )(flags, mat)
    return out.reshape(rows, cols)


def slope_of(flags, pre, start, tokens, half):
    cols = divisor(half, 768)
    per_half = half // cols

    def body(s, pre_ref, out_ref):
        out_ref[...] = gelu_slope(pre_ref[...]).T

    return pl.pallas_call(
        body,
        grid_spec=pltpu.PrefetchScalarGridSpec(
            num_scalar_prefetch=1,
            grid=(tokens // LANES, per_half),
            in_specs=[
                pl.BlockSpec((LANES, cols), lambda i, j, s: (start // LANES + i, s[1] * per_half + j))
            ],
            out_specs=pl.BlockSpec((cols, LANES), lambda i, j, s: (j, i)),
        ),
        out_shape=jax.ShapeDtypeStruct((half, tokens), F32),
        compiler_params=params(),
        cost_estimate=pl.CostEstimate(
            flops=half * tokens // WEIGHT, bytes_accessed=8 * half * tokens // WEIGHT, transcendentals=0
        ),
    )(flags, pre)


def join(flags, grad, parts):
    tokens, columns = grad.shape
    width = columns // PARTS

    def body(s, grad_ref, *refs):
        part_refs, (low_ref, term_ref) = refs[:PARTS], refs[PARTS:]

        @pl.when(s[0] == 1)
        def _():
            for slot, ref in enumerate(part_refs):
                start = pl.multiple_of(lax.bitwise_xor(s[2], slot) * width, LANES)
                term = ref[...]
                term_ref[pl.ds(start, width)] = term
                total = grad_ref[:, pl.ds(start, width)].T + term.astype(F32)
                low_ref[pl.ds(start, width)] = total.astype(LOW)

    shape = jax.ShapeDtypeStruct((columns, tokens), LOW)
    return pl.pallas_call(
        body,
        in_specs=[SMEM] + [VMEM] * (1 + PARTS),
        out_specs=[VMEM, VMEM],
        out_shape=[shape, shape],
        compiler_params=params(),
        cost_estimate=pl.CostEstimate(
            flops=4 * columns * tokens, bytes_accessed=4 * columns * tokens, transcendentals=0
        ),
    )(flags, grad, *parts)


def finish(flags, out, grad, start, term, parts):
    columns, tokens = term.shape
    width = columns // PARTS
    total_tokens = grad.shape[0]

    def body(s, *refs):
        grad_ref, term_ref, *part_refs = refs[int(out is not None) : -2]
        out_ref, joined = refs[-2:]
        for slot, ref in enumerate(part_refs):
            start = pl.multiple_of(lax.bitwise_xor(s[2], slot) * width, LANES)
            joined[pl.ds(start, width)] = ref[...]

        @pl.when(s[0] == 0)
        def _():
            out_ref[...] = grad_ref[...] + joined[...].astype(F32).T

        @pl.when(s[0] == 1)
        def _():
            source = lax.broadcasted_iota(jnp.int32, (2 * LANES, 2 * LANES), 1)
            to = lax.broadcasted_iota(jnp.int32, (2 * LANES, 2 * LANES), 0)
            wanted = jnp.where(source < LANES, 2 * source, 2 * (source - LANES) + 1)
            pick = jnp.where(to == wanted, 1.0, 0.0).astype(LOW)
            for group in range(columns // (2 * LANES)):
                even_at = group * LANES
                odd_at = columns // 2 + group * LANES
                even = joined[even_at : even_at + LANES]
                odd = joined[odd_at : odd_at + LANES]
                pair = jnp.concatenate([even, odd], axis=0)
                woven = jnp.dot(pick, pair, preferred_element_type=F32)
                at = slice(group * 2 * LANES, (group + 1) * 2 * LANES)
                first = term_ref[at].astype(F32).T
                out_ref[:, at] = grad_ref[:, at] + first + woven.T

    earlier = [] if out is None else [out]
    piece = pl.BlockSpec((width, LANES), lambda i, s: (0, i))
    rows = pl.BlockSpec((LANES, columns), lambda i, s: (start // LANES + i, 0))
    return pl.pallas_call(
        body,
        grid_spec=pltpu.PrefetchScalarGridSpec(
            num_scalar_prefetch=1,
            grid=(tokens // LANES,),
            in_specs=[ANY] * len(earlier)
            + [rows, pl.BlockSpec((columns, LANES), lambda i, s: (0, i))]
            + [piece] * PARTS,
            out_specs=rows,
            scratch_shapes=[pltpu.VMEM((columns, LANES), LOW)],
        ),
        out_shape=jax.ShapeDtypeStruct((total_tokens, columns), F32),
        input_output_aliases={1: 0} if earlier else {},
        compiler_params=params(),
    )(flags, *earlier, grad, term, *parts)


def local(grad_out, weight_in, weight_out, pre_act):
    hids = lax.axis_size("hid")
    section = lax.axis_index("section")
    side = lax.axis_index("wid") % 2
    is_up = section == 1

    def scalars(active_section):
        active = (section == active_section).astype(jnp.int32)
        return jnp.stack([active, side, lax.axis_index("hid") % PARTS]).astype(jnp.int32)

    down, up = scalars(0), scalars(1)

    def within(active, distance, block, axis="wid"):
        size = lax.axis_size(axis)
        pairs = [(active * size + i, active * size + (i ^ distance)) for i in range(size)]
        return lax.ppermute(block, ("section", axis), pairs)

    def everywhere(distance, block, axis="hid"):
        size = lax.axis_size(axis)
        return lax.ppermute(block, axis, [(i, i ^ distance) for i in range(size)])

    mat_in = weight_in[0]
    mat_out = weight_out[0]
    quarter, hid_tile = mat_in.shape
    half = hid_tile // 2
    batches, batch_tokens, _ = grad_out.shape
    total = batches * batch_tokens
    unit = total // sum(SHARES)
    starts = [unit * sum(SHARES[:k]) for k in range(len(SHARES))]
    sizes = [unit * share for share in SHARES]
    chunks = range(len(SHARES))
    grad = grad_out.reshape(total, quarter)
    pre = pre_act[0].reshape(total, hid_tile)
    grads = [grad[starts[k] : starts[k] + sizes[k]] for k in chunks]

    split_out = split_rows(up, mat_out)

    hid_rows = divisor(half, 512)
    hid_steps = half // hid_rows
    part_rows = quarter // PARTS

    def in_order(*which):
        return lambda i, s, rows: ([(w, i * rows) for w in which], i * rows)

    def product_out(flags, mat, first_row, sources, prepare, tokens, kinds, base=None):
        return product(
            flags, mat, (hid_rows, quarter),
            lambda i, s: (first_row(s) + i * hid_rows, 0), hid_steps,
            sources, prepare, tokens, [(half, kind) for kind in kinds],
            functools.partial(in_order(*range(len(kinds))), rows=hid_rows), base,
        )

    def product_in(flags, place, sources, prepare, tokens, kind):
        return product(
            flags, mat_in, (part_rows, half), place, PARTS, sources, prepare, tokens,
            [(quarter, kind)], functools.partial(in_order(0), rows=part_rows),
        )

    def product_parts(flags, place, right, tokens, base):
        def part_of(i, s):
            return lax.bitwise_xor(s[2], (i + 1) % PARTS)

        return product(
            flags, mat_in, (part_rows, half), lambda i, s: place(part_of(i, s), s), PARTS,
            [right], None, tokens, [(part_rows, LOW)] * 3 + [(part_rows, F32)],
            lambda i, s: ([(i, 0)], part_of(i, s) * part_rows), base,
        )

    def scatter_hid(active, parts):
        *others, own = parts
        got = [within(active, d + 1, part, "hid") for d, part in enumerate(others)]
        for part in got:
            own = own + part.astype(F32)
        distance = PARTS
        while distance < hids:
            own = own + within(active, distance, own, "hid")
            distance *= 2
        return own.astype(LOW)

    class Steps:
        def __init__(self):
            self.last = None

        def after(self, value):
            if self.last is None:
                return value
            return lax.optimization_barrier((value, self.last))[0]

    steps = Steps()
    hidden_full, hidden_other, slopes, parts_out, terms, gathered = {}, {}, {}, {}, {}, {}
    up_full, up_other, up_parts, up_terms, lasts = {}, {}, {}, {}, {}

    def down_hidden(k):
        tokens = sizes[k]
        sent, low = product_out(
            steps.after(down), mat_out, lambda s: (1 - s[1]) * half, [grads[k]], turned,
            tokens, (LOW,),
        )
        got = within(0, 1, sent)
        full, low_grad = product_out(
            down, mat_out, lambda s: s[1] * half, [low], None, tokens, (F32, LOW), got
        )
        steps.last = low_grad
        if k > 0:
            low_grad = lax.optimization_barrier((low_grad, hidden_other[k - 1]))[0]
        hidden_full[k], hidden_other[k] = full, within(0, 2, low_grad)

    def slope(k):
        slopes[k] = slope_of(steps.after(down), pre, starts[k], sizes[k], half)
        steps.last = slopes[k]

    def down_back(k):
        tokens = sizes[k]
        full = steps.after(hidden_full[k])
        hidden = ((full + hidden_other[k].astype(F32)) * slopes[k]).astype(LOW)
        swapped = within(0, 1, hidden)
        (partial,) = product_in(
            down, lambda i, s: (i * part_rows, s[1] * half), [hidden], None, tokens, F32
        )
        parts_out[k] = product_parts(
            down, lambda i, s: (i * part_rows, (1 - s[1]) * half), swapped, tokens, partial
        )
        steps.last = parts_out[k][0]

    def cross(k):
        *others, own = parts_out[k]
        terms[k] = scatter_hid(0, others + [steps.after(own)])
        crossed = lax.ppermute(terms[k], "section", [(0, 1)])
        steps.last = crossed
        gathered[k] = [crossed] + [within(1, d, crossed, "hid") for d in range(1, PARTS)]

    def up_hidden(k):
        tokens = sizes[k]
        low, up_terms[k] = join(steps.after(up), grads[k], gathered[k])
        low_other = within(1, 1, low)
        (partial,) = product_out(
            up, split_out, lambda s: s[1] * half, [low], None, tokens, (F32,)
        )
        full, low_grad = product_out(
            up, split_out, lambda s: (1 - s[1]) * half, [low_other], None, tokens, (F32, LOW), partial
        )
        steps.last = low_grad
        if k > 0:
            low_grad = lax.optimization_barrier((low_grad, up_other[k - 1]))[0]
        up_full[k], up_other[k] = full, within(1, 2, low_grad)

    def place(part, core):
        row = core * (PARTS // 2) + part % (PARTS // 2)
        return row * part_rows, part // (PARTS // 2) * half

    def up_back(k):
        tokens = sizes[k]
        sent, hidden = product_in(
            steps.after(up), lambda i, s: place(i, 1 - s[1]),
            [up_full[k], up_other[k], slopes[k]], hidden_of, tokens, F32,
        )
        got = within(1, 1, sent)
        up_parts[k] = product_parts(up, lambda i, s: place(i, s[1]), hidden, tokens, got)
        steps.last = up_parts[k][0]

    def gather(k):
        *others, own = up_parts[k]
        last = jnp.where(is_up, scatter_hid(1, others + [steps.after(own)]), terms[k])
        steps.last = last
        lasts[k] = [last] + [everywhere(d, last) for d in range(1, PARTS)]

    def down_first(k):
        if k < len(SHARES):
            down_hidden(k)
            slope(k)

    def crossing(k):
        if k < len(SHARES):
            cross(k)
            up_hidden(k)

    down_first(0)
    down_first(1)
    down_back(0)
    down_first(2)
    crossing(0)
    for k in chunks:
        if k + 1 < len(SHARES):
            down_back(k + 1)
            down_first(k + 3)
        if k == 0:
            up_back(0)
        crossing(k + 1)
        if k > 0:
            up_back(k)
        gather(k)
    out = None
    for k in chunks:
        out = finish(up, out, grad, starts[k], up_terms[k], lasts[k])
    return out.reshape(1, batches, batch_tokens, quarter)


def solution(mesh):
    return jax.shard_map(
        local,
        mesh=mesh,
        in_specs=(
            P(None, None, "wid"),
            P("section", "wid", "hid"),
            P("section", "hid", "wid"),
            P("section", None, None, "hid"),
        ),
        out_specs=P("section", None, None, "wid"),
        check_vma=False,
    )
```

```python
import jax
import jax.numpy as jnp
from jax import lax
from jax.experimental import pallas as pl
from jax.experimental.pallas import tpu as pltpu
from jax.sharding import PartitionSpec as P

SHARES = (1, 1)
PARTS = 4
LANES = 128
WEIGHT = 4096
LIMIT = 46 * 1024 * 1024
LOW = jnp.bfloat16
F32 = jnp.float32


def gelu_slope(pre):
    normal_cdf = 0.5 * (1.0 + lax.erf(pre * 0.7071067811865476))
    density = jnp.exp(-0.5 * pre * pre) * 0.3989422804014327
    return normal_cdf + pre * density


def params():
    return pltpu.CompilerParams(vmem_limit_bytes=LIMIT)


def divisor(size, most):
    return max(r for r in range(16, most + 1, 16) if size % r == 0)


SMEM = pl.BlockSpec(memory_space=pltpu.SMEM)
VMEM = pl.BlockSpec(memory_space=pltpu.VMEM)
ANY = pl.BlockSpec(memory_space=pl.ANY)


def product(flags, mat, block, place, steps, sources, prepare, tokens, outs, base=None, base_row=None, apart=False):
    rows, depth = block
    slots = min(4, steps)
    bare = prepare is None
    count = len(sources)

    def body(s, mat_ref, *refs):
        source_refs, refs = refs[:count], refs[count:]
        base_ref = None
        if base is not None:
            base_ref, refs = refs[0], refs[1:]
        out_refs, (buf, sem) = refs[:-2], refs[-2:]

        def fetch(i):
            row, col = place(i, s)
            piece = mat_ref.at[pl.ds(pl.multiple_of(row, 16), rows), pl.ds(pl.multiple_of(col, LANES), depth)]
            slot = lax.rem(i, slots)
            return pltpu.make_async_copy(piece, buf.at[slot], sem.at[slot])

        @pl.when(s[0] == 1)
        def _():
            for i in range(slots):
                fetch(i).start()
            right_ref = source_refs[0]
            if not bare:
                right_ref = out_refs[-1]
                prepare(right_ref, *source_refs)

            @pl.loop(0, steps)
            def _(i):
                fetch(i).wait()
                got = jnp.dot(buf[lax.rem(i, slots)], right_ref[...], preferred_element_type=F32)

                @pl.when(i + slots < steps)
                def _():
                    fetch(i + slots).start()

                if base_ref is not None:
                    start = pl.multiple_of(base_row(i, s), 16)
                    got = got + base_ref[pl.ds(start, rows)].astype(F32)
                if apart:
                    for which, ref in enumerate(out_refs[:steps]):

                        @pl.when(i == which)
                        def _(ref=ref):
                            ref[...] = got.astype(ref.dtype)
                else:
                    at = pl.ds(pl.multiple_of(i * rows, 16), rows)
                    for ref in out_refs[: len(outs)]:
                        ref[at] = got.astype(ref.dtype)

    shapes = [jax.ShapeDtypeStruct((size, tokens), kind) for size, kind in outs]
    if not bare:
        shapes.append(jax.ShapeDtypeStruct((depth, tokens), LOW))
    return pl.pallas_call(
        body,
        in_specs=[SMEM, ANY] + [VMEM] * (count + (base is not None)),
        out_specs=[VMEM] * len(shapes),
        out_shape=shapes,
        scratch_shapes=[
            pltpu.VMEM((slots, rows, depth), LOW),
            pltpu.SemaphoreType.DMA((slots,)),
        ],
        compiler_params=params(),
        cost_estimate=pl.CostEstimate(
            flops=2 * tokens * rows * depth * steps // WEIGHT,
            bytes_accessed=2 * rows * depth * steps // WEIGHT,
            transcendentals=0,
        ),
    )(flags, mat, *sources, *([] if base is None else [base]))


def turned(right_ref, grad_ref):
    right_ref[...] = grad_ref[...].T.astype(LOW)


def hidden_of(right_ref, own_ref, other_ref, slope_ref):
    total = own_ref[...] + other_ref[...].astype(F32)
    right_ref[...] = (total * slope_ref[...]).astype(LOW)


def split_rows(flags, mat):
    rows, cols = mat.shape
    step = 256
    half = step // 2
    count = rows // step
    slots = 4

    def body(s, mat_ref, out_ref, buf, done, sem_in, sem_out):
        def fetch(i, slot):
            piece = mat_ref.at[pl.ds(pl.multiple_of(i * step, step), step)]
            return pltpu.make_async_copy(piece, buf.at[slot], sem_in.at[slot])

        def put(i, slot):
            piece = out_ref.at[:, pl.ds(pl.multiple_of(i * half, half), half)]
            return pltpu.make_async_copy(done.at[slot], piece, sem_out.at[slot])

        @pl.when(s[0] == 1)
        def _():
            to = lax.broadcasted_iota(jnp.int32, (step, step), 0)
            source = lax.broadcasted_iota(jnp.int32, (step, step), 1)
            wanted = jnp.where(to < half, 2 * to, 2 * (to - half) + 1)
            pick = jnp.where(source == wanted, 1.0, 0.0).astype(LOW)
            for i in range(slots):
                fetch(i, i).start()

            @pl.loop(0, count // slots)
            def _(turn):
                for slot in range(slots):
                    i = turn * slots + slot
                    fetch(i, slot).wait()

                    @pl.when(turn > 0)
                    def _():
                        put(i - slots, slot).wait()

                    got = jnp.dot(pick, buf[slot], preferred_element_type=F32).astype(LOW)
                    done[slot, 0] = got[:half]
                    done[slot, 1] = got[half:]

                    @pl.when(turn < count // slots - 1)
                    def _():
                        fetch(i + slots, slot).start()

                    put(i, slot).start()

            for slot in range(slots):
                put(count - slots + slot, slot).wait()

    out = pl.pallas_call(
        body,
        in_specs=[SMEM, ANY],
        out_specs=ANY,
        out_shape=jax.ShapeDtypeStruct((2, rows // 2, cols), LOW),
        scratch_shapes=[
            pltpu.VMEM((slots, step, cols), LOW),
            pltpu.VMEM((slots, 2, half, cols), LOW),
            pltpu.SemaphoreType.DMA((slots,)),
            pltpu.SemaphoreType.DMA((slots,)),
        ],
        compiler_params=params(),
        cost_estimate=pl.CostEstimate(
            flops=2 * rows * step * cols // WEIGHT, bytes_accessed=4 * rows * cols // WEIGHT, transcendentals=0
        ),
    )(flags, mat)
    return out.reshape(rows, cols)


def slope_of(flags, pre, start, tokens, half):
    cols = divisor(half, 768)
    per_half = half // cols

    def body(s, pre_ref, out_ref):
        out_ref[...] = gelu_slope(pre_ref[...]).T

    return pl.pallas_call(
        body,
        grid_spec=pltpu.PrefetchScalarGridSpec(
            num_scalar_prefetch=1,
            grid=(tokens // LANES, per_half),
            in_specs=[
                pl.BlockSpec((LANES, cols), lambda i, j, s: (start // LANES + i, s[1] * per_half + j))
            ],
            out_specs=pl.BlockSpec((cols, LANES), lambda i, j, s: (j, i)),
        ),
        out_shape=jax.ShapeDtypeStruct((half, tokens), F32),
        compiler_params=params(),
        cost_estimate=pl.CostEstimate(
            flops=half * tokens // WEIGHT, bytes_accessed=8 * half * tokens // WEIGHT, transcendentals=0
        ),
    )(flags, pre)


def join(flags, grad, parts):
    tokens, columns = grad.shape
    width = columns // PARTS

    def body(s, grad_ref, *refs):
        part_refs, (low_ref, term_ref) = refs[:PARTS], refs[PARTS:]

        @pl.when(s[0] == 1)
        def _():
            for slot, ref in enumerate(part_refs):
                start = pl.multiple_of(lax.bitwise_xor(s[2], slot) * width, LANES)
                term = ref[...]
                term_ref[pl.ds(start, width)] = term
                total = grad_ref[:, pl.ds(start, width)].T + term.astype(F32)
                low_ref[pl.ds(start, width)] = total.astype(LOW)

    shape = jax.ShapeDtypeStruct((columns, tokens), LOW)
    return pl.pallas_call(
        body,
        in_specs=[SMEM] + [VMEM] * (1 + PARTS),
        out_specs=[VMEM, VMEM],
        out_shape=[shape, shape],
        compiler_params=params(),
        cost_estimate=pl.CostEstimate(
            flops=4 * columns * tokens, bytes_accessed=4 * columns * tokens, transcendentals=0
        ),
    )(flags, grad, *parts)


def finish(flags, out, grad, start, term, parts):
    columns, tokens = term.shape
    width = columns // PARTS
    total_tokens = grad.shape[0]

    def body(s, *refs):
        grad_ref, term_ref, *part_refs = refs[int(out is not None) : -2]
        out_ref, joined = refs[-2:]
        for slot, ref in enumerate(part_refs):
            start = pl.multiple_of(lax.bitwise_xor(s[2], slot) * width, LANES)
            joined[pl.ds(start, width)] = ref[...]

        @pl.when(s[0] == 0)
        def _():
            out_ref[...] = grad_ref[...] + joined[...].astype(F32).T

        @pl.when(s[0] == 1)
        def _():
            source = lax.broadcasted_iota(jnp.int32, (2 * LANES, 2 * LANES), 1)
            to = lax.broadcasted_iota(jnp.int32, (2 * LANES, 2 * LANES), 0)
            wanted = jnp.where(source < LANES, 2 * source, 2 * (source - LANES) + 1)
            pick = jnp.where(to == wanted, 1.0, 0.0).astype(LOW)
            for group in range(columns // (2 * LANES)):
                even_at = group * LANES
                odd_at = columns // 2 + group * LANES
                even = joined[even_at : even_at + LANES]
                odd = joined[odd_at : odd_at + LANES]
                pair = jnp.concatenate([even, odd], axis=0)
                woven = jnp.dot(pick, pair, preferred_element_type=F32)
                at = slice(group * 2 * LANES, (group + 1) * 2 * LANES)
                first = term_ref[at].astype(F32).T
                out_ref[:, at] = grad_ref[:, at] + first + woven.T

    earlier = [] if out is None else [out]
    piece = pl.BlockSpec((width, LANES), lambda i, s: (0, i))
    rows = pl.BlockSpec((LANES, columns), lambda i, s: (start // LANES + i, 0))
    return pl.pallas_call(
        body,
        grid_spec=pltpu.PrefetchScalarGridSpec(
            num_scalar_prefetch=1,
            grid=(tokens // LANES,),
            in_specs=[ANY] * len(earlier)
            + [rows, pl.BlockSpec((columns, LANES), lambda i, s: (0, i))]
            + [piece] * PARTS,
            out_specs=rows,
            scratch_shapes=[pltpu.VMEM((columns, LANES), LOW)],
        ),
        out_shape=jax.ShapeDtypeStruct((total_tokens, columns), F32),
        input_output_aliases={1: 0} if earlier else {},
        compiler_params=params(),
    )(flags, *earlier, grad, term, *parts)


def local(grad_out, weight_in, weight_out, pre_act):
    hids = lax.axis_size("hid")
    section = lax.axis_index("section")
    side = lax.axis_index("wid") % 2
    is_up = section == 1

    def scalars(active_section):
        active = (section == active_section).astype(jnp.int32)
        return jnp.stack([active, side, lax.axis_index("hid") % PARTS]).astype(jnp.int32)

    down, up = scalars(0), scalars(1)

    def within(active, distance, block, axis="wid"):
        size = lax.axis_size(axis)
        pairs = [(active * size + i, active * size + (i ^ distance)) for i in range(size)]
        return lax.ppermute(block, ("section", axis), pairs)

    def everywhere(distance, block, axis="hid"):
        size = lax.axis_size(axis)
        return lax.ppermute(block, axis, [(i, i ^ distance) for i in range(size)])

    mat_in = weight_in[0]
    mat_out = weight_out[0]
    quarter, hid_tile = mat_in.shape
    half = hid_tile // 2
    batches, batch_tokens, _ = grad_out.shape
    total = batches * batch_tokens
    unit = total // sum(SHARES)
    starts = [unit * sum(SHARES[:k]) for k in range(len(SHARES))]
    sizes = [unit * share for share in SHARES]
    chunks = range(len(SHARES))
    grad = grad_out.reshape(total, quarter)
    pre = pre_act[0].reshape(total, hid_tile)
    grads = [grad[starts[k] : starts[k] + sizes[k]] for k in chunks]

    split_out = split_rows(up, mat_out)

    hid_rows = divisor(half, 512)
    hid_steps = half // hid_rows
    part_rows = quarter // PARTS

    def product_out(flags, mat, first_row, sources, prepare, tokens, kinds, base=None):
        return product(
            flags, mat, (hid_rows, quarter),
            lambda i, s: (first_row(s) + i * hid_rows, 0), hid_steps,
            sources, prepare, tokens, [(half, kind) for kind in kinds],
            base, lambda i, s: i * hid_rows,
        )

    def product_in(flags, place, sources, prepare, tokens, kind):
        return product(
            flags, mat_in, (part_rows, half), place, PARTS, sources, prepare, tokens,
            [(quarter, kind)],
        )

    def product_parts(flags, place, right, tokens, base):
        def part_of(i, s):
            return lax.bitwise_xor(s[2], lax.rem(i + 1, PARTS))

        return product(
            flags, mat_in, (part_rows, half), lambda i, s: place(part_of(i, s), s), PARTS,
            [right], None, tokens, [(part_rows, LOW)] * 3 + [(part_rows, F32)],
            base, lambda i, s: part_of(i, s) * part_rows, True,
        )

    def scatter_hid(active, parts):
        *others, own = parts
        got = [within(active, d + 1, part, "hid") for d, part in enumerate(others)]
        for part in got:
            own = own + part.astype(F32)
        distance = PARTS
        while distance < hids:
            own = own + within(active, distance, own, "hid")
            distance *= 2
        return own.astype(LOW)

    class Steps:
        def __init__(self):
            self.last = None

        def after(self, value):
            if self.last is None:
                return value
            return lax.optimization_barrier((value, self.last))[0]

    steps = Steps()
    steps.last = split_out
    hidden_full, hidden_other, slopes, parts_out, terms, gathered = {}, {}, {}, {}, {}, {}
    lows, core_got = {}, {}
    up_full, up_other, up_parts, up_terms, lasts = {}, {}, {}, {}, {}

    def down_send(k):
        sent, lows[k] = product_out(
            steps.after(down), mat_out, lambda s: (1 - s[1]) * half, [grads[k]], turned,
            sizes[k], (LOW,),
        )
        steps.last = sent
        core_got[k] = within(0, 1, sent)

    def down_hidden(k):
        full, low_grad = product_out(
            steps.after(down), mat_out, lambda s: s[1] * half, [lows[k]], None, sizes[k],
            (F32, LOW), core_got[k],
        )
        steps.last = low_grad
        if k > 0:
            low_grad = lax.optimization_barrier((low_grad, hidden_other[k - 1]))[0]
        hidden_full[k], hidden_other[k] = full, within(0, 2, low_grad)

    def slope(k):
        slopes[k] = slope_of(steps.after(down), pre, starts[k], sizes[k], half)
        steps.last = slopes[k]

    def down_back(k):
        tokens = sizes[k]
        full = steps.after(hidden_full[k])
        hidden = ((full + hidden_other[k].astype(F32)) * slopes[k]).astype(LOW)
        swapped = within(0, 1, hidden)
        (partial,) = product_in(
            down, lambda i, s: (i * part_rows, s[1] * half), [hidden], None, tokens, F32
        )
        parts_out[k] = product_parts(
            down, lambda i, s: (i * part_rows, (1 - s[1]) * half), swapped, tokens, partial
        )
        steps.last = parts_out[k][0]

    def cross(k):
        *others, own = parts_out[k]
        terms[k] = scatter_hid(0, others + [steps.after(own)])
        crossed = lax.ppermute(terms[k], "section", [(0, 1)])
        steps.last = crossed
        gathered[k] = [crossed] + [within(1, d, crossed, "hid") for d in range(1, PARTS)]

    def up_hidden(k):
        tokens = sizes[k]
        low, up_terms[k] = join(steps.after(up), grads[k], gathered[k])
        low_other = within(1, 1, low)
        (partial,) = product_out(
            up, split_out, lambda s: s[1] * half, [low], None, tokens, (F32,)
        )
        full, low_grad = product_out(
            up, split_out, lambda s: (1 - s[1]) * half, [low_other], None, tokens, (F32, LOW), partial
        )
        steps.last = low_grad
        if k > 0:
            low_grad = lax.optimization_barrier((low_grad, up_other[k - 1]))[0]
        up_full[k], up_other[k] = full, within(1, 2, low_grad)

    def place(part, core):
        row = core * (PARTS // 2) + lax.rem(part, PARTS // 2)
        return row * part_rows, lax.div(part, PARTS // 2) * half

    def up_back(k):
        tokens = sizes[k]
        sent, hidden = product_in(
            steps.after(up), lambda i, s: place(i, 1 - s[1]),
            [up_full[k], up_other[k], slopes[k]], hidden_of, tokens, F32,
        )
        got = within(1, 1, sent)
        up_parts[k] = product_parts(up, lambda i, s: place(i, s[1]), hidden, tokens, got)
        steps.last = up_parts[k][0]

    def gather(k):
        *others, own = up_parts[k]
        last = jnp.where(is_up, scatter_hid(1, others + [steps.after(own)]), terms[k])
        steps.last = last
        lasts[k] = [last] + [everywhere(d, last) for d in range(1, PARTS)]

    for k in chunks:
        down_send(k)
    for k in chunks:
        down_hidden(k)
    for k in chunks:
        slope(k)
    for k in chunks:
        down_back(k)
        cross(k)
        up_hidden(k)
    for k in chunks:
        up_back(k)
        gather(k)
    out = None
    for k in chunks:
        out = finish(up, out, grad, starts[k], up_terms[k], lasts[k])
    return out.reshape(1, batches, batch_tokens, quarter)


def solution(mesh):
    return jax.shard_map(
        local,
        mesh=mesh,
        in_specs=(
            P(None, None, "wid"),
            P("section", "wid", "hid"),
            P("section", "hid", "wid"),
            P("section", None, None, "hid"),
        ),
        out_specs=P("section", None, None, "wid"),
        check_vma=False,
    )
```

```python
import jax
import jax.numpy as jnp
from jax import lax
from jax.experimental import pallas as pl
from jax.experimental.pallas import tpu as pltpu
from jax.sharding import PartitionSpec as P

SHARES = (1, 1)
PARTS = 4
LANES = 128
WEIGHT = 4096
LIMIT = 46 * 1024 * 1024
LOW = jnp.bfloat16
F32 = jnp.float32


def gelu_slope(pre):
    normal_cdf = 0.5 * (1.0 + lax.erf(pre * 0.7071067811865476))
    density = jnp.exp(-0.5 * pre * pre) * 0.3989422804014327
    return normal_cdf + pre * density


def params():
    return pltpu.CompilerParams(vmem_limit_bytes=LIMIT)


def divisor(size, most):
    return max(r for r in range(16, most + 1, 16) if size % r == 0)


SMEM = pl.BlockSpec(memory_space=pltpu.SMEM)
VMEM = pl.BlockSpec(memory_space=pltpu.VMEM)
ANY = pl.BlockSpec(memory_space=pl.ANY)


def product(flags, mat, block, place, steps, sources, prepare, tokens, outs, base=None, base_row=None, apart=False, first=None):
    rows, depth = block
    slots = min(4, steps)
    bare = prepare is None
    count = len(sources)

    def body(s, mat_ref, *refs):
        source_refs, refs = refs[:count], refs[count:]
        base_ref = None
        if base is not None:
            base_ref, refs = refs[0], refs[1:]
        if first is not None:
            chunk_ref, chunk_sem = refs[-2:]
            refs = refs[:-2]
        out_refs, (buf, sem) = refs[:-2], refs[-2:]

        def fetch(i):
            row, col = place(i, s)
            piece = mat_ref.at[pl.ds(pl.multiple_of(row, 16), rows), pl.ds(pl.multiple_of(col, LANES), depth)]
            slot = lax.rem(i, slots)
            return pltpu.make_async_copy(piece, buf.at[slot], sem.at[slot])

        @pl.when(s[0] == 1)
        def _():
            given = source_refs
            if first is not None:
                piece = source_refs[0].at[pl.ds(first, tokens)]
                chunk = pltpu.make_async_copy(piece, chunk_ref, chunk_sem)
                chunk.start()
                given = [chunk_ref]
            for i in range(slots):
                fetch(i).start()
            if first is not None:
                chunk.wait()
            right_ref = source_refs[0]
            if not bare:
                right_ref = out_refs[-1]
                prepare(right_ref, *given)

            @pl.loop(0, steps)
            def _(i):
                fetch(i).wait()
                got = jnp.dot(buf[lax.rem(i, slots)], right_ref[...], preferred_element_type=F32)

                @pl.when(i + slots < steps)
                def _():
                    fetch(i + slots).start()

                if base_ref is not None:
                    start = pl.multiple_of(base_row(i, s), 16)
                    got = got + base_ref[pl.ds(start, rows)].astype(F32)
                if apart:
                    for which, ref in enumerate(out_refs[:steps]):

                        @pl.when(i == which)
                        def _(ref=ref):
                            ref[...] = got.astype(ref.dtype)
                else:
                    for ref, (size, begin, _) in zip(out_refs, outs):

                        @pl.when((i * rows >= begin) & (i * rows < begin + size))
                        def _(ref=ref, begin=begin):
                            at = pl.multiple_of(i * rows - begin, 16)
                            ref[pl.ds(at, rows)] = got.astype(ref.dtype)

    shapes = [jax.ShapeDtypeStruct((size, tokens), kind) for size, _, kind in outs]
    if not bare:
        shapes.append(jax.ShapeDtypeStruct((depth, tokens), LOW))
    return pl.pallas_call(
        body,
        in_specs=[SMEM, ANY]
        + [VMEM if first is None else ANY] * count
        + [VMEM] * (base is not None),
        out_specs=[VMEM] * len(shapes),
        out_shape=shapes,
        scratch_shapes=[
            pltpu.VMEM((slots, rows, depth), LOW),
            pltpu.SemaphoreType.DMA((slots,)),
        ]
        + ([] if first is None else [pltpu.VMEM((tokens, depth), F32), pltpu.SemaphoreType.DMA(())]),
        compiler_params=params(),
        cost_estimate=pl.CostEstimate(
            flops=2 * tokens * rows * depth * steps // WEIGHT,
            bytes_accessed=2 * rows * depth * steps // WEIGHT,
            transcendentals=0,
        ),
    )(flags, mat, *sources, *([] if base is None else [base]))


def turned(right_ref, grad_ref):
    right_ref[...] = grad_ref[...].T.astype(LOW)


def hidden_of(right_ref, own_ref, slope_ref, *other_refs):
    row = 0
    for other_ref in other_refs:
        at = slice(row, row + other_ref.shape[0])
        total = own_ref[at] + other_ref[...].astype(F32)
        right_ref[at] = (total * slope_ref[at]).astype(LOW)
        row = at.stop


def hidden(flags, own, slope, others):
    def body(s, own_ref, slope_ref, *refs):
        @pl.when(s[0] == 1)
        def _():
            hidden_of(refs[-1], own_ref, slope_ref, *refs[:-1])

    return pl.pallas_call(
        body,
        in_specs=[SMEM] + [VMEM] * (2 + len(others)),
        out_specs=VMEM,
        out_shape=jax.ShapeDtypeStruct(own.shape, LOW),
        compiler_params=params(),
        cost_estimate=pl.CostEstimate(
            flops=own.size // WEIGHT, bytes_accessed=own.size // WEIGHT, transcendentals=0
        ),
    )(flags, own, slope, *others)


def split_rows(flags, mat):
    rows, cols = mat.shape
    step = 256
    half = step // 2
    count = rows // step
    slots = 4

    def body(s, mat_ref, out_ref, buf, done, sem_in, sem_out):
        def fetch(i, slot):
            piece = mat_ref.at[pl.ds(pl.multiple_of(i * step, step), step)]
            return pltpu.make_async_copy(piece, buf.at[slot], sem_in.at[slot])

        def put(i, slot):
            piece = out_ref.at[:, pl.ds(pl.multiple_of(i * half, half), half)]
            return pltpu.make_async_copy(done.at[slot], piece, sem_out.at[slot])

        @pl.when(s[0] == 1)
        def _():
            to = lax.broadcasted_iota(jnp.int32, (step, step), 0)
            source = lax.broadcasted_iota(jnp.int32, (step, step), 1)
            wanted = jnp.where(to < half, 2 * to, 2 * (to - half) + 1)
            pick = jnp.where(source == wanted, 1.0, 0.0).astype(LOW)
            for i in range(slots):
                fetch(i, i).start()

            @pl.loop(0, count // slots)
            def _(turn):
                for slot in range(slots):
                    i = turn * slots + slot
                    fetch(i, slot).wait()

                    @pl.when(turn > 0)
                    def _():
                        put(i - slots, slot).wait()

                    got = jnp.dot(pick, buf[slot], preferred_element_type=F32).astype(LOW)
                    done[slot, 0] = got[:half]
                    done[slot, 1] = got[half:]

                    @pl.when(turn < count // slots - 1)
                    def _():
                        fetch(i + slots, slot).start()

                    put(i, slot).start()

            for slot in range(slots):
                put(count - slots + slot, slot).wait()

    out = pl.pallas_call(
        body,
        in_specs=[SMEM, ANY],
        out_specs=ANY,
        out_shape=jax.ShapeDtypeStruct((2, rows // 2, cols), LOW),
        scratch_shapes=[
            pltpu.VMEM((slots, step, cols), LOW),
            pltpu.VMEM((slots, 2, half, cols), LOW),
            pltpu.SemaphoreType.DMA((slots,)),
            pltpu.SemaphoreType.DMA((slots,)),
        ],
        compiler_params=params(),
        cost_estimate=pl.CostEstimate(
            flops=2 * rows * step * cols // WEIGHT, bytes_accessed=4 * rows * cols // WEIGHT, transcendentals=0
        ),
    )(flags, mat)
    return out.reshape(rows, cols)


def slope_of(flags, pre, start, tokens, half):
    cols = divisor(half, 768)
    per_half = half // cols

    def body(s, pre_ref, out_ref):
        out_ref[...] = gelu_slope(pre_ref[...]).T

    return pl.pallas_call(
        body,
        grid_spec=pltpu.PrefetchScalarGridSpec(
            num_scalar_prefetch=1,
            grid=(tokens // LANES, per_half),
            in_specs=[
                pl.BlockSpec((LANES, cols), lambda i, j, s: (start // LANES + i, s[1] * per_half + j))
            ],
            out_specs=pl.BlockSpec((cols, LANES), lambda i, j, s: (j, i)),
        ),
        out_shape=jax.ShapeDtypeStruct((half, tokens), F32),
        compiler_params=params(),
        cost_estimate=pl.CostEstimate(
            flops=half * tokens // WEIGHT, bytes_accessed=8 * half * tokens // WEIGHT, transcendentals=0
        ),
    )(flags, pre)


def join(flags, grad, parts):
    tokens, columns = grad.shape
    width = columns // PARTS

    def body(s, grad_ref, *refs):
        part_refs, (low_ref, term_ref) = refs[:PARTS], refs[PARTS:]

        @pl.when(s[0] == 1)
        def _():
            for slot, ref in enumerate(part_refs):
                start = pl.multiple_of(lax.bitwise_xor(s[2], slot) * width, LANES)
                term = ref[...]
                term_ref[pl.ds(start, width)] = term
                total = grad_ref[:, pl.ds(start, width)].T + term.astype(F32)
                low_ref[pl.ds(start, width)] = total.astype(LOW)

    shape = jax.ShapeDtypeStruct((columns, tokens), LOW)
    return pl.pallas_call(
        body,
        in_specs=[SMEM] + [VMEM] * (1 + PARTS),
        out_specs=[VMEM, VMEM],
        out_shape=[shape, shape],
        compiler_params=params(),
        cost_estimate=pl.CostEstimate(
            flops=4 * columns * tokens, bytes_accessed=4 * columns * tokens, transcendentals=0
        ),
    )(flags, grad, *parts)


def finish(flags, out, grad, start, term, parts):
    columns, tokens = term.shape
    width = columns // PARTS
    total_tokens = grad.shape[0]

    def body(s, *refs):
        grad_ref, term_ref, *part_refs = refs[int(out is not None) : -2]
        out_ref, joined = refs[-2:]
        for slot, ref in enumerate(part_refs):
            start = pl.multiple_of(lax.bitwise_xor(s[2], slot) * width, LANES)
            joined[pl.ds(start, width)] = ref[...]

        @pl.when(s[0] == 0)
        def _():
            out_ref[...] = grad_ref[...] + joined[...].astype(F32).T

        @pl.when(s[0] == 1)
        def _():
            source = lax.broadcasted_iota(jnp.int32, (2 * LANES, 2 * LANES), 1)
            to = lax.broadcasted_iota(jnp.int32, (2 * LANES, 2 * LANES), 0)
            wanted = jnp.where(source < LANES, 2 * source, 2 * (source - LANES) + 1)
            pick = jnp.where(to == wanted, 1.0, 0.0).astype(LOW)
            for group in range(columns // (2 * LANES)):
                even_at = group * LANES
                odd_at = columns // 2 + group * LANES
                even = joined[even_at : even_at + LANES]
                odd = joined[odd_at : odd_at + LANES]
                pair = jnp.concatenate([even, odd], axis=0)
                woven = jnp.dot(pick, pair, preferred_element_type=F32)
                at = slice(group * 2 * LANES, (group + 1) * 2 * LANES)
                first = term_ref[at].astype(F32).T
                out_ref[:, at] = grad_ref[:, at] + first + woven.T

    earlier = [] if out is None else [out]
    piece = pl.BlockSpec((width, LANES), lambda i, s: (0, i))
    rows = pl.BlockSpec((LANES, columns), lambda i, s: (start // LANES + i, 0))
    return pl.pallas_call(
        body,
        grid_spec=pltpu.PrefetchScalarGridSpec(
            num_scalar_prefetch=1,
            grid=(tokens // LANES,),
            in_specs=[ANY] * len(earlier)
            + [rows, pl.BlockSpec((columns, LANES), lambda i, s: (0, i))]
            + [piece] * PARTS,
            out_specs=rows,
            scratch_shapes=[pltpu.VMEM((columns, LANES), LOW)],
        ),
        out_shape=jax.ShapeDtypeStruct((total_tokens, columns), F32),
        input_output_aliases={1: 0} if earlier else {},
        compiler_params=params(),
    )(flags, *earlier, grad, term, *parts)


def local(grad_out, weight_in, weight_out, pre_act):
    hids = lax.axis_size("hid")
    section = lax.axis_index("section")
    side = lax.axis_index("wid") % 2
    is_up = section == 1

    def scalars(active_section):
        active = (section == active_section).astype(jnp.int32)
        return jnp.stack([active, side, lax.axis_index("hid") % PARTS]).astype(jnp.int32)

    down, up = scalars(0), scalars(1)

    def within(active, distance, block, axis="wid"):
        size = lax.axis_size(axis)
        pairs = [(active * size + i, active * size + (i ^ distance)) for i in range(size)]
        return lax.ppermute(block, ("section", axis), pairs)

    def everywhere(distance, block, axis="hid"):
        size = lax.axis_size(axis)
        return lax.ppermute(block, axis, [(i, i ^ distance) for i in range(size)])

    mat_in = weight_in[0]
    mat_out = weight_out[0]
    quarter, hid_tile = mat_in.shape
    half = hid_tile // 2
    batches, batch_tokens, _ = grad_out.shape
    total = batches * batch_tokens
    unit = total // sum(SHARES)
    starts = [unit * sum(SHARES[:k]) for k in range(len(SHARES))]
    sizes = [unit * share for share in SHARES]
    chunks = range(len(SHARES))
    grad = grad_out.reshape(total, quarter)
    pre = pre_act[0].reshape(total, hid_tile)
    grads = [grad[starts[k] : starts[k] + sizes[k]] for k in chunks]

    split_out = split_rows(up, mat_out)

    hid_rows = divisor(half // 2, 512)
    hid_steps = half // hid_rows
    part_rows = quarter // PARTS

    def product_out(flags, mat, first_row, sources, prepare, tokens, outs, base=None, first=None):
        return product(
            flags, mat, (hid_rows, quarter),
            lambda i, s: (first_row(s) + i * hid_rows, 0), hid_steps,
            sources, prepare, tokens, outs, base, lambda i, s: i * hid_rows, first=first,
        )

    def in_pieces(k):
        count = 1 if k == 0 else 2
        size = half // count
        return [(half, 0, F32)] + [(size, n * size, LOW) for n in range(count)]

    def exchange(k, active, pieces, earlier):
        if k > 0:
            pieces = [lax.optimization_barrier((piece, earlier))[0] for piece in pieces]
        return [within(active, 2, piece) for piece in pieces]

    def product_in(flags, place, sources, prepare, tokens, kind):
        return product(
            flags, mat_in, (part_rows, half), place, PARTS, sources, prepare, tokens,
            [(quarter, 0, kind)],
        )

    def product_parts(flags, place, right, tokens, base):
        def part_of(i, s):
            return lax.bitwise_xor(s[2], lax.rem(i + 1, PARTS))

        return product(
            flags, mat_in, (part_rows, half), lambda i, s: place(part_of(i, s), s), PARTS,
            [right], None, tokens, [(part_rows, 0, LOW)] * 3 + [(part_rows, 0, F32)],
            base, lambda i, s: part_of(i, s) * part_rows, True,
        )

    def scatter_hid(active, parts):
        *others, own = parts
        got = [within(active, d + 1, part, "hid") for d, part in enumerate(others)]
        for part in got:
            own = own + part.astype(F32)
        distance = PARTS
        while distance < hids:
            own = own + within(active, distance, own, "hid")
            distance *= 2
        return own.astype(LOW)

    class Steps:
        def __init__(self):
            self.last = None

        def after(self, value):
            if self.last is None:
                return value
            return lax.optimization_barrier((value, self.last))[0]

    steps = Steps()
    steps.last = split_out
    hidden_full, hidden_other, slopes, parts_out, terms, gathered = {}, {}, {}, {}, {}, {}
    lows, core_got = {}, {}
    up_full, up_other, up_parts, up_terms, lasts = {}, {}, {}, {}, {}

    def down_send(k):
        sent, lows[k] = product_out(
            steps.after(down), mat_out, lambda s: (1 - s[1]) * half, [grad], turned,
            sizes[k], [(half, 0, LOW)], first=starts[k],
        )
        steps.last = sent
        core_got[k] = within(0, 1, sent)

    def down_hidden(k):
        full, *pieces = product_out(
            steps.after(down), mat_out, lambda s: s[1] * half, [lows[k]], None, sizes[k],
            in_pieces(k), core_got[k],
        )
        steps.last = full
        hidden_full[k] = full
        hidden_other[k] = exchange(k, 0, pieces, hidden_other[k - 1][-1] if k else None)

    def slope(k):
        slopes[k] = slope_of(steps.after(down), pre, starts[k], sizes[k], half)
        steps.last = slopes[k]

    def down_back(k):
        tokens = sizes[k]
        right = hidden(steps.after(down), hidden_full[k], slopes[k], hidden_other[k])
        swapped = within(0, 1, right)
        (partial,) = product_in(
            down, lambda i, s: (i * part_rows, s[1] * half), [right], None, tokens, F32
        )
        parts_out[k] = product_parts(
            down, lambda i, s: (i * part_rows, (1 - s[1]) * half), swapped, tokens, partial
        )
        steps.last = parts_out[k][0]

    def cross(k):
        *others, own = parts_out[k]
        if k + 1 in hidden_other:
            own = lax.optimization_barrier((own, hidden_other[k + 1][0]))[0]
        terms[k] = scatter_hid(0, others + [steps.after(own)])
        crossed = lax.ppermute(terms[k], "section", [(0, 1)])
        steps.last = crossed
        gathered[k] = [crossed] + [within(1, d, crossed, "hid") for d in range(1, PARTS)]

    def up_hidden(k):
        tokens = sizes[k]
        low, up_terms[k] = join(steps.after(up), grads[k], gathered[k])
        low_other = within(1, 1, low)
        (partial,) = product_out(
            up, split_out, lambda s: s[1] * half, [low], None, tokens, [(half, 0, F32)]
        )
        full, *pieces = product_out(
            up, split_out, lambda s: (1 - s[1]) * half, [low_other], None, tokens,
            in_pieces(k), partial,
        )
        steps.last = full
        up_full[k] = full
        up_other[k] = exchange(k, 1, pieces, up_other[k - 1][-1] if k else None)

    def place(part, core):
        row = core * (PARTS // 2) + lax.rem(part, PARTS // 2)
        return row * part_rows, lax.div(part, PARTS // 2) * half

    def up_back(k):
        tokens = sizes[k]
        sent, right = product_in(
            steps.after(up), lambda i, s: place(i, 1 - s[1]),
            [up_full[k], slopes[k]] + up_other[k], hidden_of, tokens, F32,
        )
        got = within(1, 1, sent)
        up_parts[k] = product_parts(up, lambda i, s: place(i, s[1]), right, tokens, got)
        steps.last = up_parts[k][0]

    def gather(k):
        *others, own = up_parts[k]
        if k + 1 in up_other:
            own = lax.optimization_barrier((own, up_other[k + 1][0]))[0]
        last = jnp.where(is_up, scatter_hid(1, others + [steps.after(own)]), terms[k])
        steps.last = last
        lasts[k] = [last] + [everywhere(d, last) for d in range(1, PARTS)]

    for k in chunks:
        down_send(k)
    for k in chunks:
        down_hidden(k)
    for k in chunks:
        slope(k)
    down_back(0)
    out = None
    for k in chunks:
        cross(k)
        if k + 1 < len(SHARES):
            down_back(k + 1)
        up_hidden(k)
    for k in chunks:
        up_back(k)
        if k > 0:
            out = finish(steps.after(up), out, grad, starts[k - 1], up_terms[k - 1], lasts[k - 1])
            steps.last = out
        gather(k)
    out = finish(up, out, grad, starts[k], up_terms[k], lasts[k])
    return out.reshape(1, batches, batch_tokens, quarter)


def solution(mesh):
    return jax.shard_map(
        local,
        mesh=mesh,
        in_specs=(
            P(None, None, "wid"),
            P("section", "wid", "hid"),
            P("section", "hid", "wid"),
            P("section", None, None, "hid"),
        ),
        out_specs=P("section", None, None, "wid"),
        check_vma=False,
    )
```

```python
import jax
import jax.numpy as jnp
from jax import lax
from jax.experimental import pallas as pl
from jax.experimental.pallas import tpu as pltpu
from jax.sharding import PartitionSpec as P

SHARES = (1, 1)
PARTS = 4
LANES = 128
WEIGHT = 4096
LIMIT = 46 * 1024 * 1024
LOW = jnp.bfloat16
F32 = jnp.float32


def gelu_slope(pre):
    normal_cdf = 0.5 * (1.0 + lax.erf(pre * 0.7071067811865476))
    density = jnp.exp(-0.5 * pre * pre) * 0.3989422804014327
    return normal_cdf + pre * density


def params():
    return pltpu.CompilerParams(vmem_limit_bytes=LIMIT)


def divisor(size, most):
    return max(r for r in range(16, most + 1, 16) if size % r == 0)


SMEM = pl.BlockSpec(memory_space=pltpu.SMEM)
VMEM = pl.BlockSpec(memory_space=pltpu.VMEM)
ANY = pl.BlockSpec(memory_space=pl.ANY)


def product(flags, mat, block, place, steps, sources, prepare, tokens, outs, base=None, base_row=None, apart=False, first=None):
    rows, depth = block
    slots = min(4, steps)
    bare = prepare is None
    count = len(sources)

    def body(s, mat_ref, *refs):
        source_refs, refs = refs[:count], refs[count:]
        base_ref = None
        if base is not None:
            base_ref, refs = refs[0], refs[1:]
        if first is not None:
            chunk_ref, chunk_sem = refs[-2:]
            refs = refs[:-2]
        out_refs, (buf, sem) = refs[:-2], refs[-2:]

        def fetch(i):
            row, col = place(i, s)
            piece = mat_ref.at[pl.ds(pl.multiple_of(row, 16), rows), pl.ds(pl.multiple_of(col, LANES), depth)]
            slot = lax.rem(i, slots)
            return pltpu.make_async_copy(piece, buf.at[slot], sem.at[slot])

        @pl.when(s[0] == 1)
        def _():
            given = source_refs
            if first is not None:
                piece = source_refs[0].at[pl.ds(first, tokens)]
                chunk = pltpu.make_async_copy(piece, chunk_ref, chunk_sem)
                chunk.start()
                given = [chunk_ref]
            for i in range(slots):
                fetch(i).start()
            if first is not None:
                chunk.wait()
            right_ref = source_refs[0]
            if not bare:
                right_ref = out_refs[-1]
                prepare(right_ref, *given)

            @pl.loop(0, steps)
            def _(i):
                fetch(i).wait()
                got = jnp.dot(buf[lax.rem(i, slots)], right_ref[...], preferred_element_type=F32)

                @pl.when(i + slots < steps)
                def _():
                    fetch(i + slots).start()

                if base_ref is not None:
                    start = pl.multiple_of(base_row(i, s), 16)
                    got = got + base_ref[pl.ds(start, rows)].astype(F32)
                if apart:
                    for which, ref in enumerate(out_refs[:steps]):

                        @pl.when(i == which)
                        def _(ref=ref):
                            ref[...] = got.astype(ref.dtype)
                else:
                    for ref, (size, begin, _) in zip(out_refs, outs):

                        @pl.when((i * rows >= begin) & (i * rows < begin + size))
                        def _(ref=ref, begin=begin):
                            at = pl.multiple_of(i * rows - begin, 16)
                            ref[pl.ds(at, rows)] = got.astype(ref.dtype)

    shapes = [jax.ShapeDtypeStruct((size, tokens), kind) for size, _, kind in outs]
    if not bare:
        shapes.append(jax.ShapeDtypeStruct((depth, tokens), LOW))
    return pl.pallas_call(
        body,
        in_specs=[SMEM, ANY]
        + [VMEM if first is None else ANY] * count
        + [VMEM] * (base is not None),
        out_specs=[VMEM] * len(shapes),
        out_shape=shapes,
        scratch_shapes=[
            pltpu.VMEM((slots, rows, depth), LOW),
            pltpu.SemaphoreType.DMA((slots,)),
        ]
        + ([] if first is None else [pltpu.VMEM((tokens, depth), F32), pltpu.SemaphoreType.DMA(())]),
        compiler_params=params(),
        cost_estimate=pl.CostEstimate(
            flops=2 * tokens * rows * depth * steps // WEIGHT,
            bytes_accessed=2 * rows * depth * steps // WEIGHT,
            transcendentals=0,
        ),
    )(flags, mat, *sources, *([] if base is None else [base]))


def turned(right_ref, grad_ref):
    right_ref[...] = grad_ref[...].T.astype(LOW)


def hidden_of(right_ref, own_ref, slope_ref, *other_refs):
    row = 0
    for other_ref in other_refs:
        at = slice(row, row + other_ref.shape[0])
        total = own_ref[at] + other_ref[...].astype(F32)
        right_ref[at] = (total * slope_ref[at]).astype(LOW)
        row = at.stop


def hidden(flags, own, slope, others):
    def body(s, own_ref, slope_ref, *refs):
        @pl.when(s[0] == 1)
        def _():
            hidden_of(refs[-1], own_ref, slope_ref, *refs[:-1])

    return pl.pallas_call(
        body,
        in_specs=[SMEM] + [VMEM] * (2 + len(others)),
        out_specs=VMEM,
        out_shape=jax.ShapeDtypeStruct(own.shape, LOW),
        compiler_params=params(),
        cost_estimate=pl.CostEstimate(
            flops=own.size // WEIGHT, bytes_accessed=own.size // WEIGHT, transcendentals=0
        ),
    )(flags, own, slope, *others)


def split_rows(flags, mat):
    rows, cols = mat.shape
    step = 256
    half = step // 2
    count = rows // step
    slots = 4

    def body(s, mat_ref, out_ref, buf, done, sem_in, sem_out):
        def fetch(i, slot):
            piece = mat_ref.at[pl.ds(pl.multiple_of(i * step, step), step)]
            return pltpu.make_async_copy(piece, buf.at[slot], sem_in.at[slot])

        def put(i, slot):
            piece = out_ref.at[:, pl.ds(pl.multiple_of(i * half, half), half)]
            return pltpu.make_async_copy(done.at[slot], piece, sem_out.at[slot])

        @pl.when(s[0] == 1)
        def _():
            to = lax.broadcasted_iota(jnp.int32, (step, step), 0)
            source = lax.broadcasted_iota(jnp.int32, (step, step), 1)
            wanted = jnp.where(to < half, 2 * to, 2 * (to - half) + 1)
            pick = jnp.where(source == wanted, 1.0, 0.0).astype(LOW)
            for i in range(slots):
                fetch(i, i).start()

            @pl.loop(0, count // slots)
            def _(turn):
                for slot in range(slots):
                    i = turn * slots + slot
                    fetch(i, slot).wait()

                    @pl.when(turn > 0)
                    def _():
                        put(i - slots, slot).wait()

                    got = jnp.dot(pick, buf[slot], preferred_element_type=F32).astype(LOW)
                    done[slot, 0] = got[:half]
                    done[slot, 1] = got[half:]

                    @pl.when(turn < count // slots - 1)
                    def _():
                        fetch(i + slots, slot).start()

                    put(i, slot).start()

            for slot in range(slots):
                put(count - slots + slot, slot).wait()

    out = pl.pallas_call(
        body,
        in_specs=[SMEM, ANY],
        out_specs=ANY,
        out_shape=jax.ShapeDtypeStruct((2, rows // 2, cols), LOW),
        scratch_shapes=[
            pltpu.VMEM((slots, step, cols), LOW),
            pltpu.VMEM((slots, 2, half, cols), LOW),
            pltpu.SemaphoreType.DMA((slots,)),
            pltpu.SemaphoreType.DMA((slots,)),
        ],
        compiler_params=params(),
        cost_estimate=pl.CostEstimate(
            flops=2 * rows * step * cols // WEIGHT, bytes_accessed=4 * rows * cols // WEIGHT, transcendentals=0
        ),
    )(flags, mat)
    return out.reshape(rows, cols)


def slope_of(flags, pre, start, tokens, half):
    cols = divisor(half, 768)
    per_half = half // cols

    def body(s, pre_ref, out_ref):
        out_ref[...] = gelu_slope(pre_ref[...]).T

    return pl.pallas_call(
        body,
        grid_spec=pltpu.PrefetchScalarGridSpec(
            num_scalar_prefetch=1,
            grid=(tokens // LANES, per_half),
            in_specs=[
                pl.BlockSpec((LANES, cols), lambda i, j, s: (start // LANES + i, s[1] * per_half + j))
            ],
            out_specs=pl.BlockSpec((cols, LANES), lambda i, j, s: (j, i)),
        ),
        out_shape=jax.ShapeDtypeStruct((half, tokens), F32),
        compiler_params=params(),
        cost_estimate=pl.CostEstimate(
            flops=half * tokens // WEIGHT, bytes_accessed=8 * half * tokens // WEIGHT, transcendentals=0
        ),
    )(flags, pre)


def join(flags, grad, parts):
    tokens, columns = grad.shape
    width = columns // PARTS

    def body(s, grad_ref, *refs):
        part_refs, (low_ref, term_ref) = refs[:PARTS], refs[PARTS:]

        @pl.when(s[0] == 1)
        def _():
            for slot, ref in enumerate(part_refs):
                start = pl.multiple_of(lax.bitwise_xor(s[2], slot) * width, LANES)
                term = ref[...]
                term_ref[pl.ds(start, width)] = term
                total = grad_ref[:, pl.ds(start, width)].T + term.astype(F32)
                low_ref[pl.ds(start, width)] = total.astype(LOW)

    shape = jax.ShapeDtypeStruct((columns, tokens), LOW)
    return pl.pallas_call(
        body,
        in_specs=[SMEM] + [VMEM] * (1 + PARTS),
        out_specs=[VMEM, VMEM],
        out_shape=[shape, shape],
        compiler_params=params(),
        cost_estimate=pl.CostEstimate(
            flops=4 * columns * tokens, bytes_accessed=4 * columns * tokens, transcendentals=0
        ),
    )(flags, grad, *parts)


def finish(flags, out, grad, start, term, parts):
    columns, tokens = term.shape
    width = columns // PARTS
    total_tokens = grad.shape[0]

    def body(s, *refs):
        grad_ref, term_ref, *part_refs = refs[int(out is not None) : -2]
        out_ref, joined = refs[-2:]
        for slot, ref in enumerate(part_refs):
            start = pl.multiple_of(lax.bitwise_xor(s[2], slot) * width, LANES)
            joined[pl.ds(start, width)] = ref[...]

        @pl.when(s[0] == 0)
        def _():
            out_ref[...] = grad_ref[...] + joined[...].astype(F32).T

        @pl.when(s[0] == 1)
        def _():
            source = lax.broadcasted_iota(jnp.int32, (2 * LANES, 2 * LANES), 1)
            to = lax.broadcasted_iota(jnp.int32, (2 * LANES, 2 * LANES), 0)
            wanted = jnp.where(source < LANES, 2 * source, 2 * (source - LANES) + 1)
            pick = jnp.where(to == wanted, 1.0, 0.0).astype(LOW)
            for group in range(columns // (2 * LANES)):
                even_at = group * LANES
                odd_at = columns // 2 + group * LANES
                even = joined[even_at : even_at + LANES]
                odd = joined[odd_at : odd_at + LANES]
                pair = jnp.concatenate([even, odd], axis=0)
                woven = jnp.dot(pick, pair, preferred_element_type=F32)
                at = slice(group * 2 * LANES, (group + 1) * 2 * LANES)
                first = term_ref[at].astype(F32).T
                out_ref[:, at] = grad_ref[:, at] + first + woven.T

    earlier = [] if out is None else [out]
    piece = pl.BlockSpec((width, LANES), lambda i, s: (0, i))
    rows = pl.BlockSpec((LANES, columns), lambda i, s: (start // LANES + i, 0))
    return pl.pallas_call(
        body,
        grid_spec=pltpu.PrefetchScalarGridSpec(
            num_scalar_prefetch=1,
            grid=(tokens // LANES,),
            in_specs=[ANY] * len(earlier)
            + [rows, pl.BlockSpec((columns, LANES), lambda i, s: (0, i))]
            + [piece] * PARTS,
            out_specs=rows,
            scratch_shapes=[pltpu.VMEM((columns, LANES), LOW)],
        ),
        out_shape=jax.ShapeDtypeStruct((total_tokens, columns), F32),
        input_output_aliases={1: 0} if earlier else {},
        compiler_params=params(),
    )(flags, *earlier, grad, term, *parts)


def local(grad_out, weight_in, weight_out, pre_act):
    hids = lax.axis_size("hid")
    section = lax.axis_index("section")
    side = lax.axis_index("wid") % 2
    is_up = section == 1

    def scalars(active_section):
        active = (section == active_section).astype(jnp.int32)
        return jnp.stack([active, side, lax.axis_index("hid") % PARTS]).astype(jnp.int32)

    down, up = scalars(0), scalars(1)

    def within(active, distance, block, axis="wid"):
        size = lax.axis_size(axis)
        pairs = [(active * size + i, active * size + (i ^ distance)) for i in range(size)]
        return lax.ppermute(block, ("section", axis), pairs)

    def everywhere(distance, block, axis="hid"):
        size = lax.axis_size(axis)
        return lax.ppermute(block, axis, [(i, i ^ distance) for i in range(size)])

    mat_in = weight_in[0]
    mat_out = weight_out[0]
    quarter, hid_tile = mat_in.shape
    half = hid_tile // 2
    batches, batch_tokens, _ = grad_out.shape
    total = batches * batch_tokens
    unit = total // sum(SHARES)
    starts = [unit * sum(SHARES[:k]) for k in range(len(SHARES))]
    sizes = [unit * share for share in SHARES]
    chunks = range(len(SHARES))
    grad = grad_out.reshape(total, quarter)
    pre = pre_act[0].reshape(total, hid_tile)
    grads = [grad[starts[k] : starts[k] + sizes[k]] for k in chunks]

    split_out = split_rows(up, mat_out)

    hid_rows = divisor(half // 2, 512)
    hid_steps = half // hid_rows
    part_rows = quarter // PARTS

    def product_out(flags, mat, first_row, sources, prepare, tokens, outs, base=None, first=None):
        return product(
            flags, mat, (hid_rows, quarter),
            lambda i, s: (first_row(s) + i * hid_rows, 0), hid_steps,
            sources, prepare, tokens, outs, base, lambda i, s: i * hid_rows, first=first,
        )

    def in_pieces(*shares):
        blocks = [max(1, hid_steps * sum(shares[: n + 1]) // sum(shares)) for n in range(len(shares))]
        ends = [0] + [hid_rows * block for block in blocks]
        return [(half, 0, F32)] + [(ends[n + 1] - ends[n], ends[n], LOW) for n in range(len(shares))]

    def exchange(active, pieces, earlier):
        if earlier is not None:
            pieces = [lax.optimization_barrier((piece, earlier))[0] for piece in pieces]
        return [within(active, 2, piece) for piece in pieces]

    def detour(piece):
        size = lax.axis_size("wid")
        return lax.ppermute(piece, ("section", "wid"), [(i, size + (i ^ 2)) for i in range(size)])

    def returned(piece):
        size = lax.axis_size("wid")
        return lax.ppermute(piece, ("section", "wid"), [(size + i, i) for i in range(size)])

    def product_in(flags, place, sources, prepare, tokens, kind):
        return product(
            flags, mat_in, (part_rows, half), place, PARTS, sources, prepare, tokens,
            [(quarter, 0, kind)],
        )

    def product_parts(flags, place, right, tokens, base):
        def part_of(i, s):
            return lax.bitwise_xor(s[2], lax.rem(i + 1, PARTS))

        return product(
            flags, mat_in, (part_rows, half), lambda i, s: place(part_of(i, s), s), PARTS,
            [right], None, tokens, [(part_rows, 0, LOW)] * 3 + [(part_rows, 0, F32)],
            base, lambda i, s: part_of(i, s) * part_rows, True,
        )

    def scatter_hid(active, parts):
        *others, own = parts
        got = [within(active, d + 1, part, "hid") for d, part in enumerate(others)]
        for part in got:
            own = own + part.astype(F32)
        distance = PARTS
        while distance < hids:
            own = own + within(active, distance, own, "hid")
            distance *= 2
        return own.astype(LOW)

    class Steps:
        def __init__(self):
            self.last = None

        def after(self, value):
            if self.last is None:
                return value
            return lax.optimization_barrier((value, self.last))[0]

    steps = Steps()
    steps.last = split_out
    hidden_full, hidden_other, slopes, parts_out, terms, gathered = {}, {}, {}, {}, {}, {}
    lows, core_got = {}, {}
    up_full, up_other, up_parts, up_terms, lasts = {}, {}, {}, {}, {}

    def down_send(k):
        sent, lows[k] = product_out(
            steps.after(down), mat_out, lambda s: (1 - s[1]) * half, [grad], turned,
            sizes[k], [(half, 0, LOW)], first=starts[k],
        )
        steps.last = sent
        core_got[k] = within(0, 1, sent)

    def down_hidden(k):
        full, *pieces = product_out(
            steps.after(down), mat_out, lambda s: s[1] * half, [lows[k]], None, sizes[k],
            in_pieces(*((1,) if k else (2, 1))), core_got[k],
        )
        steps.last = full
        hidden_full[k] = full
        if k > 0:
            hidden_other[k] = exchange(0, pieces, hidden_other[0][0])
        else:
            hidden_other[0] = [within(0, 2, pieces[0]), detour(pieces[1])]

    def down_return():
        hidden_other[0][1] = returned(steps.after(hidden_other[0][1]))

    def slope(k):
        slopes[k] = slope_of(steps.after(down), pre, starts[k], sizes[k], half)
        steps.last = slopes[k]

    def down_back(k):
        tokens = sizes[k]
        right = hidden(steps.after(down), hidden_full[k], slopes[k], hidden_other[k])
        swapped = within(0, 1, right)
        (partial,) = product_in(
            down, lambda i, s: (i * part_rows, s[1] * half), [right], None, tokens, F32
        )
        parts_out[k] = product_parts(
            down, lambda i, s: (i * part_rows, (1 - s[1]) * half), swapped, tokens, partial
        )
        steps.last = parts_out[k][0]

    def cross(k):
        *others, own = parts_out[k]
        terms[k] = scatter_hid(0, others + [steps.after(own)])
        crossed = lax.ppermute(terms[k], "section", [(0, 1)])
        steps.last = crossed
        gathered[k] = [crossed] + [within(1, d, crossed, "hid") for d in range(1, PARTS)]

    def up_hidden(k):
        tokens = sizes[k]
        low, up_terms[k] = join(steps.after(up), grads[k], gathered[k])
        low_other = within(1, 1, low)
        (partial,) = product_out(
            up, split_out, lambda s: s[1] * half, [low], None, tokens, [(half, 0, F32)]
        )
        full, *pieces = product_out(
            up, split_out, lambda s: (1 - s[1]) * half, [low_other], None, tokens,
            in_pieces(1), partial,
        )
        steps.last = full
        up_full[k] = full
        up_other[k] = exchange(1, pieces, up_other[k - 1][-1] if k else None)

    def place(part, core):
        row = core * (PARTS // 2) + lax.rem(part, PARTS // 2)
        return row * part_rows, lax.div(part, PARTS // 2) * half

    def up_back(k):
        tokens = sizes[k]
        sent, right = product_in(
            steps.after(up), lambda i, s: place(i, 1 - s[1]),
            [up_full[k], slopes[k]] + up_other[k], hidden_of, tokens, F32,
        )
        got = within(1, 1, sent)
        up_parts[k] = product_parts(up, lambda i, s: place(i, s[1]), right, tokens, got)
        steps.last = up_parts[k][0]

    def gather(k):
        *others, own = up_parts[k]
        last = jnp.where(is_up, scatter_hid(1, others + [steps.after(own)]), terms[k])
        steps.last = last
        lasts[k] = [last] + [everywhere(d, last) for d in range(1, PARTS)]

    for k in chunks:
        down_send(k)
    for k in chunks:
        down_hidden(k)
    slope(0)
    down_return()
    down_back(0)
    out = None
    for k in chunks:
        if k + 1 < len(SHARES):
            slope(k + 1)
        cross(k)
        if k + 1 < len(SHARES):
            down_back(k + 1)
        up_hidden(k)
    for k in chunks:
        up_back(k)
        if k > 0:
            out = finish(steps.after(up), out, grad, starts[k - 1], up_terms[k - 1], lasts[k - 1])
            steps.last = out
        gather(k)
    out = finish(up, out, grad, starts[k], up_terms[k], lasts[k])
    return out.reshape(1, batches, batch_tokens, quarter)


def solution(mesh):
    return jax.shard_map(
        local,
        mesh=mesh,
        in_specs=(
            P(None, None, "wid"),
            P("section", "wid", "hid"),
            P("section", "hid", "wid"),
            P("section", None, None, "hid"),
        ),
        out_specs=P("section", None, None, "wid"),
        check_vma=False,
    )
```

```python
import jax
import jax.numpy as jnp
from jax import lax
from jax.experimental import pallas as pl
from jax.experimental.pallas import tpu as pltpu
from jax.sharding import PartitionSpec as P

SHARES = (1, 1)
PARTS = 4
LANES = 128
WEIGHT = 4096
LIMIT = 46 * 1024 * 1024
LOW = jnp.bfloat16
F32 = jnp.float32


def gelu_slope(pre):
    normal_cdf = 0.5 * (1.0 + lax.erf(pre * 0.7071067811865476))
    density = jnp.exp(-0.5 * pre * pre) * 0.3989422804014327
    return normal_cdf + pre * density


def params():
    return pltpu.CompilerParams(vmem_limit_bytes=LIMIT)


def divisor(size, most):
    return max(r for r in range(16, most + 1, 16) if size % r == 0)


SMEM = pl.BlockSpec(memory_space=pltpu.SMEM)
VMEM = pl.BlockSpec(memory_space=pltpu.VMEM)
ANY = pl.BlockSpec(memory_space=pl.ANY)


def product(flags, mat, block, place, steps, sources, prepare, tokens, outs, base=None, base_row=None, apart=False, first=None):
    rows, depth = block
    slots = min(4, steps)
    bare = prepare is None
    count = len(sources)

    def body(s, mat_ref, *refs):
        source_refs, refs = refs[:count], refs[count:]
        base_ref = None
        if base is not None:
            base_ref, refs = refs[0], refs[1:]
        if first is not None:
            chunk_ref, chunk_sem = refs[-2:]
            refs = refs[:-2]
        out_refs, (buf, sem) = refs[:-2], refs[-2:]

        def fetch(i):
            row, col = place(i, s)
            piece = mat_ref.at[pl.ds(pl.multiple_of(row, 16), rows), pl.ds(pl.multiple_of(col, LANES), depth)]
            slot = lax.rem(i, slots)
            return pltpu.make_async_copy(piece, buf.at[slot], sem.at[slot])

        @pl.when(s[0] == 1)
        def _():
            given = source_refs
            if first is not None:
                piece = source_refs[0].at[pl.ds(first, tokens)]
                chunk = pltpu.make_async_copy(piece, chunk_ref, chunk_sem)
                chunk.start()
                given = [chunk_ref]
            for i in range(slots):
                fetch(i).start()
            if first is not None:
                chunk.wait()
            right_ref = source_refs[0]
            if not bare:
                right_ref = out_refs[-1]
                prepare(right_ref, *given)

            @pl.loop(0, steps)
            def _(i):
                fetch(i).wait()
                got = jnp.dot(buf[lax.rem(i, slots)], right_ref[...], preferred_element_type=F32)

                @pl.when(i + slots < steps)
                def _():
                    fetch(i + slots).start()

                if base_ref is not None:
                    start = pl.multiple_of(base_row(i, s), 16)
                    got = got + base_ref[pl.ds(start, rows)].astype(F32)
                if apart:
                    for which, ref in enumerate(out_refs[:steps]):

                        @pl.when(i == which)
                        def _(ref=ref):
                            ref[...] = got.astype(ref.dtype)
                else:
                    for ref, (size, begin, _) in zip(out_refs, outs):

                        @pl.when((i * rows >= begin) & (i * rows < begin + size))
                        def _(ref=ref, begin=begin):
                            at = pl.multiple_of(i * rows - begin, 16)
                            ref[pl.ds(at, rows)] = got.astype(ref.dtype)

    shapes = [jax.ShapeDtypeStruct((size, tokens), kind) for size, _, kind in outs]
    if not bare:
        shapes.append(jax.ShapeDtypeStruct((depth, tokens), LOW))
    return pl.pallas_call(
        body,
        in_specs=[SMEM, ANY]
        + [VMEM if first is None else ANY] * count
        + [VMEM] * (base is not None),
        out_specs=[VMEM] * len(shapes),
        out_shape=shapes,
        scratch_shapes=[
            pltpu.VMEM((slots, rows, depth), LOW),
            pltpu.SemaphoreType.DMA((slots,)),
        ]
        + ([] if first is None else [pltpu.VMEM((tokens, depth), F32), pltpu.SemaphoreType.DMA(())]),
        compiler_params=params(),
        cost_estimate=pl.CostEstimate(
            flops=2 * tokens * rows * depth * steps // WEIGHT,
            bytes_accessed=2 * rows * depth * steps // WEIGHT,
            transcendentals=0,
        ),
    )(flags, mat, *sources, *([] if base is None else [base]))


def turned(right_ref, grad_ref):
    right_ref[...] = grad_ref[...].T.astype(LOW)


def hidden_of(right_ref, own_ref, slope_ref, *other_refs):
    row = 0
    for other_ref in other_refs:
        at = slice(row, row + other_ref.shape[0])
        total = own_ref[at] + other_ref[...].astype(F32)
        right_ref[at] = (total * slope_ref[at]).astype(LOW)
        row = at.stop


def hidden(flags, own, slope, others):
    def body(s, own_ref, slope_ref, *refs):
        @pl.when(s[0] == 1)
        def _():
            hidden_of(refs[-1], own_ref, slope_ref, *refs[:-1])

    return pl.pallas_call(
        body,
        in_specs=[SMEM] + [VMEM] * (2 + len(others)),
        out_specs=VMEM,
        out_shape=jax.ShapeDtypeStruct(own.shape, LOW),
        compiler_params=params(),
        cost_estimate=pl.CostEstimate(
            flops=own.size // WEIGHT, bytes_accessed=own.size // WEIGHT, transcendentals=0
        ),
    )(flags, own, slope, *others)


def split_rows(flags, mat):
    rows, cols = mat.shape
    step = 256
    half = step // 2
    count = rows // step
    slots = 4

    def body(s, mat_ref, out_ref, buf, done, sem_in, sem_out):
        def fetch(i, slot):
            piece = mat_ref.at[pl.ds(pl.multiple_of(i * step, step), step)]
            return pltpu.make_async_copy(piece, buf.at[slot], sem_in.at[slot])

        def put(i, slot):
            piece = out_ref.at[:, pl.ds(pl.multiple_of(i * half, half), half)]
            return pltpu.make_async_copy(done.at[slot], piece, sem_out.at[slot])

        @pl.when(s[0] == 1)
        def _():
            to = lax.broadcasted_iota(jnp.int32, (step, step), 0)
            source = lax.broadcasted_iota(jnp.int32, (step, step), 1)
            wanted = jnp.where(to < half, 2 * to, 2 * (to - half) + 1)
            pick = jnp.where(source == wanted, 1.0, 0.0).astype(LOW)
            for i in range(slots):
                fetch(i, i).start()

            @pl.loop(0, count // slots)
            def _(turn):
                for slot in range(slots):
                    i = turn * slots + slot
                    fetch(i, slot).wait()

                    @pl.when(turn > 0)
                    def _():
                        put(i - slots, slot).wait()

                    got = jnp.dot(pick, buf[slot], preferred_element_type=F32).astype(LOW)
                    done[slot, 0] = got[:half]
                    done[slot, 1] = got[half:]

                    @pl.when(turn < count // slots - 1)
                    def _():
                        fetch(i + slots, slot).start()

                    put(i, slot).start()

            for slot in range(slots):
                put(count - slots + slot, slot).wait()

    out = pl.pallas_call(
        body,
        in_specs=[SMEM, ANY],
        out_specs=ANY,
        out_shape=jax.ShapeDtypeStruct((2, rows // 2, cols), LOW),
        scratch_shapes=[
            pltpu.VMEM((slots, step, cols), LOW),
            pltpu.VMEM((slots, 2, half, cols), LOW),
            pltpu.SemaphoreType.DMA((slots,)),
            pltpu.SemaphoreType.DMA((slots,)),
        ],
        compiler_params=params(),
        cost_estimate=pl.CostEstimate(
            flops=2 * rows * step * cols // WEIGHT, bytes_accessed=4 * rows * cols // WEIGHT, transcendentals=0
        ),
    )(flags, mat)
    return out.reshape(rows, cols)


def slope_of(flags, pre, start, tokens, half):
    cols = divisor(half, 768)
    per_half = half // cols

    def body(s, pre_ref, out_ref):
        out_ref[...] = gelu_slope(pre_ref[...]).T

    return pl.pallas_call(
        body,
        grid_spec=pltpu.PrefetchScalarGridSpec(
            num_scalar_prefetch=1,
            grid=(tokens // LANES, per_half),
            in_specs=[
                pl.BlockSpec((LANES, cols), lambda i, j, s: (start // LANES + i, s[1] * per_half + j))
            ],
            out_specs=pl.BlockSpec((cols, LANES), lambda i, j, s: (j, i)),
        ),
        out_shape=jax.ShapeDtypeStruct((half, tokens), F32),
        compiler_params=params(),
        cost_estimate=pl.CostEstimate(
            flops=half * tokens // WEIGHT, bytes_accessed=8 * half * tokens // WEIGHT, transcendentals=0
        ),
    )(flags, pre)


def join(flags, grad, parts):
    tokens, columns = grad.shape
    width = columns // PARTS

    def body(s, grad_ref, *refs):
        part_refs, (low_ref, term_ref) = refs[:PARTS], refs[PARTS:]

        @pl.when(s[0] == 1)
        def _():
            for slot, ref in enumerate(part_refs):
                start = pl.multiple_of(lax.bitwise_xor(s[2], slot) * width, LANES)
                term = ref[...]
                term_ref[pl.ds(start, width)] = term
                total = grad_ref[:, pl.ds(start, width)].T + term.astype(F32)
                low_ref[pl.ds(start, width)] = total.astype(LOW)

    shape = jax.ShapeDtypeStruct((columns, tokens), LOW)
    return pl.pallas_call(
        body,
        in_specs=[SMEM] + [VMEM] * (1 + PARTS),
        out_specs=[VMEM, VMEM],
        out_shape=[shape, shape],
        compiler_params=params(),
        cost_estimate=pl.CostEstimate(
            flops=4 * columns * tokens, bytes_accessed=4 * columns * tokens, transcendentals=0
        ),
    )(flags, grad, *parts)


def finish(flags, out, grad, start, term, parts):
    columns, tokens = term.shape
    width = columns // PARTS
    total_tokens = grad.shape[0]

    def body(s, *refs):
        grad_ref, term_ref, *part_refs = refs[int(out is not None) : -2]
        out_ref, joined = refs[-2:]
        for slot, ref in enumerate(part_refs):
            start = pl.multiple_of(lax.bitwise_xor(s[2], slot) * width, LANES)
            joined[pl.ds(start, width)] = ref[...]

        @pl.when(s[0] == 0)
        def _():
            out_ref[...] = grad_ref[...] + joined[...].astype(F32).T

        @pl.when(s[0] == 1)
        def _():
            source = lax.broadcasted_iota(jnp.int32, (2 * LANES, 2 * LANES), 1)
            to = lax.broadcasted_iota(jnp.int32, (2 * LANES, 2 * LANES), 0)
            wanted = jnp.where(source < LANES, 2 * source, 2 * (source - LANES) + 1)
            pick = jnp.where(to == wanted, 1.0, 0.0).astype(LOW)
            for group in range(columns // (2 * LANES)):
                even_at = group * LANES
                odd_at = columns // 2 + group * LANES
                even = joined[even_at : even_at + LANES]
                odd = joined[odd_at : odd_at + LANES]
                pair = jnp.concatenate([even, odd], axis=0)
                woven = jnp.dot(pick, pair, preferred_element_type=F32)
                at = slice(group * 2 * LANES, (group + 1) * 2 * LANES)
                first = term_ref[at].astype(F32).T
                out_ref[:, at] = grad_ref[:, at] + first + woven.T

    earlier = [] if out is None else [out]
    piece = pl.BlockSpec((width, LANES), lambda i, s: (0, i))
    rows = pl.BlockSpec((LANES, columns), lambda i, s: (start // LANES + i, 0))
    return pl.pallas_call(
        body,
        grid_spec=pltpu.PrefetchScalarGridSpec(
            num_scalar_prefetch=1,
            grid=(tokens // LANES,),
            in_specs=[ANY] * len(earlier)
            + [rows, pl.BlockSpec((columns, LANES), lambda i, s: (0, i))]
            + [piece] * PARTS,
            out_specs=rows,
            scratch_shapes=[pltpu.VMEM((columns, LANES), LOW)],
        ),
        out_shape=jax.ShapeDtypeStruct((total_tokens, columns), F32),
        input_output_aliases={1: 0} if earlier else {},
        compiler_params=params(),
    )(flags, *earlier, grad, term, *parts)


def local(grad_out, weight_in, weight_out, pre_act):
    hids = lax.axis_size("hid")
    section = lax.axis_index("section")
    side = lax.axis_index("wid") % 2
    is_up = section == 1

    def scalars(active_section):
        active = (section == active_section).astype(jnp.int32)
        return jnp.stack([active, side, lax.axis_index("hid") % PARTS]).astype(jnp.int32)

    down, up = scalars(0), scalars(1)

    def within(active, distance, block, axis="wid"):
        size = lax.axis_size(axis)
        pairs = [(active * size + i, active * size + (i ^ distance)) for i in range(size)]
        return lax.ppermute(block, ("section", axis), pairs)

    def everywhere(distance, block, axis="hid"):
        size = lax.axis_size(axis)
        return lax.ppermute(block, axis, [(i, i ^ distance) for i in range(size)])

    mat_in = weight_in[0]
    mat_out = weight_out[0]
    quarter, hid_tile = mat_in.shape
    half = hid_tile // 2
    batches, batch_tokens, _ = grad_out.shape
    total = batches * batch_tokens
    unit = total // sum(SHARES)
    starts = [unit * sum(SHARES[:k]) for k in range(len(SHARES))]
    sizes = [unit * share for share in SHARES]
    chunks = range(len(SHARES))
    last_chunk = len(SHARES) - 1
    grad = grad_out.reshape(total, quarter)
    pre = pre_act[0].reshape(total, hid_tile)
    grads = [grad[starts[k] : starts[k] + sizes[k]] for k in chunks]

    split_out = split_rows(up, mat_out)

    hid_rows = divisor(half // 2, 512)
    hid_steps = half // hid_rows
    part_rows = quarter // PARTS

    def product_out(flags, mat, first_row, sources, prepare, tokens, outs, base=None, first=None):
        return product(
            flags, mat, (hid_rows, quarter),
            lambda i, s: (first_row(s) + i * hid_rows, 0), hid_steps,
            sources, prepare, tokens, outs, base, lambda i, s: i * hid_rows, first=first,
        )

    def in_pieces(*shares):
        blocks = [max(1, hid_steps * sum(shares[: n + 1]) // sum(shares)) for n in range(len(shares))]
        ends = [0] + [hid_rows * block for block in blocks]
        return [(half, 0, F32)] + [(ends[n + 1] - ends[n], ends[n], LOW) for n in range(len(shares))]

    def exchange(active, pieces, earlier):
        if earlier is not None:
            pieces = [lax.optimization_barrier((piece, earlier))[0] for piece in pieces]
        return [within(active, 2, piece) for piece in pieces]

    def detour(piece):
        size = lax.axis_size("wid")
        return lax.ppermute(piece, ("section", "wid"), [(i, size + (i ^ 2)) for i in range(size)])

    def returned(piece):
        size = lax.axis_size("wid")
        return lax.ppermute(piece, ("section", "wid"), [(size + i, i) for i in range(size)])

    def across(term, distance):
        size = lax.axis_size("hid")
        pairs = [(i, size + (i ^ distance)) for i in range(size)]
        return lax.ppermute(term, ("section", "hid"), pairs)

    def product_in(flags, place, sources, prepare, tokens, kind):
        return product(
            flags, mat_in, (part_rows, half), place, PARTS, sources, prepare, tokens,
            [(quarter, 0, kind)],
        )

    def product_parts(flags, place, right, tokens, base):
        def part_of(i, s):
            return lax.bitwise_xor(s[2], lax.rem(i + 1, PARTS))

        return product(
            flags, mat_in, (part_rows, half), lambda i, s: place(part_of(i, s), s), PARTS,
            [right], None, tokens, [(part_rows, 0, LOW)] * 3 + [(part_rows, 0, F32)],
            base, lambda i, s: part_of(i, s) * part_rows, True,
        )

    def scatter_hid(active, parts):
        *others, own = parts
        got = [within(active, d + 1, part, "hid") for d, part in enumerate(others)]
        for part in got:
            own = own + part.astype(F32)
        distance = PARTS
        while distance < hids:
            own = own + within(active, distance, own, "hid")
            distance *= 2
        return own.astype(LOW)

    class Steps:
        def __init__(self):
            self.last = None

        def after(self, value):
            if self.last is None:
                return value
            return lax.optimization_barrier((value, self.last))[0]

    steps = Steps()
    steps.last = split_out
    hidden_full, hidden_other, slopes, parts_out, terms, gathered = {}, {}, {}, {}, {}, {}
    lows, core_got = {}, {}
    up_full, up_other, up_parts, up_terms, lasts = {}, {}, {}, {}, {}

    def down_send(k):
        sent, lows[k] = product_out(
            steps.after(down), mat_out, lambda s: (1 - s[1]) * half, [grad], turned,
            sizes[k], [(half, 0, LOW)], first=starts[k],
        )
        steps.last = sent
        core_got[k] = within(0, 1, sent)

    def down_hidden(k):
        full, *pieces = product_out(
            steps.after(down), mat_out, lambda s: s[1] * half, [lows[k]], None, sizes[k],
            in_pieces(*((1,) if k else (2, 1))), core_got[k],
        )
        steps.last = full
        hidden_full[k] = full
        if k > 0:
            hidden_other[k] = exchange(0, pieces, hidden_other[0][0])
        else:
            hidden_other[0] = [within(0, 2, pieces[0]), detour(pieces[1])]

    def down_return():
        hidden_other[0][1] = returned(steps.after(hidden_other[0][1]))

    def slope(k):
        slopes[k] = slope_of(steps.after(down), pre, starts[k], sizes[k], half)
        steps.last = slopes[k]

    def down_back(k):
        tokens = sizes[k]
        right = hidden(steps.after(down), hidden_full[k], slopes[k], hidden_other[k])
        swapped = within(0, 1, right)
        (partial,) = product_in(
            down, lambda i, s: (i * part_rows, s[1] * half), [right], None, tokens, F32
        )
        parts_out[k] = product_parts(
            down, lambda i, s: (i * part_rows, (1 - s[1]) * half), swapped, tokens, partial
        )
        steps.last = parts_out[k][0]

    def cross(k):
        *others, own = parts_out[k]
        terms[k] = scatter_hid(0, others + [steps.after(own)])
        if k == 0:
            crossed = across(terms[k], 0)
            steps.last = crossed
            gathered[k] = [crossed] + [within(1, d, crossed, "hid") for d in range(1, PARTS)]
        else:
            gathered[k] = [across(terms[k], d) for d in range(PARTS)]
            steps.last = gathered[k][0]

    def up_hidden(k):
        tokens = sizes[k]
        low, up_terms[k] = join(steps.after(up), grads[k], gathered[k])
        low_other = within(1, 1, low)
        (partial,) = product_out(
            up, split_out, lambda s: s[1] * half, [low], None, tokens, [(half, 0, F32)]
        )
        full, *pieces = product_out(
            up, split_out, lambda s: (1 - s[1]) * half, [low_other], None, tokens,
            in_pieces(1), partial,
        )
        steps.last = full
        up_full[k] = full
        up_other[k] = exchange(1, pieces, up_other[k - 1][0] if k else None)

    def place(part, core):
        row = core * (PARTS // 2) + lax.rem(part, PARTS // 2)
        return row * part_rows, lax.div(part, PARTS // 2) * half

    def up_back(k):
        tokens = sizes[k]
        sent, right = product_in(
            steps.after(up), lambda i, s: place(i, 1 - s[1]),
            [up_full[k], slopes[k]] + up_other[k], hidden_of, tokens, F32,
        )
        got = within(1, 1, sent)
        up_parts[k] = product_parts(up, lambda i, s: place(i, s[1]), right, tokens, got)
        steps.last = up_parts[k][0]

    def gather(k):
        *others, own = up_parts[k]
        last = jnp.where(is_up, scatter_hid(1, others + [steps.after(own)]), terms[k])
        steps.last = last
        lasts[k] = [last] + [everywhere(d, last) for d in range(1, PARTS)]

    for k in chunks:
        down_send(k)
    for k in chunks:
        down_hidden(k)
    down_return()
    slope(0)
    down_back(0)
    slope(1)
    cross(0)
    down_back(1)
    up_hidden(0)
    cross(1)
    up_hidden(1)
    up_back(0)
    gather(0)
    up_back(1)
    out = finish(steps.after(up), None, grad, starts[0], up_terms[0], lasts[0])
    steps.last = out
    gather(1)
    k = last_chunk
    out = finish(up, out, grad, starts[k], up_terms[k], lasts[k])
    return out.reshape(1, batches, batch_tokens, quarter)


def solution(mesh):
    return jax.shard_map(
        local,
        mesh=mesh,
        in_specs=(
            P(None, None, "wid"),
            P("section", "wid", "hid"),
            P("section", "hid", "wid"),
            P("section", None, None, "hid"),
        ),
        out_specs=P("section", None, None, "wid"),
        check_vma=False,
    )
```

```python
import jax
import jax.numpy as jnp
from jax import lax
from jax.experimental import pallas as pl
from jax.experimental.pallas import tpu as pltpu
from jax.sharding import PartitionSpec as P

SHARES = (1, 1)
PARTS = 4
LANES = 128
WEIGHT = 4096
LIMIT = 46 * 1024 * 1024
LOW = jnp.bfloat16
F32 = jnp.float32


def gelu_slope(pre):
    normal_cdf = 0.5 * (1.0 + lax.erf(pre * 0.7071067811865476))
    density = jnp.exp(-0.5 * pre * pre) * 0.3989422804014327
    return normal_cdf + pre * density


def params():
    return pltpu.CompilerParams(vmem_limit_bytes=LIMIT)


def divisor(size, most):
    return max(r for r in range(16, most + 1, 16) if size % r == 0)


SMEM = pl.BlockSpec(memory_space=pltpu.SMEM)
VMEM = pl.BlockSpec(memory_space=pltpu.VMEM)
ANY = pl.BlockSpec(memory_space=pl.ANY)


def product(flags, mat, block, place, steps, sources, prepare, tokens, outs, base=None, base_row=None, apart=False, first=None):
    rows, depth = block
    slots = min(4, steps)
    bare = prepare is None
    count = len(sources)

    def body(s, mat_ref, *refs):
        source_refs, refs = refs[:count], refs[count:]
        base_ref = None
        if base is not None:
            base_ref, refs = refs[0], refs[1:]
        if first is not None:
            chunk_ref, chunk_sem = refs[-2:]
            refs = refs[:-2]
        out_refs, (buf, sem) = refs[:-2], refs[-2:]

        def fetch(i):
            row, col = place(i, s)
            piece = mat_ref.at[pl.ds(pl.multiple_of(row, 16), rows), pl.ds(pl.multiple_of(col, LANES), depth)]
            slot = lax.rem(i, slots)
            return pltpu.make_async_copy(piece, buf.at[slot], sem.at[slot])

        @pl.when(s[0] == 1)
        def _():
            given = source_refs
            if first is not None:
                piece = source_refs[0].at[pl.ds(first, tokens)]
                chunk = pltpu.make_async_copy(piece, chunk_ref, chunk_sem)
                chunk.start()
                given = [chunk_ref]
            for i in range(slots):
                fetch(i).start()
            if first is not None:
                chunk.wait()
            right_ref = source_refs[0]
            if not bare:
                right_ref = out_refs[-1]
                prepare(right_ref, *given)

            @pl.loop(0, steps)
            def _(i):
                fetch(i).wait()
                got = jnp.dot(buf[lax.rem(i, slots)], right_ref[...], preferred_element_type=F32)

                @pl.when(i + slots < steps)
                def _():
                    fetch(i + slots).start()

                if base_ref is not None:
                    start = pl.multiple_of(base_row(i, s), 16)
                    got = got + base_ref[pl.ds(start, rows)].astype(F32)
                if apart:
                    for which, ref in enumerate(out_refs[:steps]):

                        @pl.when(i == which)
                        def _(ref=ref):
                            ref[...] = got.astype(ref.dtype)
                else:
                    for ref, (size, begin, _) in zip(out_refs, outs):

                        @pl.when((i * rows >= begin) & (i * rows < begin + size))
                        def _(ref=ref, begin=begin):
                            at = pl.multiple_of(i * rows - begin, 16)
                            ref[pl.ds(at, rows)] = got.astype(ref.dtype)

    shapes = [jax.ShapeDtypeStruct((size, tokens), kind) for size, _, kind in outs]
    if not bare:
        shapes.append(jax.ShapeDtypeStruct((depth, tokens), LOW))
    return pl.pallas_call(
        body,
        in_specs=[SMEM, ANY]
        + [VMEM if first is None else ANY] * count
        + [VMEM] * (base is not None),
        out_specs=[VMEM] * len(shapes),
        out_shape=shapes,
        scratch_shapes=[
            pltpu.VMEM((slots, rows, depth), LOW),
            pltpu.SemaphoreType.DMA((slots,)),
        ]
        + ([] if first is None else [pltpu.VMEM((tokens, depth), F32), pltpu.SemaphoreType.DMA(())]),
        compiler_params=params(),
        cost_estimate=pl.CostEstimate(
            flops=2 * tokens * rows * depth * steps // WEIGHT,
            bytes_accessed=2 * rows * depth * steps // WEIGHT,
            transcendentals=0,
        ),
    )(flags, mat, *sources, *([] if base is None else [base]))


def pair_product(flags, mat, rows, own, other):
    _, height, depth = mat.shape
    tokens = own.shape[1]
    steps = height // rows
    slots = min(3, steps)

    def body(s, mat_ref, own_ref, other_ref, full_ref, low_ref, buf, sem):
        def fetch(i):
            piece = mat_ref.at[:, pl.ds(pl.multiple_of(i * rows, 16), rows)]
            slot = lax.rem(i, slots)
            return pltpu.make_async_copy(piece, buf.at[slot], sem.at[slot])

        @pl.when(s[0] == 1)
        def _():
            for i in range(slots):
                fetch(i).start()

            @pl.loop(0, steps)
            def _(i):
                fetch(i).wait()
                slot = lax.rem(i, slots)
                got = jnp.dot(buf[slot, s[1]], own_ref[...], preferred_element_type=F32)
                got = got + jnp.dot(
                    buf[slot, 1 - s[1]], other_ref[...], preferred_element_type=F32
                )

                @pl.when(i + slots < steps)
                def _():
                    fetch(i + slots).start()

                at = pl.ds(pl.multiple_of(i * rows, 16), rows)
                full_ref[at] = got
                low_ref[at] = got.astype(LOW)

    return pl.pallas_call(
        body,
        in_specs=[SMEM, ANY, VMEM, VMEM],
        out_specs=[VMEM, VMEM],
        out_shape=[
            jax.ShapeDtypeStruct((height, tokens), F32),
            jax.ShapeDtypeStruct((height, tokens), LOW),
        ],
        scratch_shapes=[
            pltpu.VMEM((slots, 2, rows, depth), LOW),
            pltpu.SemaphoreType.DMA((slots,)),
        ],
        compiler_params=params(),
        cost_estimate=pl.CostEstimate(
            flops=4 * tokens * height * depth // WEIGHT,
            bytes_accessed=4 * height * depth // WEIGHT,
            transcendentals=0,
        ),
    )(flags, mat, own, other)


def turned(right_ref, grad_ref):
    right_ref[...] = grad_ref[...].T.astype(LOW)


def hidden_of(right_ref, own_ref, slope_ref, *other_refs):
    row = 0
    for other_ref in other_refs:
        at = slice(row, row + other_ref.shape[0])
        total = own_ref[at] + other_ref[...].astype(F32)
        right_ref[at] = (total * slope_ref[at]).astype(LOW)
        row = at.stop


def hidden(flags, own, slope, others):
    def body(s, own_ref, slope_ref, *refs):
        @pl.when(s[0] == 1)
        def _():
            hidden_of(refs[-1], own_ref, slope_ref, *refs[:-1])

    return pl.pallas_call(
        body,
        in_specs=[SMEM] + [VMEM] * (2 + len(others)),
        out_specs=VMEM,
        out_shape=jax.ShapeDtypeStruct(own.shape, LOW),
        compiler_params=params(),
        cost_estimate=pl.CostEstimate(
            flops=own.size // WEIGHT, bytes_accessed=own.size // WEIGHT, transcendentals=0
        ),
    )(flags, own, slope, *others)


def split_rows(flags, mat):
    rows, cols = mat.shape
    step = 256
    half = step // 2
    count = rows // step
    slots = 4

    def body(s, mat_ref, out_ref, buf, done, sem_in, sem_out):
        def fetch(i, slot):
            piece = mat_ref.at[pl.ds(pl.multiple_of(i * step, step), step)]
            return pltpu.make_async_copy(piece, buf.at[slot], sem_in.at[slot])

        def put(i, slot):
            piece = out_ref.at[:, pl.ds(pl.multiple_of(i * half, half), half)]
            return pltpu.make_async_copy(done.at[slot], piece, sem_out.at[slot])

        @pl.when(s[0] == 1)
        def _():
            to = lax.broadcasted_iota(jnp.int32, (step, step), 0)
            source = lax.broadcasted_iota(jnp.int32, (step, step), 1)
            wanted = jnp.where(to < half, 2 * to, 2 * (to - half) + 1)
            pick = jnp.where(source == wanted, 1.0, 0.0).astype(LOW)
            for i in range(slots):
                fetch(i, i).start()

            @pl.loop(0, count // slots)
            def _(turn):
                for slot in range(slots):
                    i = turn * slots + slot
                    fetch(i, slot).wait()

                    @pl.when(turn > 0)
                    def _():
                        put(i - slots, slot).wait()

                    got = jnp.dot(pick, buf[slot], preferred_element_type=F32).astype(LOW)
                    done[slot, 0] = got[:half]
                    done[slot, 1] = got[half:]

                    @pl.when(turn < count // slots - 1)
                    def _():
                        fetch(i + slots, slot).start()

                    put(i, slot).start()

            for slot in range(slots):
                put(count - slots + slot, slot).wait()

    out = pl.pallas_call(
        body,
        in_specs=[SMEM, ANY],
        out_specs=ANY,
        out_shape=jax.ShapeDtypeStruct((2, rows // 2, cols), LOW),
        scratch_shapes=[
            pltpu.VMEM((slots, step, cols), LOW),
            pltpu.VMEM((slots, 2, half, cols), LOW),
            pltpu.SemaphoreType.DMA((slots,)),
            pltpu.SemaphoreType.DMA((slots,)),
        ],
        compiler_params=params(),
        cost_estimate=pl.CostEstimate(
            flops=2 * rows * step * cols // WEIGHT, bytes_accessed=4 * rows * cols // WEIGHT, transcendentals=0
        ),
    )(flags, mat)
    return out


def slope_of(flags, pre, start, tokens, half):
    cols = divisor(half, 768)
    per_half = half // cols

    def body(s, pre_ref, out_ref):
        out_ref[...] = gelu_slope(pre_ref[...]).T

    return pl.pallas_call(
        body,
        grid_spec=pltpu.PrefetchScalarGridSpec(
            num_scalar_prefetch=1,
            grid=(tokens // LANES, per_half),
            in_specs=[
                pl.BlockSpec((LANES, cols), lambda i, j, s: (start // LANES + i, s[1] * per_half + j))
            ],
            out_specs=pl.BlockSpec((cols, LANES), lambda i, j, s: (j, i)),
        ),
        out_shape=jax.ShapeDtypeStruct((half, tokens), F32),
        compiler_params=params(),
        cost_estimate=pl.CostEstimate(
            flops=half * tokens // WEIGHT, bytes_accessed=8 * half * tokens // WEIGHT, transcendentals=0
        ),
    )(flags, pre)


def join(flags, grad, parts):
    tokens, columns = grad.shape
    width = columns // PARTS

    def body(s, grad_ref, *refs):
        part_refs, (low_ref, term_ref) = refs[:PARTS], refs[PARTS:]

        @pl.when(s[0] == 1)
        def _():
            for slot, ref in enumerate(part_refs):
                start = pl.multiple_of(lax.bitwise_xor(s[2], slot) * width, LANES)
                term = ref[...]
                term_ref[pl.ds(start, width)] = term
                total = grad_ref[:, pl.ds(start, width)].T + term.astype(F32)
                low_ref[pl.ds(start, width)] = total.astype(LOW)

    shape = jax.ShapeDtypeStruct((columns, tokens), LOW)
    return pl.pallas_call(
        body,
        in_specs=[SMEM] + [VMEM] * (1 + PARTS),
        out_specs=[VMEM, VMEM],
        out_shape=[shape, shape],
        compiler_params=params(),
        cost_estimate=pl.CostEstimate(
            flops=4 * columns * tokens, bytes_accessed=4 * columns * tokens, transcendentals=0
        ),
    )(flags, grad, *parts)


def finish(flags, out, grad, start, term, parts):
    columns, tokens = term.shape
    width = columns // PARTS
    total_tokens = grad.shape[0]

    def body(s, *refs):
        grad_ref, term_ref, *part_refs = refs[int(out is not None) : -2]
        out_ref, joined = refs[-2:]
        for slot, ref in enumerate(part_refs):
            start = pl.multiple_of(lax.bitwise_xor(s[2], slot) * width, LANES)
            joined[pl.ds(start, width)] = ref[...]

        @pl.when(s[0] == 0)
        def _():
            out_ref[...] = grad_ref[...] + joined[...].astype(F32).T

        @pl.when(s[0] == 1)
        def _():
            source = lax.broadcasted_iota(jnp.int32, (2 * LANES, 2 * LANES), 1)
            to = lax.broadcasted_iota(jnp.int32, (2 * LANES, 2 * LANES), 0)
            wanted = jnp.where(source < LANES, 2 * source, 2 * (source - LANES) + 1)
            pick = jnp.where(to == wanted, 1.0, 0.0).astype(LOW)
            for group in range(columns // (2 * LANES)):
                even_at = group * LANES
                odd_at = columns // 2 + group * LANES
                even = joined[even_at : even_at + LANES]
                odd = joined[odd_at : odd_at + LANES]
                pair = jnp.concatenate([even, odd], axis=0)
                woven = jnp.dot(pick, pair, preferred_element_type=F32)
                at = slice(group * 2 * LANES, (group + 1) * 2 * LANES)
                first = term_ref[at].astype(F32).T
                out_ref[:, at] = grad_ref[:, at] + first + woven.T

    earlier = [] if out is None else [out]
    piece = pl.BlockSpec((width, LANES), lambda i, s: (0, i))
    rows = pl.BlockSpec((LANES, columns), lambda i, s: (start // LANES + i, 0))
    return pl.pallas_call(
        body,
        grid_spec=pltpu.PrefetchScalarGridSpec(
            num_scalar_prefetch=1,
            grid=(tokens // LANES,),
            in_specs=[ANY] * len(earlier)
            + [rows, pl.BlockSpec((columns, LANES), lambda i, s: (0, i))]
            + [piece] * PARTS,
            out_specs=rows,
            scratch_shapes=[pltpu.VMEM((columns, LANES), LOW)],
        ),
        out_shape=jax.ShapeDtypeStruct((total_tokens, columns), F32),
        input_output_aliases={1: 0} if earlier else {},
        compiler_params=params(),
    )(flags, *earlier, grad, term, *parts)


def local(grad_out, weight_in, weight_out, pre_act):
    hids = lax.axis_size("hid")
    section = lax.axis_index("section")
    side = lax.axis_index("wid") % 2
    is_up = section == 1

    def scalars(active_section):
        active = (section == active_section).astype(jnp.int32)
        return jnp.stack([active, side, lax.axis_index("hid") % PARTS]).astype(jnp.int32)

    down, up = scalars(0), scalars(1)

    def within(active, distance, block, axis="wid"):
        size = lax.axis_size(axis)
        pairs = [(active * size + i, active * size + (i ^ distance)) for i in range(size)]
        return lax.ppermute(block, ("section", axis), pairs)

    def everywhere(distance, block, axis="hid"):
        size = lax.axis_size(axis)
        return lax.ppermute(block, axis, [(i, i ^ distance) for i in range(size)])

    mat_in = weight_in[0]
    mat_out = weight_out[0]
    quarter, hid_tile = mat_in.shape
    half = hid_tile // 2
    batches, batch_tokens, _ = grad_out.shape
    total = batches * batch_tokens
    unit = total // sum(SHARES)
    starts = [unit * sum(SHARES[:k]) for k in range(len(SHARES))]
    sizes = [unit * share for share in SHARES]
    chunks = range(len(SHARES))
    last_chunk = len(SHARES) - 1
    grad = grad_out.reshape(total, quarter)
    pre = pre_act[0].reshape(total, hid_tile)
    grads = [grad[starts[k] : starts[k] + sizes[k]] for k in chunks]

    split_out = split_rows(up, mat_out)

    hid_rows = divisor(half // 2, 512)
    hid_steps = half // hid_rows
    part_rows = quarter // PARTS

    def product_out(flags, mat, first_row, sources, prepare, tokens, outs, base=None, first=None):
        return product(
            flags, mat, (hid_rows, quarter),
            lambda i, s: (first_row(s) + i * hid_rows, 0), hid_steps,
            sources, prepare, tokens, outs, base, lambda i, s: i * hid_rows, first=first,
        )

    def in_pieces(*shares):
        blocks = [max(1, hid_steps * sum(shares[: n + 1]) // sum(shares)) for n in range(len(shares))]
        ends = [0] + [hid_rows * block for block in blocks]
        return [(half, 0, F32)] + [(ends[n + 1] - ends[n], ends[n], LOW) for n in range(len(shares))]

    def exchange(active, pieces, earlier):
        if earlier is not None:
            pieces = [lax.optimization_barrier((piece, earlier))[0] for piece in pieces]
        return [within(active, 2, piece) for piece in pieces]

    def detour(piece):
        size = lax.axis_size("wid")
        return lax.ppermute(piece, ("section", "wid"), [(i, size + (i ^ 2)) for i in range(size)])

    def returned(piece):
        size = lax.axis_size("wid")
        return lax.ppermute(piece, ("section", "wid"), [(size + i, i) for i in range(size)])

    def across(term, distance):
        size = lax.axis_size("hid")
        pairs = [(i, size + (i ^ distance)) for i in range(size)]
        return lax.ppermute(term, ("section", "hid"), pairs)

    def product_in(flags, place, sources, prepare, tokens, kind):
        return product(
            flags, mat_in, (part_rows, half), place, PARTS, sources, prepare, tokens,
            [(quarter, 0, kind)],
        )

    def product_parts(flags, place, right, tokens, base):
        def part_of(i, s):
            return lax.bitwise_xor(s[2], lax.rem(i + 1, PARTS))

        return product(
            flags, mat_in, (part_rows, half), lambda i, s: place(part_of(i, s), s), PARTS,
            [right], None, tokens, [(part_rows, 0, LOW)] * 3 + [(part_rows, 0, F32)],
            base, lambda i, s: part_of(i, s) * part_rows, True,
        )

    def send_parts(active, parts):
        return [within(active, d + 1, part, "hid") for d, part in enumerate(parts[:-1])]

    def sum_hid(active, own, got):
        for part in got:
            own = own + part.astype(F32)
        distance = PARTS
        while distance < hids:
            own = own + within(active, distance, own, "hid")
            distance *= 2
        return own.astype(LOW)

    class Steps:
        def __init__(self):
            self.last = None

        def after(self, value):
            if self.last is None:
                return value
            return lax.optimization_barrier((value, self.last))[0]

    steps = Steps()
    steps.last = split_out
    hidden_full, hidden_other, slopes, parts_out, terms, gathered = {}, {}, {}, {}, {}, {}
    lows, core_got, parts_got = {}, {}, {}
    up_full, up_other, up_parts, up_terms, lasts = {}, {}, {}, {}, {}

    def down_send(k):
        sent, lows[k] = product_out(
            steps.after(down), mat_out, lambda s: (1 - s[1]) * half, [grad], turned,
            sizes[k], [(half, 0, LOW)], first=starts[k],
        )
        steps.last = sent
        core_got[k] = within(0, 1, sent)

    def down_hidden(k):
        full, *pieces = product_out(
            steps.after(down), mat_out, lambda s: s[1] * half, [lows[k]], None, sizes[k],
            in_pieces(*((1,) if k else (2, 1))), core_got[k],
        )
        steps.last = full
        hidden_full[k] = full
        if k > 0:
            hidden_other[k] = exchange(0, pieces, hidden_other[0][0])
        else:
            hidden_other[0] = [within(0, 2, pieces[0]), detour(pieces[1])]

    def down_return():
        hidden_other[0][1] = returned(steps.after(hidden_other[0][1]))

    def slope(k):
        slopes[k] = slope_of(steps.after(down), pre, starts[k], sizes[k], half)
        steps.last = slopes[k]

    def down_back(k):
        tokens = sizes[k]
        right = hidden(steps.after(down), hidden_full[k], slopes[k], hidden_other[k])
        swapped = within(0, 1, right)
        (partial,) = product_in(
            down, lambda i, s: (i * part_rows, s[1] * half), [right], None, tokens, F32
        )
        parts_out[k] = product_parts(
            down, lambda i, s: (i * part_rows, (1 - s[1]) * half), swapped, tokens, partial
        )
        parts_got[k] = send_parts(0, parts_out[k])
        steps.last = parts_out[k][0]

    def cross(k):
        terms[k] = sum_hid(0, steps.after(parts_out[k][-1]), parts_got[k])
        if k == 0:
            crossed = across(terms[k], 0)
            steps.last = crossed
            gathered[k] = [crossed] + [within(1, d, crossed, "hid") for d in range(1, PARTS)]
        else:
            gathered[k] = [across(terms[k], d) for d in range(PARTS)]
            steps.last = gathered[k][0]

    def up_hidden(k):
        tokens = sizes[k]
        low, up_terms[k] = join(steps.after(up), grads[k], gathered[k])
        low_other = within(1, 1, low)
        flags = up
        if k + 1 in parts_got:
            flags = lax.optimization_barrier((up, *parts_got[k + 1]))[0]
        full, low_grad = pair_product(flags, split_out, hid_rows, low, low_other)
        steps.last = full
        up_full[k] = full
        up_other[k] = exchange(1, [low_grad], up_other[k - 1][0] if k else None)

    def place(part, core):
        row = core * (PARTS // 2) + lax.rem(part, PARTS // 2)
        return row * part_rows, lax.div(part, PARTS // 2) * half

    def up_back(k):
        tokens = sizes[k]
        sent, right = product_in(
            steps.after(up), lambda i, s: place(i, 1 - s[1]),
            [up_full[k], slopes[k]] + up_other[k], hidden_of, tokens, F32,
        )
        got = within(1, 1, sent)
        up_parts[k] = product_parts(up, lambda i, s: place(i, s[1]), right, tokens, got)
        steps.last = up_parts[k][0]

    def gather(k):
        own = steps.after(up_parts[k][-1])
        last = jnp.where(is_up, sum_hid(1, own, send_parts(1, up_parts[k])), terms[k])
        steps.last = last
        lasts[k] = [last] + [everywhere(d, last) for d in range(1, PARTS)]
        steps.last = lasts[k][1]

    for k in chunks:
        down_send(k)
    for k in chunks:
        down_hidden(k)
    down_return()
    slope(0)
    down_back(0)
    slope(1)
    cross(0)
    down_back(1)
    up_hidden(0)
    cross(1)
    up_hidden(1)
    up_back(0)
    gather(0)
    up_back(1)
    out = finish(steps.after(up), None, grad, starts[0], up_terms[0], lasts[0])
    steps.last = out
    gather(1)
    k = last_chunk
    out = finish(up, out, grad, starts[k], up_terms[k], lasts[k])
    return out.reshape(1, batches, batch_tokens, quarter)


def solution(mesh):
    return jax.shard_map(
        local,
        mesh=mesh,
        in_specs=(
            P(None, None, "wid"),
            P("section", "wid", "hid"),
            P("section", "hid", "wid"),
            P("section", None, None, "hid"),
        ),
        out_specs=P("section", None, None, "wid"),
        check_vma=False,
    )
```

```python
import jax
import jax.numpy as jnp
from jax import lax
from jax.experimental import pallas as pl
from jax.experimental.pallas import tpu as pltpu
from jax.sharding import PartitionSpec as P

SHARES = (1, 1)
PARTS = 4
LANES = 128
WEIGHT = 4096
LIMIT = 46 * 1024 * 1024
LOW = jnp.bfloat16
F32 = jnp.float32


def gelu_slope(pre):
    normal_cdf = 0.5 * (1.0 + lax.erf(pre * 0.7071067811865476))
    density = jnp.exp(-0.5 * pre * pre) * 0.3989422804014327
    return normal_cdf + pre * density


def params():
    return pltpu.CompilerParams(vmem_limit_bytes=LIMIT)


def divisor(size, most):
    return max(r for r in range(16, most + 1, 16) if size % r == 0)


SMEM = pl.BlockSpec(memory_space=pltpu.SMEM)
VMEM = pl.BlockSpec(memory_space=pltpu.VMEM)
ANY = pl.BlockSpec(memory_space=pl.ANY)


def product(flags, mat, block, place, steps, sources, prepare, tokens, outs, base=None, base_row=None, apart=False, first=None):
    rows, depth = block
    slots = min(4, steps)
    bare = prepare is None
    count = len(sources)

    def body(s, mat_ref, *refs):
        source_refs, refs = refs[:count], refs[count:]
        base_ref = None
        if base is not None:
            base_ref, refs = refs[0], refs[1:]
        if first is not None:
            chunk_ref, chunk_sem = refs[-2:]
            refs = refs[:-2]
        out_refs, (buf, sem) = refs[:-2], refs[-2:]

        def fetch(i):
            row, col = place(i, s)
            piece = mat_ref.at[pl.ds(pl.multiple_of(row, 16), rows), pl.ds(pl.multiple_of(col, LANES), depth)]
            slot = lax.rem(i, slots)
            return pltpu.make_async_copy(piece, buf.at[slot], sem.at[slot])

        @pl.when(s[0] == 1)
        def _():
            given = source_refs
            if first is not None:
                piece = source_refs[0].at[pl.ds(first, tokens)]
                chunk = pltpu.make_async_copy(piece, chunk_ref, chunk_sem)
                chunk.start()
                given = [chunk_ref]
            for i in range(slots):
                fetch(i).start()
            if first is not None:
                chunk.wait()
            right_ref = source_refs[0]
            if not bare:
                right_ref = out_refs[-1]
                prepare(right_ref, *given)

            @pl.loop(0, steps)
            def _(i):
                fetch(i).wait()
                got = jnp.dot(buf[lax.rem(i, slots)], right_ref[...], preferred_element_type=F32)

                @pl.when(i + slots < steps)
                def _():
                    fetch(i + slots).start()

                if base_ref is not None:
                    start = pl.multiple_of(base_row(i, s), 16)
                    got = got + base_ref[pl.ds(start, rows)].astype(F32)
                if apart:
                    for which, ref in enumerate(out_refs[:steps]):

                        @pl.when(i == which)
                        def _(ref=ref):
                            ref[...] = got.astype(ref.dtype)
                else:
                    for ref, (size, begin, _) in zip(out_refs, outs):

                        @pl.when((i * rows >= begin) & (i * rows < begin + size))
                        def _(ref=ref, begin=begin):
                            at = pl.multiple_of(i * rows - begin, 16)
                            ref[pl.ds(at, rows)] = got.astype(ref.dtype)

    shapes = [jax.ShapeDtypeStruct((size, tokens), kind) for size, _, kind in outs]
    if not bare:
        shapes.append(jax.ShapeDtypeStruct((depth, tokens), LOW))
    return pl.pallas_call(
        body,
        in_specs=[SMEM, ANY]
        + [VMEM if first is None else ANY] * count
        + [VMEM] * (base is not None),
        out_specs=[VMEM] * len(shapes),
        out_shape=shapes,
        scratch_shapes=[
            pltpu.VMEM((slots, rows, depth), LOW),
            pltpu.SemaphoreType.DMA((slots,)),
        ]
        + ([] if first is None else [pltpu.VMEM((tokens, depth), F32), pltpu.SemaphoreType.DMA(())]),
        compiler_params=params(),
        cost_estimate=pl.CostEstimate(
            flops=2 * tokens * rows * depth * steps // WEIGHT,
            bytes_accessed=2 * rows * depth * steps // WEIGHT,
            transcendentals=0,
        ),
    )(flags, mat, *sources, *([] if base is None else [base]))


def pair_product(flags, mat, rows, own, other):
    _, height, depth = mat.shape
    tokens = own.shape[1]
    steps = height // rows
    slots = min(3, steps)

    def body(s, mat_ref, own_ref, other_ref, full_ref, low_ref, buf, sem):
        def fetch(i):
            piece = mat_ref.at[:, pl.ds(pl.multiple_of(i * rows, 16), rows)]
            slot = lax.rem(i, slots)
            return pltpu.make_async_copy(piece, buf.at[slot], sem.at[slot])

        @pl.when(s[0] == 1)
        def _():
            for i in range(slots):
                fetch(i).start()

            @pl.loop(0, steps)
            def _(i):
                fetch(i).wait()
                slot = lax.rem(i, slots)
                got = jnp.dot(buf[slot, s[1]], own_ref[...], preferred_element_type=F32)
                got = got + jnp.dot(
                    buf[slot, 1 - s[1]], other_ref[...], preferred_element_type=F32
                )

                @pl.when(i + slots < steps)
                def _():
                    fetch(i + slots).start()

                at = pl.ds(pl.multiple_of(i * rows, 16), rows)
                full_ref[at] = got
                low_ref[at] = got.astype(LOW)

    return pl.pallas_call(
        body,
        in_specs=[SMEM, ANY, VMEM, VMEM],
        out_specs=[VMEM, VMEM],
        out_shape=[
            jax.ShapeDtypeStruct((height, tokens), F32),
            jax.ShapeDtypeStruct((height, tokens), LOW),
        ],
        scratch_shapes=[
            pltpu.VMEM((slots, 2, rows, depth), LOW),
            pltpu.SemaphoreType.DMA((slots,)),
        ],
        compiler_params=params(),
        cost_estimate=pl.CostEstimate(
            flops=4 * tokens * height * depth // WEIGHT,
            bytes_accessed=4 * height * depth // WEIGHT,
            transcendentals=0,
        ),
    )(flags, mat, own, other)


def back_pair(flags, mat, parts, own, other):
    half, tokens = own.shape
    rows = mat.shape[0] // parts
    slots = 3

    def body(s, mat_ref, own_ref, other_ref, *refs):
        out_refs, (buf, sem) = refs[:parts], refs[parts:]

        def fetch(i, core):
            row = lax.bitwise_xor(s[2], lax.rem(i + 1, parts)) * rows
            piece = mat_ref.at[pl.ds(pl.multiple_of(row, 16), rows), core * half : (core + 1) * half]
            slot = lax.rem(i, slots)
            return pltpu.make_async_copy(piece, buf.at[slot, core], sem.at[slot, core])

        def both(i, act):
            for core in range(2):
                act(fetch(i, core))

        @pl.when(s[0] == 1)
        def _():
            for i in range(slots):
                both(i, lambda copy: copy.start())

            @pl.loop(0, parts)
            def _(i):
                both(i, lambda copy: copy.wait())
                slot = lax.rem(i, slots)
                got = jnp.dot(buf[slot, s[1]], own_ref[...], preferred_element_type=F32)
                got = got + jnp.dot(
                    buf[slot, 1 - s[1]], other_ref[...], preferred_element_type=F32
                )

                @pl.when(i + slots < parts)
                def _():
                    both(i + slots, lambda copy: copy.start())

                for which, ref in enumerate(out_refs):

                    @pl.when(i == which)
                    def _(ref=ref):
                        ref[...] = got.astype(ref.dtype)

    return pl.pallas_call(
        body,
        in_specs=[SMEM, ANY, VMEM, VMEM],
        out_specs=[VMEM] * parts,
        out_shape=[jax.ShapeDtypeStruct((rows, tokens), LOW)] * (parts - 1)
        + [jax.ShapeDtypeStruct((rows, tokens), F32)],
        scratch_shapes=[
            pltpu.VMEM((slots, 2, rows, half), LOW),
            pltpu.SemaphoreType.DMA((slots, 2)),
        ],
        compiler_params=params(),
        cost_estimate=pl.CostEstimate(
            flops=4 * tokens * rows * parts * half // WEIGHT,
            bytes_accessed=4 * rows * parts * half // WEIGHT,
            transcendentals=0,
        ),
    )(flags, mat, own, other)


def turned(right_ref, grad_ref):
    right_ref[...] = grad_ref[...].T.astype(LOW)


def hidden_of(right_ref, own_ref, slope_ref, *other_refs):
    row = 0
    for other_ref in other_refs:
        at = slice(row, row + other_ref.shape[0])
        total = own_ref[at] + other_ref[...].astype(F32)
        right_ref[at] = (total * slope_ref[at]).astype(LOW)
        row = at.stop


def hidden(flags, own, slope, others):
    def body(s, own_ref, slope_ref, *refs):
        @pl.when(s[0] == 1)
        def _():
            hidden_of(refs[-1], own_ref, slope_ref, *refs[:-1])

    return pl.pallas_call(
        body,
        in_specs=[SMEM] + [VMEM] * (2 + len(others)),
        out_specs=VMEM,
        out_shape=jax.ShapeDtypeStruct(own.shape, LOW),
        compiler_params=params(),
        cost_estimate=pl.CostEstimate(
            flops=own.size // WEIGHT, bytes_accessed=own.size // WEIGHT, transcendentals=0
        ),
    )(flags, own, slope, *others)


def split_rows(flags, mat):
    rows, cols = mat.shape
    step = 256
    half = step // 2
    count = rows // step
    slots = 4

    def body(s, mat_ref, out_ref, buf, done, sem_in, sem_out):
        def fetch(i, slot):
            piece = mat_ref.at[pl.ds(pl.multiple_of(i * step, step), step)]
            return pltpu.make_async_copy(piece, buf.at[slot], sem_in.at[slot])

        def put(i, slot):
            piece = out_ref.at[:, pl.ds(pl.multiple_of(i * half, half), half)]
            return pltpu.make_async_copy(done.at[slot], piece, sem_out.at[slot])

        @pl.when(s[0] == 1)
        def _():
            to = lax.broadcasted_iota(jnp.int32, (step, step), 0)
            source = lax.broadcasted_iota(jnp.int32, (step, step), 1)
            wanted = jnp.where(to < half, 2 * to, 2 * (to - half) + 1)
            pick = jnp.where(source == wanted, 1.0, 0.0).astype(LOW)
            for i in range(slots):
                fetch(i, i).start()

            @pl.loop(0, count // slots)
            def _(turn):
                for slot in range(slots):
                    i = turn * slots + slot
                    fetch(i, slot).wait()

                    @pl.when(turn > 0)
                    def _():
                        put(i - slots, slot).wait()

                    got = jnp.dot(pick, buf[slot], preferred_element_type=F32).astype(LOW)
                    done[slot, 0] = got[:half]
                    done[slot, 1] = got[half:]

                    @pl.when(turn < count // slots - 1)
                    def _():
                        fetch(i + slots, slot).start()

                    put(i, slot).start()

            for slot in range(slots):
                put(count - slots + slot, slot).wait()

    out = pl.pallas_call(
        body,
        in_specs=[SMEM, ANY],
        out_specs=ANY,
        out_shape=jax.ShapeDtypeStruct((2, rows // 2, cols), LOW),
        scratch_shapes=[
            pltpu.VMEM((slots, step, cols), LOW),
            pltpu.VMEM((slots, 2, half, cols), LOW),
            pltpu.SemaphoreType.DMA((slots,)),
            pltpu.SemaphoreType.DMA((slots,)),
        ],
        compiler_params=params(),
        cost_estimate=pl.CostEstimate(
            flops=2 * rows * step * cols // WEIGHT, bytes_accessed=4 * rows * cols // WEIGHT, transcendentals=0
        ),
    )(flags, mat)
    return out


def slope_of(flags, pre, start, tokens, half):
    cols = divisor(half, 768)
    per_half = half // cols

    def body(s, pre_ref, out_ref):
        out_ref[...] = gelu_slope(pre_ref[...]).T

    return pl.pallas_call(
        body,
        grid_spec=pltpu.PrefetchScalarGridSpec(
            num_scalar_prefetch=1,
            grid=(tokens // LANES, per_half),
            in_specs=[
                pl.BlockSpec((LANES, cols), lambda i, j, s: (start // LANES + i, s[1] * per_half + j))
            ],
            out_specs=pl.BlockSpec((cols, LANES), lambda i, j, s: (j, i)),
        ),
        out_shape=jax.ShapeDtypeStruct((half, tokens), F32),
        compiler_params=params(),
        cost_estimate=pl.CostEstimate(
            flops=half * tokens // WEIGHT, bytes_accessed=8 * half * tokens // WEIGHT, transcendentals=0
        ),
    )(flags, pre)


def join(flags, grad, parts):
    tokens, columns = grad.shape
    width = columns // PARTS

    def body(s, grad_ref, *refs):
        part_refs, (low_ref, term_ref) = refs[:PARTS], refs[PARTS:]

        @pl.when(s[0] == 1)
        def _():
            for slot, ref in enumerate(part_refs):
                start = pl.multiple_of(lax.bitwise_xor(s[2], slot) * width, LANES)
                term = ref[...]
                term_ref[pl.ds(start, width)] = term
                total = grad_ref[:, pl.ds(start, width)].T + term.astype(F32)
                low_ref[pl.ds(start, width)] = total.astype(LOW)

    shape = jax.ShapeDtypeStruct((columns, tokens), LOW)
    return pl.pallas_call(
        body,
        in_specs=[SMEM] + [VMEM] * (1 + PARTS),
        out_specs=[VMEM, VMEM],
        out_shape=[shape, shape],
        compiler_params=params(),
        cost_estimate=pl.CostEstimate(
            flops=4 * columns * tokens, bytes_accessed=4 * columns * tokens, transcendentals=0
        ),
    )(flags, grad, *parts)


def finish(flags, out, grad, start, term, parts):
    columns, tokens = term.shape
    width = columns // PARTS
    total_tokens = grad.shape[0]

    def body(s, *refs):
        grad_ref, term_ref, *part_refs = refs[int(out is not None) : -2]
        out_ref, joined = refs[-2:]
        for slot, ref in enumerate(part_refs):
            start = pl.multiple_of(lax.bitwise_xor(s[2], slot) * width, LANES)
            joined[pl.ds(start, width)] = ref[...]

        @pl.when(s[0] == 0)
        def _():
            out_ref[...] = grad_ref[...] + joined[...].astype(F32).T

        @pl.when(s[0] == 1)
        def _():
            source = lax.broadcasted_iota(jnp.int32, (2 * LANES, 2 * LANES), 1)
            to = lax.broadcasted_iota(jnp.int32, (2 * LANES, 2 * LANES), 0)
            wanted = jnp.where(source < LANES, 2 * source, 2 * (source - LANES) + 1)
            pick = jnp.where(to == wanted, 1.0, 0.0).astype(LOW)
            for group in range(columns // (2 * LANES)):
                even_at = group * LANES
                odd_at = columns // 2 + group * LANES
                even = joined[even_at : even_at + LANES]
                odd = joined[odd_at : odd_at + LANES]
                pair = jnp.concatenate([even, odd], axis=0)
                woven = jnp.dot(pick, pair, preferred_element_type=F32)
                at = slice(group * 2 * LANES, (group + 1) * 2 * LANES)
                first = term_ref[at].astype(F32).T
                out_ref[:, at] = grad_ref[:, at] + first + woven.T

    earlier = [] if out is None else [out]
    piece = pl.BlockSpec((width, LANES), lambda i, s: (0, i))
    rows = pl.BlockSpec((LANES, columns), lambda i, s: (start // LANES + i, 0))
    return pl.pallas_call(
        body,
        grid_spec=pltpu.PrefetchScalarGridSpec(
            num_scalar_prefetch=1,
            grid=(tokens // LANES,),
            in_specs=[ANY] * len(earlier)
            + [rows, pl.BlockSpec((columns, LANES), lambda i, s: (0, i))]
            + [piece] * PARTS,
            out_specs=rows,
            scratch_shapes=[pltpu.VMEM((columns, LANES), LOW)],
        ),
        out_shape=jax.ShapeDtypeStruct((total_tokens, columns), F32),
        input_output_aliases={1: 0} if earlier else {},
        compiler_params=params(),
    )(flags, *earlier, grad, term, *parts)


def local(grad_out, weight_in, weight_out, pre_act):
    hids = lax.axis_size("hid")
    section = lax.axis_index("section")
    side = lax.axis_index("wid") % 2
    is_up = section == 1

    def scalars(active_section):
        active = (section == active_section).astype(jnp.int32)
        return jnp.stack([active, side, lax.axis_index("hid") % PARTS]).astype(jnp.int32)

    down, up = scalars(0), scalars(1)

    def within(active, distance, block, axis="wid"):
        size = lax.axis_size(axis)
        pairs = [(active * size + i, active * size + (i ^ distance)) for i in range(size)]
        return lax.ppermute(block, ("section", axis), pairs)

    def everywhere(distance, block, axis="hid"):
        size = lax.axis_size(axis)
        return lax.ppermute(block, axis, [(i, i ^ distance) for i in range(size)])

    mat_in = weight_in[0]
    mat_out = weight_out[0]
    quarter, hid_tile = mat_in.shape
    half = hid_tile // 2
    batches, batch_tokens, _ = grad_out.shape
    total = batches * batch_tokens
    unit = total // sum(SHARES)
    starts = [unit * sum(SHARES[:k]) for k in range(len(SHARES))]
    sizes = [unit * share for share in SHARES]
    chunks = range(len(SHARES))
    last_chunk = len(SHARES) - 1
    grad = grad_out.reshape(total, quarter)
    pre = pre_act[0].reshape(total, hid_tile)
    grads = [grad[starts[k] : starts[k] + sizes[k]] for k in chunks]

    split_out = split_rows(up, mat_out)

    hid_rows = divisor(half // 2, 512)
    hid_steps = half // hid_rows
    part_rows = quarter // PARTS

    def product_out(flags, mat, first_row, sources, prepare, tokens, outs, base=None, first=None):
        return product(
            flags, mat, (hid_rows, quarter),
            lambda i, s: (first_row(s) + i * hid_rows, 0), hid_steps,
            sources, prepare, tokens, outs, base, lambda i, s: i * hid_rows, first=first,
        )

    def in_pieces(*shares):
        blocks = [max(1, hid_steps * sum(shares[: n + 1]) // sum(shares)) for n in range(len(shares))]
        ends = [0] + [hid_rows * block for block in blocks]
        return [(half, 0, F32)] + [(ends[n + 1] - ends[n], ends[n], LOW) for n in range(len(shares))]

    def exchange(active, pieces, earlier):
        if earlier is not None:
            pieces = [lax.optimization_barrier((piece, earlier))[0] for piece in pieces]
        return [within(active, 2, piece) for piece in pieces]

    def detour(piece):
        size = lax.axis_size("wid")
        return lax.ppermute(piece, ("section", "wid"), [(i, size + (i ^ 2)) for i in range(size)])

    def returned(piece):
        size = lax.axis_size("wid")
        return lax.ppermute(piece, ("section", "wid"), [(size + i, i) for i in range(size)])

    def across(term, distance):
        size = lax.axis_size("hid")
        pairs = [(i, size + (i ^ distance)) for i in range(size)]
        return lax.ppermute(term, ("section", "hid"), pairs)

    def product_in(flags, place, sources, prepare, tokens, kind):
        return product(
            flags, mat_in, (part_rows, half), place, PARTS, sources, prepare, tokens,
            [(quarter, 0, kind)],
        )

    def product_parts(flags, place, right, tokens, base):
        def part_of(i, s):
            return lax.bitwise_xor(s[2], lax.rem(i + 1, PARTS))

        return product(
            flags, mat_in, (part_rows, half), lambda i, s: place(part_of(i, s), s), PARTS,
            [right], None, tokens, [(part_rows, 0, LOW)] * 3 + [(part_rows, 0, F32)],
            base, lambda i, s: part_of(i, s) * part_rows, True,
        )

    def send_parts(active, parts):
        return [within(active, d + 1, part, "hid") for d, part in enumerate(parts[:-1])]

    def sum_hid(active, own, got):
        for part in got:
            own = own + part.astype(F32)
        distance = PARTS
        while distance < hids:
            own = own + within(active, distance, own, "hid")
            distance *= 2
        return own.astype(LOW)

    class Steps:
        def __init__(self):
            self.last = None

        def after(self, value):
            if self.last is None:
                return value
            return lax.optimization_barrier((value, self.last))[0]

    steps = Steps()
    steps.last = split_out
    hidden_full, hidden_other, slopes, parts_out, terms, gathered = {}, {}, {}, {}, {}, {}
    lows, core_got, parts_got = {}, {}, {}
    up_full, up_other, up_parts, up_terms, lasts = {}, {}, {}, {}, {}

    def down_send(k):
        sent, lows[k] = product_out(
            steps.after(down), mat_out, lambda s: (1 - s[1]) * half, [grad], turned,
            sizes[k], [(half, 0, LOW)], first=starts[k],
        )
        steps.last = sent
        core_got[k] = within(0, 1, sent)

    def down_hidden(k):
        full, *pieces = product_out(
            steps.after(down), mat_out, lambda s: s[1] * half, [lows[k]], None, sizes[k],
            in_pieces(*((1,) if k else (2, 1))), core_got[k],
        )
        steps.last = full
        hidden_full[k] = full
        if k > 0:
            hidden_other[k] = exchange(0, pieces, hidden_other[0][0])
        else:
            hidden_other[0] = [within(0, 2, pieces[0]), detour(pieces[1])]

    def down_return():
        hidden_other[0][1] = returned(steps.after(hidden_other[0][1]))

    def slope(k):
        slopes[k] = slope_of(steps.after(down), pre, starts[k], sizes[k], half)
        steps.last = slopes[k]

    def down_back(k):
        tokens = sizes[k]
        right = hidden(steps.after(down), hidden_full[k], slopes[k], hidden_other[k])
        swapped = within(0, 1, right)
        parts_out[k] = back_pair(down, mat_in, PARTS, right, swapped)
        parts_got[k] = send_parts(0, parts_out[k])
        steps.last = parts_out[k][0]

    def cross(k):
        terms[k] = sum_hid(0, steps.after(parts_out[k][-1]), parts_got[k])
        if k == 0:
            crossed = across(terms[k], 0)
            steps.last = crossed
            gathered[k] = [crossed] + [within(1, d, crossed, "hid") for d in range(1, PARTS)]
        else:
            gathered[k] = [across(terms[k], d) for d in range(PARTS)]
            steps.last = gathered[k][0]

    def up_hidden(k):
        tokens = sizes[k]
        low, up_terms[k] = join(steps.after(up), grads[k], gathered[k])
        low_other = within(1, 1, low)
        flags = up
        if k + 1 in parts_got:
            flags = lax.optimization_barrier((up, *parts_got[k + 1]))[0]
        full, low_grad = pair_product(flags, split_out, hid_rows, low, low_other)
        steps.last = full
        up_full[k] = full
        up_other[k] = exchange(1, [low_grad], up_other[k - 1][0] if k else None)

    def place(part, core):
        row = core * (PARTS // 2) + lax.rem(part, PARTS // 2)
        return row * part_rows, lax.div(part, PARTS // 2) * half

    def up_back(k):
        tokens = sizes[k]
        sent, right = product_in(
            steps.after(up), lambda i, s: place(i, 1 - s[1]),
            [up_full[k], slopes[k]] + up_other[k], hidden_of, tokens, F32,
        )
        got = within(1, 1, sent)
        up_parts[k] = product_parts(up, lambda i, s: place(i, s[1]), right, tokens, got)
        steps.last = up_parts[k][0]

    def gather(k):
        own = steps.after(up_parts[k][-1])
        last = jnp.where(is_up, sum_hid(1, own, send_parts(1, up_parts[k])), terms[k])
        steps.last = last
        lasts[k] = [last] + [everywhere(d, last) for d in range(1, PARTS)]
        steps.last = lasts[k][1]

    for k in chunks:
        down_send(k)
    for k in chunks:
        down_hidden(k)
    down_return()
    slope(0)
    down_back(0)
    slope(1)
    cross(0)
    down_back(1)
    up_hidden(0)
    cross(1)
    up_hidden(1)
    up_back(0)
    gather(0)
    up_back(1)
    out = finish(steps.after(up), None, grad, starts[0], up_terms[0], lasts[0])
    steps.last = out
    gather(1)
    k = last_chunk
    out = finish(up, out, grad, starts[k], up_terms[k], lasts[k])
    return out.reshape(1, batches, batch_tokens, quarter)


def solution(mesh):
    return jax.shard_map(
        local,
        mesh=mesh,
        in_specs=(
            P(None, None, "wid"),
            P("section", "wid", "hid"),
            P("section", "hid", "wid"),
            P("section", None, None, "hid"),
        ),
        out_specs=P("section", None, None, "wid"),
        check_vma=False,
    )
```

```python
import jax
import jax.numpy as jnp
from jax import lax
from jax.experimental import pallas as pl
from jax.experimental.pallas import tpu as pltpu
from jax.sharding import PartitionSpec as P

SHARES = (1, 1)
PARTS = 4
LANES = 128
WEIGHT = 4096
LIMIT = 46 * 1024 * 1024
LOW = jnp.bfloat16
F32 = jnp.float32


def gelu_slope(pre):
    normal_cdf = 0.5 * (1.0 + lax.erf(pre * 0.7071067811865476))
    density = jnp.exp(-0.5 * pre * pre) * 0.3989422804014327
    return normal_cdf + pre * density


def params():
    return pltpu.CompilerParams(vmem_limit_bytes=LIMIT)


def divisor(size, most):
    return max(r for r in range(16, most + 1, 16) if size % r == 0)


SMEM = pl.BlockSpec(memory_space=pltpu.SMEM)
VMEM = pl.BlockSpec(memory_space=pltpu.VMEM)
ANY = pl.BlockSpec(memory_space=pl.ANY)


def product(flags, mat, block, place, steps, sources, prepare, tokens, outs, base=None, base_row=None, apart=False, first=None):
    rows, depth = block
    slots = min(4, steps)
    bare = prepare is None
    count = len(sources)

    def body(s, mat_ref, *refs):
        source_refs, refs = refs[:count], refs[count:]
        base_ref = None
        if base is not None:
            base_ref, refs = refs[0], refs[1:]
        if first is not None:
            chunk_ref, chunk_sem = refs[-2:]
            refs = refs[:-2]
        out_refs, (buf, sem) = refs[:-2], refs[-2:]

        def fetch(i):
            row, col = place(i, s)
            piece = mat_ref.at[pl.ds(pl.multiple_of(row, 16), rows), pl.ds(pl.multiple_of(col, LANES), depth)]
            slot = lax.rem(i, slots)
            return pltpu.make_async_copy(piece, buf.at[slot], sem.at[slot])

        @pl.when(s[0] == 1)
        def _():
            given = source_refs
            if first is not None:
                piece = source_refs[0].at[pl.ds(first, tokens)]
                chunk = pltpu.make_async_copy(piece, chunk_ref, chunk_sem)
                chunk.start()
                given = [chunk_ref]
            for i in range(slots):
                fetch(i).start()
            if first is not None:
                chunk.wait()
            right_ref = source_refs[0]
            if not bare:
                right_ref = out_refs[-1]
                prepare(right_ref, *given)

            @pl.loop(0, steps)
            def _(i):
                fetch(i).wait()
                got = jnp.dot(buf[lax.rem(i, slots)], right_ref[...], preferred_element_type=F32)

                @pl.when(i + slots < steps)
                def _():
                    fetch(i + slots).start()

                if base_ref is not None:
                    start = pl.multiple_of(base_row(i, s), 16)
                    got = got + base_ref[pl.ds(start, rows)].astype(F32)
                if apart:
                    for which, ref in enumerate(out_refs[:steps]):

                        @pl.when(i == which)
                        def _(ref=ref):
                            ref[...] = got.astype(ref.dtype)
                else:
                    for ref, (size, begin, _) in zip(out_refs, outs):

                        @pl.when((i * rows >= begin) & (i * rows < begin + size))
                        def _(ref=ref, begin=begin):
                            at = pl.multiple_of(i * rows - begin, 16)
                            ref[pl.ds(at, rows)] = got.astype(ref.dtype)

    shapes = [jax.ShapeDtypeStruct((size, tokens), kind) for size, _, kind in outs]
    if not bare:
        shapes.append(jax.ShapeDtypeStruct((depth, tokens), LOW))
    return pl.pallas_call(
        body,
        in_specs=[SMEM, ANY]
        + [VMEM if first is None else ANY] * count
        + [VMEM] * (base is not None),
        out_specs=[VMEM] * len(shapes),
        out_shape=shapes,
        scratch_shapes=[
            pltpu.VMEM((slots, rows, depth), LOW),
            pltpu.SemaphoreType.DMA((slots,)),
        ]
        + ([] if first is None else [pltpu.VMEM((tokens, depth), F32), pltpu.SemaphoreType.DMA(())]),
        compiler_params=params(),
        cost_estimate=pl.CostEstimate(
            flops=2 * tokens * rows * depth * steps // WEIGHT,
            bytes_accessed=2 * rows * depth * steps // WEIGHT,
            transcendentals=0,
        ),
    )(flags, mat, *sources, *([] if base is None else [base]))


def pair_product(flags, mat, rows, own, other):
    _, height, depth = mat.shape
    tokens = own.shape[1]
    steps = height // rows
    slots = min(3, steps)

    def body(s, mat_ref, own_ref, other_ref, full_ref, low_ref, buf, sem):
        def fetch(i):
            piece = mat_ref.at[:, pl.ds(pl.multiple_of(i * rows, 16), rows)]
            slot = lax.rem(i, slots)
            return pltpu.make_async_copy(piece, buf.at[slot], sem.at[slot])

        @pl.when(s[0] == 1)
        def _():
            for i in range(slots):
                fetch(i).start()

            @pl.loop(0, steps)
            def _(i):
                fetch(i).wait()
                slot = lax.rem(i, slots)
                got = jnp.dot(buf[slot, s[1]], own_ref[...], preferred_element_type=F32)
                got = got + jnp.dot(
                    buf[slot, 1 - s[1]], other_ref[...], preferred_element_type=F32
                )

                @pl.when(i + slots < steps)
                def _():
                    fetch(i + slots).start()

                at = pl.ds(pl.multiple_of(i * rows, 16), rows)
                full_ref[at] = got
                low_ref[at] = got.astype(LOW)

    return pl.pallas_call(
        body,
        in_specs=[SMEM, ANY, VMEM, VMEM],
        out_specs=[VMEM, VMEM],
        out_shape=[
            jax.ShapeDtypeStruct((height, tokens), F32),
            jax.ShapeDtypeStruct((height, tokens), LOW),
        ],
        scratch_shapes=[
            pltpu.VMEM((slots, 2, rows, depth), LOW),
            pltpu.SemaphoreType.DMA((slots,)),
        ],
        compiler_params=params(),
        cost_estimate=pl.CostEstimate(
            flops=4 * tokens * height * depth // WEIGHT,
            bytes_accessed=4 * height * depth // WEIGHT,
            transcendentals=0,
        ),
    )(flags, mat, own, other)


def back_pair(flags, mat, parts, own, other):
    half, tokens = own.shape
    rows = mat.shape[0] // parts
    slots = 3

    def body(s, mat_ref, own_ref, other_ref, *refs):
        out_refs, (buf, sem) = refs[:parts], refs[parts:]

        def fetch(i, core):
            row = lax.bitwise_xor(s[2], lax.rem(i + 1, parts)) * rows
            piece = mat_ref.at[pl.ds(pl.multiple_of(row, 16), rows), core * half : (core + 1) * half]
            slot = lax.rem(i, slots)
            return pltpu.make_async_copy(piece, buf.at[slot, core], sem.at[slot, core])

        def both(i, act):
            for core in range(2):
                act(fetch(i, core))

        @pl.when(s[0] == 1)
        def _():
            for i in range(slots):
                both(i, lambda copy: copy.start())

            @pl.loop(0, parts)
            def _(i):
                both(i, lambda copy: copy.wait())
                slot = lax.rem(i, slots)
                got = jnp.dot(buf[slot, s[1]], own_ref[...], preferred_element_type=F32)
                got = got + jnp.dot(
                    buf[slot, 1 - s[1]], other_ref[...], preferred_element_type=F32
                )

                @pl.when(i + slots < parts)
                def _():
                    both(i + slots, lambda copy: copy.start())

                for which, ref in enumerate(out_refs):

                    @pl.when(i == which)
                    def _(ref=ref):
                        ref[...] = got.astype(ref.dtype)

    return pl.pallas_call(
        body,
        in_specs=[SMEM, ANY, VMEM, VMEM],
        out_specs=[VMEM] * parts,
        out_shape=[jax.ShapeDtypeStruct((rows, tokens), LOW)] * (parts - 1)
        + [jax.ShapeDtypeStruct((rows, tokens), F32)],
        scratch_shapes=[
            pltpu.VMEM((slots, 2, rows, half), LOW),
            pltpu.SemaphoreType.DMA((slots, 2)),
        ],
        compiler_params=params(),
        cost_estimate=pl.CostEstimate(
            flops=4 * tokens * rows * parts * half // WEIGHT,
            bytes_accessed=4 * rows * parts * half // WEIGHT,
            transcendentals=0,
        ),
    )(flags, mat, own, other)


def turned(right_ref, grad_ref):
    right_ref[...] = grad_ref[...].T.astype(LOW)


def hidden_of(right_ref, own_ref, slope_ref, *other_refs):
    row = 0
    for other_ref in other_refs:
        at = slice(row, row + other_ref.shape[0])
        total = own_ref[at] + other_ref[...].astype(F32)
        right_ref[at] = (total * slope_ref[at]).astype(LOW)
        row = at.stop


def hidden(flags, own, slope, others):
    def body(s, own_ref, slope_ref, *refs):
        @pl.when(s[0] == 1)
        def _():
            hidden_of(refs[-1], own_ref, slope_ref, *refs[:-1])

    return pl.pallas_call(
        body,
        in_specs=[SMEM] + [VMEM] * (2 + len(others)),
        out_specs=VMEM,
        out_shape=jax.ShapeDtypeStruct(own.shape, LOW),
        compiler_params=params(),
        cost_estimate=pl.CostEstimate(
            flops=own.size // WEIGHT, bytes_accessed=own.size // WEIGHT, transcendentals=0
        ),
    )(flags, own, slope, *others)


def split_rows(flags, mat):
    rows, cols = mat.shape
    step = 256
    half = step // 2
    count = rows // step
    slots = 4

    def body(s, mat_ref, out_ref, buf, done, sem_in, sem_out):
        def fetch(i, slot):
            piece = mat_ref.at[pl.ds(pl.multiple_of(i * step, step), step)]
            return pltpu.make_async_copy(piece, buf.at[slot], sem_in.at[slot])

        def put(i, slot):
            piece = out_ref.at[:, pl.ds(pl.multiple_of(i * half, half), half)]
            return pltpu.make_async_copy(done.at[slot], piece, sem_out.at[slot])

        @pl.when(s[0] == 1)
        def _():
            to = lax.broadcasted_iota(jnp.int32, (step, step), 0)
            source = lax.broadcasted_iota(jnp.int32, (step, step), 1)
            wanted = jnp.where(to < half, 2 * to, 2 * (to - half) + 1)
            pick = jnp.where(source == wanted, 1.0, 0.0).astype(LOW)
            for i in range(slots):
                fetch(i, i).start()

            @pl.loop(0, count // slots)
            def _(turn):
                for slot in range(slots):
                    i = turn * slots + slot
                    fetch(i, slot).wait()

                    @pl.when(turn > 0)
                    def _():
                        put(i - slots, slot).wait()

                    got = jnp.dot(pick, buf[slot], preferred_element_type=F32).astype(LOW)
                    done[slot, 0] = got[:half]
                    done[slot, 1] = got[half:]

                    @pl.when(turn < count // slots - 1)
                    def _():
                        fetch(i + slots, slot).start()

                    put(i, slot).start()

            for slot in range(slots):
                put(count - slots + slot, slot).wait()

    out = pl.pallas_call(
        body,
        in_specs=[SMEM, ANY],
        out_specs=ANY,
        out_shape=jax.ShapeDtypeStruct((2, rows // 2, cols), LOW),
        scratch_shapes=[
            pltpu.VMEM((slots, step, cols), LOW),
            pltpu.VMEM((slots, 2, half, cols), LOW),
            pltpu.SemaphoreType.DMA((slots,)),
            pltpu.SemaphoreType.DMA((slots,)),
        ],
        compiler_params=params(),
        cost_estimate=pl.CostEstimate(
            flops=2 * rows * step * cols // WEIGHT, bytes_accessed=4 * rows * cols // WEIGHT, transcendentals=0
        ),
    )(flags, mat)
    return out


def slope_of(flags, pre, start, tokens, half):
    cols = divisor(half, 768)
    per_half = half // cols

    def body(s, pre_ref, out_ref):
        out_ref[...] = gelu_slope(pre_ref[...]).T

    return pl.pallas_call(
        body,
        grid_spec=pltpu.PrefetchScalarGridSpec(
            num_scalar_prefetch=1,
            grid=(tokens // LANES, per_half),
            in_specs=[
                pl.BlockSpec((LANES, cols), lambda i, j, s: (start // LANES + i, s[1] * per_half + j))
            ],
            out_specs=pl.BlockSpec((cols, LANES), lambda i, j, s: (j, i)),
        ),
        out_shape=jax.ShapeDtypeStruct((half, tokens), F32),
        compiler_params=params(),
        cost_estimate=pl.CostEstimate(
            flops=half * tokens // WEIGHT, bytes_accessed=8 * half * tokens // WEIGHT, transcendentals=0
        ),
    )(flags, pre)


def join(flags, grad, parts):
    tokens, columns = grad.shape
    width = columns // PARTS

    def body(s, grad_ref, *refs):
        part_refs, (low_ref, term_ref) = refs[:PARTS], refs[PARTS:]

        @pl.when(s[0] == 1)
        def _():
            for slot, ref in enumerate(part_refs):
                start = pl.multiple_of(lax.bitwise_xor(s[2], slot) * width, LANES)
                term = ref[...]
                term_ref[pl.ds(start, width)] = term
                total = grad_ref[:, pl.ds(start, width)].T + term.astype(F32)
                low_ref[pl.ds(start, width)] = total.astype(LOW)

    shape = jax.ShapeDtypeStruct((columns, tokens), LOW)
    return pl.pallas_call(
        body,
        in_specs=[SMEM] + [VMEM] * (1 + PARTS),
        out_specs=[VMEM, VMEM],
        out_shape=[shape, shape],
        compiler_params=params(),
        cost_estimate=pl.CostEstimate(
            flops=4 * columns * tokens, bytes_accessed=4 * columns * tokens, transcendentals=0
        ),
    )(flags, grad, *parts)


def finish(flags, out, grad, start, term, parts):
    columns, tokens = term.shape
    width = columns // PARTS
    total_tokens = grad.shape[0]

    def body(s, *refs):
        grad_ref, term_ref, *part_refs = refs[int(out is not None) : -2]
        out_ref, joined = refs[-2:]
        for slot, ref in enumerate(part_refs):
            start = pl.multiple_of(lax.bitwise_xor(s[2], slot) * width, LANES)
            joined[pl.ds(start, width)] = ref[...]

        @pl.when(s[0] == 0)
        def _():
            out_ref[...] = grad_ref[...] + joined[...].astype(F32).T

        @pl.when(s[0] == 1)
        def _():
            source = lax.broadcasted_iota(jnp.int32, (2 * LANES, 2 * LANES), 1)
            to = lax.broadcasted_iota(jnp.int32, (2 * LANES, 2 * LANES), 0)
            wanted = jnp.where(source < LANES, 2 * source, 2 * (source - LANES) + 1)
            pick = jnp.where(to == wanted, 1.0, 0.0).astype(LOW)
            for group in range(columns // (2 * LANES)):
                even_at = group * LANES
                odd_at = columns // 2 + group * LANES
                even = joined[even_at : even_at + LANES]
                odd = joined[odd_at : odd_at + LANES]
                pair = jnp.concatenate([even, odd], axis=0)
                woven = jnp.dot(pick, pair, preferred_element_type=F32)
                at = slice(group * 2 * LANES, (group + 1) * 2 * LANES)
                first = term_ref[at].astype(F32).T
                out_ref[:, at] = grad_ref[:, at] + first + woven.T

    earlier = [] if out is None else [out]
    piece = pl.BlockSpec((width, LANES), lambda i, s: (0, i))
    rows = pl.BlockSpec((LANES, columns), lambda i, s: (start // LANES + i, 0))
    return pl.pallas_call(
        body,
        grid_spec=pltpu.PrefetchScalarGridSpec(
            num_scalar_prefetch=1,
            grid=(tokens // LANES,),
            in_specs=[ANY] * len(earlier)
            + [rows, pl.BlockSpec((columns, LANES), lambda i, s: (0, i))]
            + [piece] * PARTS,
            out_specs=rows,
            scratch_shapes=[pltpu.VMEM((columns, LANES), LOW)],
        ),
        out_shape=jax.ShapeDtypeStruct((total_tokens, columns), F32),
        input_output_aliases={1: 0} if earlier else {},
        compiler_params=params(),
    )(flags, *earlier, grad, term, *parts)


def local(grad_out, weight_in, weight_out, pre_act):
    hids = lax.axis_size("hid")
    section = lax.axis_index("section")
    side = lax.axis_index("wid") % 2
    is_up = section == 1

    def scalars(active_section):
        active = (section == active_section).astype(jnp.int32)
        return jnp.stack([active, side, lax.axis_index("hid") % PARTS]).astype(jnp.int32)

    down, up = scalars(0), scalars(1)

    def within(active, distance, block, axis="wid"):
        size = lax.axis_size(axis)
        pairs = [(active * size + i, active * size + (i ^ distance)) for i in range(size)]
        return lax.ppermute(block, ("section", axis), pairs)

    def everywhere(distance, block, axis="hid"):
        size = lax.axis_size(axis)
        return lax.ppermute(block, axis, [(i, i ^ distance) for i in range(size)])

    mat_in = weight_in[0]
    mat_out = weight_out[0]
    quarter, hid_tile = mat_in.shape
    half = hid_tile // 2
    batches, batch_tokens, _ = grad_out.shape
    total = batches * batch_tokens
    unit = total // sum(SHARES)
    starts = [unit * sum(SHARES[:k]) for k in range(len(SHARES))]
    sizes = [unit * share for share in SHARES]
    chunks = range(len(SHARES))
    last_chunk = len(SHARES) - 1
    grad = grad_out.reshape(total, quarter)
    pre = pre_act[0].reshape(total, hid_tile)
    grads = [grad[starts[k] : starts[k] + sizes[k]] for k in chunks]

    split_out = split_rows(up, mat_out)

    hid_rows = divisor(half // 2, 512)
    hid_steps = half // hid_rows
    part_rows = quarter // PARTS

    def product_out(flags, mat, first_row, sources, prepare, tokens, outs, base=None, first=None):
        return product(
            flags, mat, (hid_rows, quarter),
            lambda i, s: (first_row(s) + i * hid_rows, 0), hid_steps,
            sources, prepare, tokens, outs, base, lambda i, s: i * hid_rows, first=first,
        )

    def in_pieces(*shares):
        blocks = [max(1, hid_steps * sum(shares[: n + 1]) // sum(shares)) for n in range(len(shares))]
        ends = [0] + [hid_rows * block for block in blocks]
        return [(half, 0, F32)] + [(ends[n + 1] - ends[n], ends[n], LOW) for n in range(len(shares))]

    def exchange(active, pieces, earlier):
        if earlier is not None:
            pieces = [lax.optimization_barrier((piece, earlier))[0] for piece in pieces]
        return [within(active, 2, piece) for piece in pieces]

    def detour(active, piece):
        size = lax.axis_size("wid")
        pairs = [(active * size + i, (1 - active) * size + (i ^ 2)) for i in range(size)]
        return lax.ppermute(piece, ("section", "wid"), pairs)

    def returned(active, piece):
        size = lax.axis_size("wid")
        pairs = [((1 - active) * size + i, active * size + i) for i in range(size)]
        return lax.ppermute(piece, ("section", "wid"), pairs)

    def across(term, distance):
        size = lax.axis_size("hid")
        pairs = [(i, size + (i ^ distance)) for i in range(size)]
        return lax.ppermute(term, ("section", "hid"), pairs)

    def product_in(flags, place, sources, prepare, tokens, kind):
        return product(
            flags, mat_in, (part_rows, half), place, PARTS, sources, prepare, tokens,
            [(quarter, 0, kind)],
        )

    def product_parts(flags, place, right, tokens, base):
        def part_of(i, s):
            return lax.bitwise_xor(s[2], lax.rem(i + 1, PARTS))

        return product(
            flags, mat_in, (part_rows, half), lambda i, s: place(part_of(i, s), s), PARTS,
            [right], None, tokens, [(part_rows, 0, LOW)] * 3 + [(part_rows, 0, F32)],
            base, lambda i, s: part_of(i, s) * part_rows, True,
        )

    def send_parts(active, parts):
        return [within(active, d + 1, part, "hid") for d, part in enumerate(parts[:-1])]

    def sum_hid(active, own, got):
        for part in got:
            own = own + part.astype(F32)
        distance = PARTS
        while distance < hids:
            own = own + within(active, distance, own, "hid")
            distance *= 2
        return own.astype(LOW)

    class Steps:
        def __init__(self):
            self.last = None

        def after(self, value):
            if self.last is None:
                return value
            return lax.optimization_barrier((value, self.last))[0]

    steps = Steps()
    steps.last = split_out
    hidden_full, hidden_other, slopes, parts_out, terms, gathered = {}, {}, {}, {}, {}, {}
    lows, core_got, parts_got = {}, {}, {}
    up_full, up_other, up_parts, up_terms, lasts = {}, {}, {}, {}, {}

    def down_send(k):
        sent, lows[k] = product_out(
            steps.after(down), mat_out, lambda s: (1 - s[1]) * half, [grad], turned,
            sizes[k], [(half, 0, LOW)], first=starts[k],
        )
        steps.last = sent
        core_got[k] = within(0, 1, sent)

    def down_hidden(k):
        full, *pieces = product_out(
            steps.after(down), mat_out, lambda s: s[1] * half, [lows[k]], None, sizes[k],
            in_pieces(*((1,) if k else (2, 1))), core_got[k],
        )
        steps.last = full
        hidden_full[k] = full
        if k > 0:
            hidden_other[k] = exchange(0, pieces, hidden_other[0][0])
        else:
            hidden_other[0] = [within(0, 2, pieces[0]), detour(0, pieces[1])]

    def down_return():
        hidden_other[0][1] = returned(0, steps.after(hidden_other[0][1]))

    def slope(k):
        slopes[k] = slope_of(steps.after(down), pre, starts[k], sizes[k], half)
        steps.last = slopes[k]

    def down_back(k):
        tokens = sizes[k]
        right = hidden(steps.after(down), hidden_full[k], slopes[k], hidden_other[k])
        swapped = within(0, 1, right)
        parts_out[k] = back_pair(down, mat_in, PARTS, right, swapped)
        parts_got[k] = send_parts(0, parts_out[k])
        steps.last = parts_out[k][0]

    def cross(k):
        terms[k] = sum_hid(0, steps.after(parts_out[k][-1]), parts_got[k])
        if k == 0:
            crossed = across(terms[k], 0)
            steps.last = crossed
            gathered[k] = [crossed] + [within(1, d, crossed, "hid") for d in range(1, PARTS)]
        else:
            gathered[k] = [across(terms[k], d) for d in range(PARTS)]
            steps.last = gathered[k][0]

    def up_hidden(k):
        tokens = sizes[k]
        low, up_terms[k] = join(steps.after(up), grads[k], gathered[k])
        low_other = within(1, 1, low)
        flags = up
        if k + 1 in parts_got:
            flags = lax.optimization_barrier((up, *parts_got[k + 1]))[0]
        full, low_grad = pair_product(flags, split_out, hid_rows, low, low_other)
        steps.last = full
        up_full[k] = full
        up_other[k] = exchange(
            1, [low_grad if k < last_chunk else low_grad[hid_rows:]], up_other[k - 1][0] if k else None
        )
        if k == last_chunk:
            up_other[k].insert(0, detour(1, low_grad[:hid_rows]))

    def up_return():
        up_other[last_chunk][0] = returned(1, steps.after(up_other[last_chunk][0]))

    def place(part, core):
        row = core * (PARTS // 2) + lax.rem(part, PARTS // 2)
        return row * part_rows, lax.div(part, PARTS // 2) * half

    def up_back(k):
        tokens = sizes[k]
        sent, right = product_in(
            steps.after(up), lambda i, s: place(i, 1 - s[1]),
            [up_full[k], slopes[k]] + up_other[k], hidden_of, tokens, F32,
        )
        got = within(1, 1, sent)
        up_parts[k] = product_parts(up, lambda i, s: place(i, s[1]), right, tokens, got)
        steps.last = up_parts[k][0]

    def gather(k):
        own = steps.after(up_parts[k][-1])
        if k < last_chunk:
            own = lax.optimization_barrier((own, up_other[last_chunk][0]))[0]
        last = jnp.where(is_up, sum_hid(1, own, send_parts(1, up_parts[k])), terms[k])
        steps.last = last
        lasts[k] = [last] + [everywhere(d, last) for d in range(1, PARTS)]

    for k in chunks:
        down_send(k)
    for k in chunks:
        down_hidden(k)
    down_return()
    slope(0)
    down_back(0)
    slope(1)
    cross(0)
    down_back(1)
    up_hidden(0)
    cross(1)
    up_hidden(1)
    up_back(0)
    up_return()
    gather(0)
    up_back(1)
    out = finish(steps.after(up), None, grad, starts[0], up_terms[0], lasts[0])
    steps.last = out
    gather(1)
    k = last_chunk
    out = finish(up, out, grad, starts[k], up_terms[k], lasts[k])
    return out.reshape(1, batches, batch_tokens, quarter)


def solution(mesh):
    return jax.shard_map(
        local,
        mesh=mesh,
        in_specs=(
            P(None, None, "wid"),
            P("section", "wid", "hid"),
            P("section", "hid", "wid"),
            P("section", None, None, "hid"),
        ),
        out_specs=P("section", None, None, "wid"),
        check_vma=False,
    )
```

```python
import jax
import jax.numpy as jnp
from jax import lax
from jax.experimental import pallas as pl
from jax.experimental.pallas import tpu as pltpu
from jax.sharding import PartitionSpec as P

SHARES = (1, 1)
PARTS = 4
LANES = 128
WEIGHT = 4096
LIMIT = 46 * 1024 * 1024
LOW = jnp.bfloat16
F32 = jnp.float32


def gelu_slope(pre):
    normal_cdf = 0.5 * (1.0 + lax.erf(pre * 0.7071067811865476))
    density = jnp.exp(-0.5 * pre * pre) * 0.3989422804014327
    return normal_cdf + pre * density


def params():
    return pltpu.CompilerParams(vmem_limit_bytes=LIMIT)


def divisor(size, most):
    return max(r for r in range(16, most + 1, 16) if size % r == 0)


SMEM = pl.BlockSpec(memory_space=pltpu.SMEM)
VMEM = pl.BlockSpec(memory_space=pltpu.VMEM)
ANY = pl.BlockSpec(memory_space=pl.ANY)


def product(flags, mat, block, place, steps, sources, prepare, tokens, outs, base=None, base_row=None, apart=False, first=None):
    rows, depth = block
    slots = min(4, steps)
    bare = prepare is None
    count = len(sources)

    def body(s, mat_ref, *refs):
        source_refs, refs = refs[:count], refs[count:]
        base_ref = None
        if base is not None:
            base_ref, refs = refs[0], refs[1:]
        if first is not None:
            chunk_ref, chunk_sem = refs[-2:]
            refs = refs[:-2]
        out_refs, (buf, sem) = refs[:-2], refs[-2:]

        def fetch(i):
            row, col = place(i, s)
            piece = mat_ref.at[pl.ds(pl.multiple_of(row, 16), rows), pl.ds(pl.multiple_of(col, LANES), depth)]
            slot = lax.rem(i, slots)
            return pltpu.make_async_copy(piece, buf.at[slot], sem.at[slot])

        @pl.when(s[0] == 1)
        def _():
            given = source_refs
            if first is not None:
                piece = source_refs[0].at[pl.ds(first, tokens)]
                chunk = pltpu.make_async_copy(piece, chunk_ref, chunk_sem)
                chunk.start()
                given = [chunk_ref]
            for i in range(slots):
                fetch(i).start()
            if first is not None:
                chunk.wait()
            right_ref = source_refs[0]
            if not bare:
                right_ref = out_refs[-1]
                prepare(right_ref, *given)

            @pl.loop(0, steps)
            def _(i):
                fetch(i).wait()
                got = jnp.dot(buf[lax.rem(i, slots)], right_ref[...], preferred_element_type=F32)

                @pl.when(i + slots < steps)
                def _():
                    fetch(i + slots).start()

                if base_ref is not None:
                    start = pl.multiple_of(base_row(i, s), 16)
                    got = got + base_ref[pl.ds(start, rows)].astype(F32)
                if apart:
                    for which, ref in enumerate(out_refs[:steps]):

                        @pl.when(i == which)
                        def _(ref=ref):
                            ref[...] = got.astype(ref.dtype)
                else:
                    for ref, (size, begin, _) in zip(out_refs, outs):

                        @pl.when((i * rows >= begin) & (i * rows < begin + size))
                        def _(ref=ref, begin=begin):
                            at = pl.multiple_of(i * rows - begin, 16)
                            ref[pl.ds(at, rows)] = got.astype(ref.dtype)

    shapes = [jax.ShapeDtypeStruct((size, tokens), kind) for size, _, kind in outs]
    if not bare:
        shapes.append(jax.ShapeDtypeStruct((depth, tokens), LOW))
    return pl.pallas_call(
        body,
        in_specs=[SMEM, ANY]
        + [VMEM if first is None else ANY] * count
        + [VMEM] * (base is not None),
        out_specs=[VMEM] * len(shapes),
        out_shape=shapes,
        scratch_shapes=[
            pltpu.VMEM((slots, rows, depth), LOW),
            pltpu.SemaphoreType.DMA((slots,)),
        ]
        + ([] if first is None else [pltpu.VMEM((tokens, depth), F32), pltpu.SemaphoreType.DMA(())]),
        compiler_params=params(),
        cost_estimate=pl.CostEstimate(
            flops=2 * tokens * rows * depth * steps // WEIGHT,
            bytes_accessed=2 * rows * depth * steps // WEIGHT,
            transcendentals=0,
        ),
    )(flags, mat, *sources, *([] if base is None else [base]))


def pair_product(flags, mat, rows, own, other):
    _, height, depth = mat.shape
    tokens = own.shape[1]
    steps = height // rows
    slots = min(3, steps)

    def body(s, mat_ref, own_ref, other_ref, full_ref, low_ref, buf, sem):
        def fetch(i):
            piece = mat_ref.at[:, pl.ds(pl.multiple_of(i * rows, 16), rows)]
            slot = lax.rem(i, slots)
            return pltpu.make_async_copy(piece, buf.at[slot], sem.at[slot])

        @pl.when(s[0] == 1)
        def _():
            for i in range(slots):
                fetch(i).start()

            @pl.loop(0, steps)
            def _(i):
                fetch(i).wait()
                slot = lax.rem(i, slots)
                got = jnp.dot(buf[slot, s[1]], own_ref[...], preferred_element_type=F32)
                got = got + jnp.dot(
                    buf[slot, 1 - s[1]], other_ref[...], preferred_element_type=F32
                )

                @pl.when(i + slots < steps)
                def _():
                    fetch(i + slots).start()

                at = pl.ds(pl.multiple_of(i * rows, 16), rows)
                full_ref[at] = got
                low_ref[at] = got.astype(LOW)

    return pl.pallas_call(
        body,
        in_specs=[SMEM, ANY, VMEM, VMEM],
        out_specs=[VMEM, VMEM],
        out_shape=[
            jax.ShapeDtypeStruct((height, tokens), F32),
            jax.ShapeDtypeStruct((height, tokens), LOW),
        ],
        scratch_shapes=[
            pltpu.VMEM((slots, 2, rows, depth), LOW),
            pltpu.SemaphoreType.DMA((slots,)),
        ],
        compiler_params=params(),
        cost_estimate=pl.CostEstimate(
            flops=4 * tokens * height * depth // WEIGHT,
            bytes_accessed=4 * height * depth // WEIGHT,
            transcendentals=0,
        ),
    )(flags, mat, own, other)


def back_pair(flags, mat, parts, own, other):
    half, tokens = own.shape
    rows = mat.shape[0] // parts
    slots = 3

    def body(s, mat_ref, own_ref, other_ref, *refs):
        out_refs, (buf, sem) = refs[:parts], refs[parts:]

        def fetch(i, core):
            row = lax.bitwise_xor(s[2], lax.rem(i + 1, parts)) * rows
            piece = mat_ref.at[pl.ds(pl.multiple_of(row, 16), rows), core * half : (core + 1) * half]
            slot = lax.rem(i, slots)
            return pltpu.make_async_copy(piece, buf.at[slot, core], sem.at[slot, core])

        def both(i, act):
            for core in range(2):
                act(fetch(i, core))

        @pl.when(s[0] == 1)
        def _():
            for i in range(slots):
                both(i, lambda copy: copy.start())

            @pl.loop(0, parts)
            def _(i):
                both(i, lambda copy: copy.wait())
                slot = lax.rem(i, slots)
                got = jnp.dot(buf[slot, s[1]], own_ref[...], preferred_element_type=F32)
                got = got + jnp.dot(
                    buf[slot, 1 - s[1]], other_ref[...], preferred_element_type=F32
                )

                @pl.when(i + slots < parts)
                def _():
                    both(i + slots, lambda copy: copy.start())

                for which, ref in enumerate(out_refs):

                    @pl.when(i == which)
                    def _(ref=ref):
                        ref[...] = got.astype(ref.dtype)

    return pl.pallas_call(
        body,
        in_specs=[SMEM, ANY, VMEM, VMEM],
        out_specs=[VMEM] * parts,
        out_shape=[jax.ShapeDtypeStruct((rows, tokens), LOW)] * (parts - 1)
        + [jax.ShapeDtypeStruct((rows, tokens), F32)],
        scratch_shapes=[
            pltpu.VMEM((slots, 2, rows, half), LOW),
            pltpu.SemaphoreType.DMA((slots, 2)),
        ],
        compiler_params=params(),
        cost_estimate=pl.CostEstimate(
            flops=4 * tokens * rows * parts * half // WEIGHT,
            bytes_accessed=4 * rows * parts * half // WEIGHT,
            transcendentals=0,
        ),
    )(flags, mat, own, other)


def turned(right_ref, grad_ref):
    right_ref[...] = grad_ref[...].T.astype(LOW)


def hidden_of(right_ref, own_ref, slope_ref, *other_refs):
    row = 0
    for other_ref in other_refs:
        at = slice(row, row + other_ref.shape[0])
        total = own_ref[at] + other_ref[...].astype(F32)
        right_ref[at] = (total * slope_ref[at]).astype(LOW)
        row = at.stop


def hidden(flags, own, slope, others):
    def body(s, own_ref, slope_ref, *refs):
        @pl.when(s[0] == 1)
        def _():
            hidden_of(refs[-1], own_ref, slope_ref, *refs[:-1])

    return pl.pallas_call(
        body,
        in_specs=[SMEM] + [VMEM] * (2 + len(others)),
        out_specs=VMEM,
        out_shape=jax.ShapeDtypeStruct(own.shape, LOW),
        compiler_params=params(),
        cost_estimate=pl.CostEstimate(
            flops=own.size // WEIGHT, bytes_accessed=own.size // WEIGHT, transcendentals=0
        ),
    )(flags, own, slope, *others)


def split_rows(flags, mat):
    rows, cols = mat.shape
    step = 256
    half = step // 2
    count = rows // step
    slots = 4

    def body(s, mat_ref, out_ref, buf, done, sem_in, sem_out):
        def fetch(i, slot):
            piece = mat_ref.at[pl.ds(pl.multiple_of(i * step, step), step)]
            return pltpu.make_async_copy(piece, buf.at[slot], sem_in.at[slot])

        def put(i, slot):
            piece = out_ref.at[:, pl.ds(pl.multiple_of(i * half, half), half)]
            return pltpu.make_async_copy(done.at[slot], piece, sem_out.at[slot])

        @pl.when(s[0] == 1)
        def _():
            to = lax.broadcasted_iota(jnp.int32, (step, step), 0)
            source = lax.broadcasted_iota(jnp.int32, (step, step), 1)
            wanted = jnp.where(to < half, 2 * to, 2 * (to - half) + 1)
            pick = jnp.where(source == wanted, 1.0, 0.0).astype(LOW)
            for i in range(slots):
                fetch(i, i).start()

            @pl.loop(0, count // slots)
            def _(turn):
                for slot in range(slots):
                    i = turn * slots + slot
                    fetch(i, slot).wait()

                    @pl.when(turn > 0)
                    def _():
                        put(i - slots, slot).wait()

                    got = jnp.dot(pick, buf[slot], preferred_element_type=F32).astype(LOW)
                    done[slot, 0] = got[:half]
                    done[slot, 1] = got[half:]

                    @pl.when(turn < count // slots - 1)
                    def _():
                        fetch(i + slots, slot).start()

                    put(i, slot).start()

            for slot in range(slots):
                put(count - slots + slot, slot).wait()

    out = pl.pallas_call(
        body,
        in_specs=[SMEM, ANY],
        out_specs=ANY,
        out_shape=jax.ShapeDtypeStruct((2, rows // 2, cols), LOW),
        scratch_shapes=[
            pltpu.VMEM((slots, step, cols), LOW),
            pltpu.VMEM((slots, 2, half, cols), LOW),
            pltpu.SemaphoreType.DMA((slots,)),
            pltpu.SemaphoreType.DMA((slots,)),
        ],
        compiler_params=params(),
        cost_estimate=pl.CostEstimate(
            flops=2 * rows * step * cols // WEIGHT, bytes_accessed=4 * rows * cols // WEIGHT, transcendentals=0
        ),
    )(flags, mat)
    return out


def slope_of(flags, pre, start, tokens, half):
    cols = divisor(half, 768)
    per_half = half // cols

    def body(s, pre_ref, out_ref):
        out_ref[...] = gelu_slope(pre_ref[...]).T

    return pl.pallas_call(
        body,
        grid_spec=pltpu.PrefetchScalarGridSpec(
            num_scalar_prefetch=1,
            grid=(tokens // LANES, per_half),
            in_specs=[
                pl.BlockSpec((LANES, cols), lambda i, j, s: (start // LANES + i, s[1] * per_half + j))
            ],
            out_specs=pl.BlockSpec((cols, LANES), lambda i, j, s: (j, i)),
        ),
        out_shape=jax.ShapeDtypeStruct((half, tokens), F32),
        compiler_params=params(),
        cost_estimate=pl.CostEstimate(
            flops=half * tokens // WEIGHT, bytes_accessed=8 * half * tokens // WEIGHT, transcendentals=0
        ),
    )(flags, pre)


def join(flags, grad, parts):
    tokens, columns = grad.shape
    width = columns // PARTS

    def body(s, grad_ref, *refs):
        part_refs, (low_ref, term_ref) = refs[:PARTS], refs[PARTS:]

        @pl.when(s[0] == 1)
        def _():
            for slot, ref in enumerate(part_refs):
                start = pl.multiple_of(lax.bitwise_xor(s[2], slot) * width, LANES)
                term = ref[...]
                term_ref[pl.ds(start, width)] = term
                total = grad_ref[:, pl.ds(start, width)].T + term.astype(F32)
                low_ref[pl.ds(start, width)] = total.astype(LOW)

    shape = jax.ShapeDtypeStruct((columns, tokens), LOW)
    return pl.pallas_call(
        body,
        in_specs=[SMEM] + [VMEM] * (1 + PARTS),
        out_specs=[VMEM, VMEM],
        out_shape=[shape, shape],
        compiler_params=params(),
        cost_estimate=pl.CostEstimate(
            flops=4 * columns * tokens, bytes_accessed=4 * columns * tokens, transcendentals=0
        ),
    )(flags, grad, *parts)


def finish(flags, out, grad, start, term, parts):
    columns, tokens = term.shape
    width = columns // PARTS
    total_tokens = grad.shape[0]

    def body(s, *refs):
        grad_ref, term_ref, *part_refs = refs[int(out is not None) : -2]
        out_ref, joined = refs[-2:]
        for slot, ref in enumerate(part_refs):
            start = pl.multiple_of(lax.bitwise_xor(s[2], slot) * width, LANES)
            joined[pl.ds(start, width)] = ref[...]

        @pl.when(s[0] == 0)
        def _():
            out_ref[...] = grad_ref[...] + joined[...].astype(F32).T

        @pl.when(s[0] == 1)
        def _():
            source = lax.broadcasted_iota(jnp.int32, (2 * LANES, 2 * LANES), 1)
            to = lax.broadcasted_iota(jnp.int32, (2 * LANES, 2 * LANES), 0)
            wanted = jnp.where(source < LANES, 2 * source, 2 * (source - LANES) + 1)
            pick = jnp.where(to == wanted, 1.0, 0.0).astype(LOW)
            for group in range(columns // (2 * LANES)):
                even_at = group * LANES
                odd_at = columns // 2 + group * LANES
                even = joined[even_at : even_at + LANES]
                odd = joined[odd_at : odd_at + LANES]
                pair = jnp.concatenate([even, odd], axis=0)
                woven = jnp.dot(pick, pair, preferred_element_type=F32)
                at = slice(group * 2 * LANES, (group + 1) * 2 * LANES)
                first = term_ref[at].astype(F32).T
                out_ref[:, at] = grad_ref[:, at] + first + woven.T

    earlier = [] if out is None else [out]
    piece = pl.BlockSpec((width, LANES), lambda i, s: (0, i))
    rows = pl.BlockSpec((LANES, columns), lambda i, s: (start // LANES + i, 0))
    return pl.pallas_call(
        body,
        grid_spec=pltpu.PrefetchScalarGridSpec(
            num_scalar_prefetch=1,
            grid=(tokens // LANES,),
            in_specs=[ANY] * len(earlier)
            + [rows, pl.BlockSpec((columns, LANES), lambda i, s: (0, i))]
            + [piece] * PARTS,
            out_specs=rows,
            scratch_shapes=[pltpu.VMEM((columns, LANES), LOW)],
        ),
        out_shape=jax.ShapeDtypeStruct((total_tokens, columns), F32),
        input_output_aliases={1: 0} if earlier else {},
        compiler_params=params(),
    )(flags, *earlier, grad, term, *parts)


def local(grad_out, weight_in, weight_out, pre_act):
    hids = lax.axis_size("hid")
    section = lax.axis_index("section")
    side = lax.axis_index("wid") % 2
    is_up = section == 1

    def scalars(active_section):
        active = (section == active_section).astype(jnp.int32)
        return jnp.stack([active, side, lax.axis_index("hid") % PARTS]).astype(jnp.int32)

    down, up = scalars(0), scalars(1)

    def within(active, distance, block, axis="wid"):
        size = lax.axis_size(axis)
        pairs = [(active * size + i, active * size + (i ^ distance)) for i in range(size)]
        return lax.ppermute(block, ("section", axis), pairs)

    def everywhere(distance, block, axis="hid"):
        size = lax.axis_size(axis)
        return lax.ppermute(block, axis, [(i, i ^ distance) for i in range(size)])

    mat_in = weight_in[0]
    mat_out = weight_out[0]
    quarter, hid_tile = mat_in.shape
    half = hid_tile // 2
    batches, batch_tokens, _ = grad_out.shape
    total = batches * batch_tokens
    unit = total // sum(SHARES)
    starts = [unit * sum(SHARES[:k]) for k in range(len(SHARES))]
    sizes = [unit * share for share in SHARES]
    chunks = range(len(SHARES))
    last_chunk = len(SHARES) - 1
    grad = grad_out.reshape(total, quarter)
    pre = pre_act[0].reshape(total, hid_tile)
    grads = [grad[starts[k] : starts[k] + sizes[k]] for k in chunks]

    split_out = split_rows(up, mat_out)

    hid_rows = divisor(half // 2, 512)
    hid_steps = half // hid_rows
    part_rows = quarter // PARTS

    def product_out(flags, mat, first_row, sources, prepare, tokens, outs, base=None, first=None):
        return product(
            flags, mat, (hid_rows, quarter),
            lambda i, s: (first_row(s) + i * hid_rows, 0), hid_steps,
            sources, prepare, tokens, outs, base, lambda i, s: i * hid_rows, first=first,
        )

    def in_pieces(*shares):
        blocks = [max(1, hid_steps * sum(shares[: n + 1]) // sum(shares)) for n in range(len(shares))]
        ends = [0] + [hid_rows * block for block in blocks]
        return [(half, 0, F32)] + [(ends[n + 1] - ends[n], ends[n], LOW) for n in range(len(shares))]

    def exchange(active, pieces, earlier):
        if earlier is not None:
            pieces = [lax.optimization_barrier((piece, earlier))[0] for piece in pieces]
        return [within(active, 2, piece) for piece in pieces]

    def detour(active, piece):
        size = lax.axis_size("wid")
        pairs = [(active * size + i, (1 - active) * size + (i ^ 2)) for i in range(size)]
        return lax.ppermute(piece, ("section", "wid"), pairs)

    def returned(active, piece):
        size = lax.axis_size("wid")
        pairs = [((1 - active) * size + i, active * size + i) for i in range(size)]
        return lax.ppermute(piece, ("section", "wid"), pairs)

    def across(term, distance):
        size = lax.axis_size("hid")
        pairs = [(i, size + (i ^ distance)) for i in range(size)]
        return lax.ppermute(term, ("section", "hid"), pairs)

    def product_in(flags, place, sources, prepare, tokens, kind):
        return product(
            flags, mat_in, (part_rows, half), place, PARTS, sources, prepare, tokens,
            [(quarter, 0, kind)],
        )

    def product_parts(flags, place, right, tokens, base):
        def part_of(i, s):
            return lax.bitwise_xor(s[2], lax.rem(i + 1, PARTS))

        return product(
            flags, mat_in, (part_rows, half), lambda i, s: place(part_of(i, s), s), PARTS,
            [right], None, tokens, [(part_rows, 0, LOW)] * 3 + [(part_rows, 0, F32)],
            base, lambda i, s: part_of(i, s) * part_rows, True,
        )

    def send_parts(active, parts):
        return [within(active, d + 1, part, "hid") for d, part in enumerate(parts[:-1])]

    def sum_hid(active, own, got):
        for part in got:
            own = own + part.astype(F32)
        distance = PARTS
        while distance < hids:
            own = own + within(active, distance, own, "hid")
            distance *= 2
        return own.astype(LOW)

    class Steps:
        def __init__(self):
            self.last = None

        def after(self, value):
            if self.last is None:
                return value
            return lax.optimization_barrier((value, self.last))[0]

    steps = Steps()
    steps.last = split_out
    hidden_full, hidden_other, slopes, parts_out, terms, gathered = {}, {}, {}, {}, {}, {}
    lows, core_got, parts_got = {}, {}, {}
    up_full, up_other, up_parts, up_terms, lasts = {}, {}, {}, {}, {}

    def down_send(k):
        sent, lows[k] = product_out(
            steps.after(down), mat_out, lambda s: (1 - s[1]) * half, [grad], turned,
            sizes[k], [(half, 0, LOW)], first=starts[k],
        )
        steps.last = sent
        core_got[k] = within(0, 1, sent)

    def down_hidden(k):
        full, *pieces = product_out(
            steps.after(down), mat_out, lambda s: s[1] * half, [lows[k]], None, sizes[k],
            in_pieces(*((1,) if k else (2, 1))), core_got[k],
        )
        steps.last = full
        hidden_full[k] = full
        if k > 0:
            hidden_other[k] = exchange(0, pieces, hidden_other[0][0])
        else:
            hidden_other[0] = [within(0, 2, pieces[0]), detour(0, pieces[1])]

    def down_return():
        hidden_other[0][1] = returned(0, steps.after(hidden_other[0][1]))

    def slope(k):
        slopes[k] = slope_of(steps.after(down), pre, starts[k], sizes[k], half)
        steps.last = slopes[k]

    def down_back(k):
        tokens = sizes[k]
        right = hidden(steps.after(down), hidden_full[k], slopes[k], hidden_other[k])
        swapped = within(0, 1, right)
        parts_out[k] = back_pair(down, mat_in, PARTS, right, swapped)
        parts_got[k] = send_parts(0, parts_out[k])
        steps.last = parts_out[k][0]

    def cross(k):
        terms[k] = sum_hid(0, steps.after(parts_out[k][-1]), parts_got[k])
        if k == 0:
            crossed = across(terms[k], 0)
            steps.last = crossed
            gathered[k] = [crossed] + [within(1, d, crossed, "hid") for d in range(1, PARTS)]
        else:
            far = within(0, PARTS - 1, terms[k], "hid")
            gathered[k] = [across(terms[k], d) for d in range(PARTS - 1)] + [across(far, 0)]
            steps.last = gathered[k][0]

    def up_hidden(k):
        tokens = sizes[k]
        low, up_terms[k] = join(steps.after(up), grads[k], gathered[k])
        low_other = within(1, 1, low)
        flags = up
        if k + 1 in parts_got:
            flags = lax.optimization_barrier((up, *parts_got[k + 1]))[0]
        full, low_grad = pair_product(flags, split_out, hid_rows, low, low_other)
        steps.last = full
        up_full[k] = full
        up_other[k] = exchange(
            1, [low_grad if k < last_chunk else low_grad[hid_rows:]], up_other[k - 1][0] if k else None
        )
        if k == last_chunk:
            up_other[k].insert(0, detour(1, low_grad[:hid_rows]))

    def up_return():
        up_other[last_chunk][0] = returned(1, steps.after(up_other[last_chunk][0]))

    def place(part, core):
        row = core * (PARTS // 2) + lax.rem(part, PARTS // 2)
        return row * part_rows, lax.div(part, PARTS // 2) * half

    def up_back(k):
        tokens = sizes[k]
        sent, right = product_in(
            steps.after(up), lambda i, s: place(i, 1 - s[1]),
            [up_full[k], slopes[k]] + up_other[k], hidden_of, tokens, F32,
        )
        got = within(1, 1, sent)
        up_parts[k] = product_parts(up, lambda i, s: place(i, s[1]), right, tokens, got)
        steps.last = up_parts[k][0]

    def gather(k):
        own = steps.after(up_parts[k][-1])
        if k < last_chunk:
            own = lax.optimization_barrier((own, up_other[last_chunk][0]))[0]
        last = jnp.where(is_up, sum_hid(1, own, send_parts(1, up_parts[k])), terms[k])
        steps.last = last
        lasts[k] = [last] + [everywhere(d, last) for d in range(1, PARTS)]

    for k in chunks:
        down_send(k)
    for k in chunks:
        down_hidden(k)
    down_return()
    slope(0)
    down_back(0)
    slope(1)
    cross(0)
    down_back(1)
    up_hidden(0)
    cross(1)
    up_hidden(1)
    up_back(0)
    up_return()
    gather(0)
    up_back(1)
    out = finish(steps.after(up), None, grad, starts[0], up_terms[0], lasts[0])
    steps.last = out
    gather(1)
    k = last_chunk
    out = finish(up, out, grad, starts[k], up_terms[k], lasts[k])
    return out.reshape(1, batches, batch_tokens, quarter)


def solution(mesh):
    return jax.shard_map(
        local,
        mesh=mesh,
        in_specs=(
            P(None, None, "wid"),
            P("section", "wid", "hid"),
            P("section", "hid", "wid"),
            P("section", None, None, "hid"),
        ),
        out_specs=P("section", None, None, "wid"),
        check_vma=False,
    )
```
